32 devices in a mesh: groups: 2 (over y), renv: 16 (over z, x, core).
Axes of the slice: x: 2, y: 2, z: 4, core: 2. Of those that a mesh axis runs over, the one named last changes fastest.
Arguments:
- psi: float32 [256, 16384], P(('groups', 'renv')), parts along dimension 0, may hold values from -18 to 18, as said below
- left_env: float32 [128, 16384], P('groups'), parts along dimension 0, may hold values from -1 to 1.5
- right_env: float32 [512, 16384], P(('groups', 'renv')), parts along dimension 0, may hold values from -1 to 1.5
- send_block: int32 [512, 1], P(('groups', 'renv')), parts along dimension 0, may hold values from 0 to 7
- send_left: int32 [512, 1, 2], P(('groups', 'renv')), parts along dimension 0, may hold values from 0 to 63
- send_live: int32 [512, 1, 2], P(('groups', 'renv')), parts along dimension 0, may hold values from 0 to 1, as said below
- recv_right: int32 [512, 1, 2], P(('groups', 'renv')), parts along dimension 0, may hold values from 0 to 15
- recv_out: int32 [512, 1, 2], P(('groups', 'renv')), parts along dimension 0, may hold values from 0 to 7
- loc_block: int32 [1024], P(('groups', 'renv')), parts along dimension 0, may hold values from 0 to 7
- loc_left: int32 [1024], P(('groups', 'renv')), parts along dimension 0, may hold values from 0 to 63
- loc_right: int32 [1024], P(('groups', 'renv')), parts along dimension 0, may hold values from 0 to 15
Outputs:
- hpsi: float32 [256, 16384], P(('groups', 'renv')), parts along dimension 0
- residual: float32 [256, 16384], P(('groups', 'renv')), parts along dimension 0
The draws below stay inside these ranges and needn't reach their ends.
There are 2 independent parts, one for each index of `groups`. The reference program is written for one: setup_inputs(seed, part) draws one part's arguments, and reference() takes and returns one part's arrays. A program takes and returns all parts, laid end to end along the dimension named above; each array names one. Nothing has to cross between parts.
Inputs may be any that keep to these rules, and one draw needn't show every extreme that they name: psi blocks of owner-ordered index i have entries of size growing with i. `send_live`: in every draw some receiver has every term live from every sender.
All inputs are finite; a program needn't handle non-finite values.
Results may differ from the reference program's by a relative error of at most 0.0003.
Values sent between devices are 32-bit elements; how exact they have to be, the bound alone decides.
No kernel may reach another device: no remote copies, remote signals or barrier semaphores. Data moves between devices by JAX's collectives and lax.ppermute only.
A program may use at most 128 MiB of HBM per device.

```python
import math
import jax
import jax.numpy as jnp
from jax import lax

SECTOR = 128
TERMS = 2
SLOTS = 1
BLOCKS_DEV = 8
RIGHT_DEV = 16
LEFT_BLOCKS = 64
LOCAL_DEV = 32
BLOCKS = 128
RIGHT_BLOCKS = 256
LOCAL_TERMS = 512
PAIRS = 256
N_RENV = 16


def dominant(noise, diag, spread):
    eye = jnp.eye(SECTOR, dtype=jnp.float32)
    mats = diag * eye + spread / math.sqrt(SECTOR) * noise
    return mats.reshape(noise.shape[0], SECTOR * SECTOR)


def draw_psi(key, part):
    key = jax.random.fold_in(key, 5)
    base_key, noise_key = jax.random.split(key)
    place = jnp.arange(BLOCKS, dtype=jnp.float32) / max(BLOCKS - 1, 1)
    rise = 1.0 + 2.0 * place
    common = jnp.clip(jax.random.normal(base_key, (1, SECTOR * SECTOR), jnp.float32), -6.0, 6.0)
    values = jnp.clip(jax.random.normal(noise_key, (BLOCKS, SECTOR * SECTOR), jnp.float32), -6.0, 6.0)
    mixed = 0.6 * common + 0.8 * values
    return jnp.clip(mixed * rise[:, None], -18.0, 18.0)


def draw_left_env(key, part):
    key = jax.random.fold_in(key, 7)
    noise = jnp.clip(jax.random.normal(key, (LEFT_BLOCKS, SECTOR, SECTOR), jnp.float32), -4.0, 4.0)
    return dominant(noise, 0.5, 0.25)


def draw_right_env(key, part):
    key = jax.random.fold_in(key, 9)
    noise = jnp.clip(jax.random.normal(key, (RIGHT_BLOCKS, SECTOR, SECTOR), jnp.float32), -4.0, 4.0)
    return dominant(noise, 0.5, 0.25)


def draw_send_live(key, part):
    key = jax.random.fold_in(key, 11)
    first, second, third = jax.random.split(key, 3)
    level = jax.random.randint(first, (N_RENV,), 0, 4)
    chosen = jax.random.randint(second, (), 0, N_RENV)
    level = jnp.where(jnp.arange(N_RENV) == chosen, 3, level)
    rate = jnp.left_shift(jnp.ones_like(level), level)
    target = jnp.tile(rate, N_RENV)
    draws = jax.random.randint(third, (PAIRS, SLOTS, TERMS), 0, 8)
    return (draws < target[:, None, None]).astype(jnp.int32)


def plant(values, stream_key, smallest, top_value):
    shape = values.shape
    spot = [jax.random.randint(jax.random.fold_in(stream_key, axis), (), 0, shape[axis]) for axis in range(len(shape))]
    values = values.at[tuple(spot)].set(smallest)
    longest = shape.index(max(shape))
    spot[longest] = (spot[longest] + 1) % shape[longest]
    return values.at[tuple(spot)].set(top_value)


def setup_inputs(seed: int = 0, part: int = 0) -> dict:
    keys = jax.random.split(jax.random.key(seed), 12)
    part_splits = jax.random.split(jax.random.fold_in(keys[11], part), 12)
    return {
        "psi": draw_psi(jax.random.fold_in(jax.random.fold_in(keys[11], part), 71), part),
        "left_env": draw_left_env(jax.random.fold_in(jax.random.fold_in(keys[11], part), 71), part),
        "right_env": draw_right_env(jax.random.fold_in(jax.random.fold_in(keys[11], part), 71), part),
        "send_block": plant(jax.random.randint(part_splits[3], (PAIRS, SLOTS), 0, BLOCKS_DEV), jax.random.fold_in(part_splits[3], 1), 0, BLOCKS_DEV - 1).astype(jnp.int32),
        "send_left": plant(jax.random.randint(part_splits[4], (PAIRS, SLOTS, TERMS), 0, LEFT_BLOCKS), jax.random.fold_in(part_splits[4], 1), 0, LEFT_BLOCKS - 1).astype(jnp.int32),
        "send_live": draw_send_live(jax.random.fold_in(jax.random.fold_in(keys[11], part), 71), part),
        "recv_right": plant(jax.random.randint(part_splits[6], (PAIRS, SLOTS, TERMS), 0, RIGHT_DEV), jax.random.fold_in(part_splits[6], 1), 0, RIGHT_DEV - 1).astype(jnp.int32),
        "recv_out": plant(jax.random.randint(part_splits[7], (PAIRS, SLOTS, TERMS), 0, BLOCKS_DEV), jax.random.fold_in(part_splits[7], 1), 0, BLOCKS_DEV - 1).astype(jnp.int32),
        "loc_block": plant(jax.random.randint(part_splits[8], (LOCAL_TERMS,), 0, BLOCKS_DEV), jax.random.fold_in(part_splits[8], 1), 0, BLOCKS_DEV - 1).astype(jnp.int32),
        "loc_left": plant(jax.random.randint(part_splits[9], (LOCAL_TERMS,), 0, LEFT_BLOCKS), jax.random.fold_in(part_splits[9], 1), 0, LEFT_BLOCKS - 1).astype(jnp.int32),
        "loc_right": plant(jax.random.randint(part_splits[10], (LOCAL_TERMS,), 0, RIGHT_DEV), jax.random.fold_in(part_splits[10], 1), 0, RIGHT_DEV - 1).astype(jnp.int32),
    }


HI = lax.Precision.HIGHEST


def reference(psi, left_env, right_env, send_block, send_left, send_live, recv_right, recv_out, loc_block, loc_left, loc_right):
    count = N_RENV
    psi_dev = psi.reshape(count, BLOCKS_DEV, SECTOR, SECTOR)
    right_dev = right_env.reshape(count, RIGHT_DEV, SECTOR, SECTOR)
    left_mats = left_env.reshape(LEFT_BLOCKS, SECTOR, SECTOR)
    blocks = send_block.reshape(count, count, SLOTS)
    lefts = send_left.reshape(count, count, SLOTS, TERMS)
    marks = send_live.reshape(count, count, SLOTS, TERMS).astype(jnp.float32)
    rights = recv_right.reshape(count, count, SLOTS, TERMS)
    outputs = recv_out.reshape(count, count, SLOTS, TERMS)
    lblock = loc_block.reshape(count, LOCAL_DEV)
    lleft = loc_left.reshape(count, LOCAL_DEV)
    lright = loc_right.reshape(count, LOCAL_DEV)
    owners = jnp.arange(count, dtype=jnp.int32)
    labels = jnp.arange(BLOCKS_DEV, dtype=jnp.int32)

    def one_owner(owner):
        sources = psi_dev[owners[:, None], blocks[:, owner, :]]
        lmats = left_mats[lefts[:, owner]]
        moved = jnp.einsum("scgij,scjk->scgik", lmats, sources, precision=HI)
        moved = moved * marks[:, owner][..., None, None]
        mine = right_dev[owner]
        placed = jnp.einsum("scgik,scgkl->scgil", moved, mine[rights[owner]], precision=HI)
        onehot = (outputs[owner][..., None] == labels).astype(jnp.float32)
        total = jnp.einsum("scgb,scgil->bil", onehot, placed, precision=HI)
        own_psi = psi_dev[owner]
        near = jnp.einsum("kij,kjl->kil", left_mats[lleft[owner]], own_psi[lblock[owner]], precision=HI)
        near = jnp.einsum("kil,klm->kim", near, mine[lright[owner]], precision=HI)
        keep = (lblock[owner][:, None] == labels).astype(jnp.float32)
        return total + jnp.einsum("kb,kim->bim", keep, near, precision=HI)

    hpsi = lax.map(one_owner, owners).reshape(BLOCKS, SECTOR * SECTOR)
    correlation = jnp.sum(psi * hpsi)
    norm = jnp.sum(psi * psi)
    theta = correlation / (norm + 1e-6)
    return hpsi, hpsi - theta * psi
```

```python
import math

import jax
import jax.numpy as jnp
from jax import lax
from jax.experimental import pallas as pl
from jax.experimental.pallas import tpu as pltpu
from jax.sharding import PartitionSpec as P

F32 = jnp.float32
BF16 = jnp.bfloat16
SUB = 8
VMEM = pl.BlockSpec(memory_space=pltpu.VMEM)
SMEM = pl.BlockSpec(memory_space=pltpu.SMEM)


def as_rows(blocks, sector):
    count = blocks.shape[0]
    split = blocks.reshape(count // SUB, SUB, sector, sector)
    return split.transpose(0, 2, 1, 3).reshape(count * sector, sector)


def from_rows(rows, count):
    sector = rows.shape[1]
    split = rows.reshape(count // SUB, sector, SUB, sector)
    return split.transpose(0, 2, 1, 3).reshape(count, sector * sector)


def pick(ref, block):
    sector = ref.shape[1]
    start = (block // SUB) * (SUB * sector) + block % SUB
    return ref[pl.ds(start, sector, stride=SUB), :]


def halves(mat):
    high = mat.astype(BF16)
    low = (mat - high.astype(F32)).astype(BF16)
    return jnp.concatenate([high, low], axis=1)


def doubled(mat):
    both = halves(mat)
    return jnp.concatenate([both, both], axis=0)


def product(left, right):
    sector = right.shape[1] // 2
    wide = jnp.dot(left, right, preferred_element_type=F32)
    return wide[:, :sector] + wide[:, sector:]


def gather_kernel(block_ref, psi_ref, out_ref):
    def body(i, carry):
        out_ref[i] = pick(psi_ref, block_ref[i])
        return carry

    lax.fori_loop(0, out_ref.shape[0], body, 0, unroll=4)


def local_kernel(block_ref, left_ref, right_ref, psi_rows, left_rows, right_rows, near_ref, lefts_ref, rights_ref, psis_ref):
    owned = near_ref.shape[0]

    def split_left(i, carry):
        lefts_ref[i] = halves(pick(left_rows, i))
        return carry

    lax.fori_loop(0, lefts_ref.shape[0], split_left, 0, unroll=4)

    def split_right(i, carry):
        rights_ref[i] = doubled(pick(right_rows, i))
        return carry

    lax.fori_loop(0, rights_ref.shape[0], split_right, 0, unroll=4)

    def split_psi(i, carry):
        psis_ref[i] = doubled(pick(psi_rows, i))
        return carry

    lax.fori_loop(0, owned, split_psi, 0, unroll=4)
    near_ref[...] = jnp.zeros_like(near_ref)

    def term(k, carry):
        block = block_ref[k]
        moved = product(lefts_ref[left_ref[k]], psis_ref[block])
        near_ref[block] += product(halves(moved), rights_ref[right_ref[k]])
        return carry

    lax.fori_loop(0, block_ref.shape[0], term, 0, unroll=4)


def remote_kernel(terms, meta_ref, rindex_ref, out_index_ref, came_ref, near_ref, lefts_ref, rights_ref, psi_rows, hpsi_rows, sums_ref, acc):
    count, sector, _ = came_ref.shape
    owned = near_ref.shape[0]
    acc[...] = near_ref[...]

    def block(i, carry):
        weight = doubled(came_ref[i])
        base = i * 2 * terms
        stack = jnp.concatenate([lefts_ref[meta_ref[base + g]] for g in range(terms)], axis=0)
        moved = product(stack, weight)
        for g in range(terms):
            live = meta_ref[base + terms + g].astype(F32)
            one = moved[g * sector : (g + 1) * sector] * live
            acc[out_index_ref[i * terms + g]] += product(halves(one), rights_ref[rindex_ref[i * terms + g]])
        return carry

    lax.fori_loop(0, count, block, 0, unroll=2)
    for b in range(owned):
        start = (b // SUB) * (SUB * sector) + b % SUB
        hpsi_rows[pl.ds(start, sector, stride=SUB), :] = acc[b]
    psi = psi_rows[...]
    corr = jnp.sum(psi * hpsi_rows[...], axis=0, keepdims=True)
    norm = jnp.sum(psi * psi, axis=0, keepdims=True)
    row = lax.broadcasted_iota(jnp.int32, sums_ref.shape, 0)
    sums_ref[...] = jnp.where(row == 0, corr, jnp.where(row == 1, norm, 0.0))


def residual_kernel(sums_ref, hpsi_rows, psi_rows, out_ref):
    total = jnp.sum(sums_ref[...], axis=0)
    whole = jnp.sum(total, axis=1, keepdims=True)
    theta = whole[0:1] / (whole[1:2] + 1e-06)
    out_ref[...] = hpsi_rows[...] - theta * psi_rows[...]


def shards(
    psi,
    left_env,
    right_env,
    send_block,
    send_left,
    send_live,
    recv_right,
    recv_out,
    loc_block,
    loc_left,
    loc_right,
):
    peers = lax.axis_size("renv")
    owned = psi.shape[0]
    sector = math.isqrt(psi.shape[1])
    slots = send_block.shape[1]
    terms = send_left.shape[2]
    count = peers * slots
    lefts = left_env.shape[0]
    rights = right_env.shape[0]
    psi_rows = as_rows(psi, sector)
    left_rows = as_rows(left_env, sector)
    right_rows = as_rows(right_env, sector)
    limit = pltpu.CompilerParams(vmem_limit_bytes=40 * 2**20)

    sent = pl.pallas_call(
        gather_kernel,
        out_shape=jax.ShapeDtypeStruct((count, sector, sector), F32),
        in_specs=[SMEM, VMEM],
        out_specs=VMEM,
        compiler_params=limit,
        name="gather_blocks",
    )(send_block.reshape(count), psi_rows)
    came = lax.all_to_all(sent.reshape(peers, slots, sector, sector), "renv", split_axis=0, concat_axis=0, tiled=True)
    came = came.reshape(count, sector, sector)

    meta = jnp.concatenate([send_left, send_live], axis=2)
    meta = lax.all_to_all(meta, "renv", split_axis=0, concat_axis=0, tiled=True).reshape(count * 2 * terms)

    near, left_parts, right_parts = pl.pallas_call(
        local_kernel,
        out_shape=(
            jax.ShapeDtypeStruct((owned, sector, sector), F32),
            jax.ShapeDtypeStruct((lefts, sector, 2 * sector), BF16),
            jax.ShapeDtypeStruct((rights, 2 * sector, 2 * sector), BF16),
        ),
        in_specs=[SMEM] * 3 + [VMEM] * 3,
        out_specs=(VMEM,) * 3,
        scratch_shapes=[pltpu.VMEM((owned, 2 * sector, 2 * sector), BF16)],
        compiler_params=limit,
        cost_estimate=pl.CostEstimate(flops=2 * 10**9, bytes_accessed=13 * 2**20, transcendentals=0),
        name="local_terms",
    )(loc_block, loc_left, loc_right, psi_rows, left_rows, right_rows)

    hpsi_rows, sums = pl.pallas_call(
        lambda *refs: remote_kernel(terms, *refs),
        out_shape=(
            jax.ShapeDtypeStruct((owned * sector, sector), F32),
            jax.ShapeDtypeStruct((SUB, sector), F32),
        ),
        in_specs=[SMEM] * 3 + [VMEM] * 5,
        out_specs=(VMEM,) * 2,
        scratch_shapes=[pltpu.VMEM((owned, sector, sector), F32)],
        compiler_params=limit,
        name="remote_terms",
    )(meta, recv_right.reshape(-1), recv_out.reshape(-1), came, near, left_parts, right_parts, psi_rows)

    spread = jnp.broadcast_to(sums[None], (peers, SUB, sector))
    sums = lax.all_to_all(spread, "renv", split_axis=0, concat_axis=0, tiled=True)
    residual_rows = pl.pallas_call(
        residual_kernel,
        out_shape=jax.ShapeDtypeStruct((owned * sector, sector), F32),
        in_specs=[VMEM] * 3,
        out_specs=VMEM,
        compiler_params=limit,
        name="residual",
    )(sums, hpsi_rows, psi_rows)
    return (from_rows(hpsi_rows, owned), from_rows(residual_rows, owned))


def solution(mesh):
    placed = (
        P(("groups", "renv"), None),
        P("groups", None),
        P(("groups", "renv"), None),
        P(("groups", "renv"), None),
        P(("groups", "renv"), None, None),
        P(("groups", "renv"), None, None),
        P(("groups", "renv"), None, None),
        P(("groups", "renv"), None, None),
        P(("groups", "renv")),
        P(("groups", "renv")),
        P(("groups", "renv")),
    )
    return jax.shard_map(
        shards,
        mesh=mesh,
        in_specs=placed,
        out_specs=(P(("groups", "renv"), None), P(("groups", "renv"), None)),
        check_vma=False,
    )
```

```python
import math

import jax
import jax.numpy as jnp
from jax import lax
from jax.experimental import pallas as pl
from jax.experimental.pallas import tpu as pltpu
from jax.sharding import PartitionSpec as P

F32 = jnp.float32
BF16 = jnp.bfloat16
SUB = 8
VMEM = pl.BlockSpec(memory_space=pltpu.VMEM)
SMEM = pl.BlockSpec(memory_space=pltpu.SMEM)
HBM = pl.BlockSpec(memory_space=pltpu.HBM)


def as_rows(blocks, sector):
    count = blocks.shape[0]
    split = blocks.reshape(count // SUB, SUB, sector, sector)
    return split.transpose(0, 2, 1, 3).reshape(count * sector, sector)


def from_rows(rows, count):
    sector = rows.shape[1]
    split = rows.reshape(count // SUB, sector, SUB, sector)
    return split.transpose(0, 2, 1, 3).reshape(count, sector * sector)


def pick(ref, block):
    sector = ref.shape[1]
    start = (block // SUB) * (SUB * sector) + block % SUB
    return ref[pl.ds(start, sector, stride=SUB), :]


def halves(mat):
    high = mat.astype(BF16)
    low = (mat - high.astype(F32)).astype(BF16)
    return jnp.concatenate([high, low], axis=1)


def doubled(mat):
    both = halves(mat)
    return jnp.concatenate([both, both], axis=0)


def product(left, right):
    sector = right.shape[1] // 2
    wide = jnp.dot(left, right, preferred_element_type=F32)
    return wide[:, :sector] + wide[:, sector:]


def gather_kernel(order, me_ref, block_ref, psi_hbm, *rest):
    outs, (psi_rows, stage, fetch_sem, put_sems) = rest[: len(order)], rest[len(order) :]
    fetch = pltpu.make_async_copy(psi_hbm, psi_rows, fetch_sem)
    fetch.start()
    fetch.wait()
    puts = []
    for i, step in enumerate(order):
        stage[i] = pick(psi_rows, block_ref[peer(me_ref[0], step)])
        put = pltpu.make_async_copy(stage.at[i], outs[i], put_sems.at[i])
        put.start()
        puts.append(put)
    for put in puts:
        put.wait()


def peer(me, step):
    return lax.bitwise_xor(me, step)


def local_kernel(
    terms,
    me_ref,
    send_block_ref,
    send_left_ref,
    send_live_ref,
    rindex_ref,
    out_index_ref,
    block_ref,
    left_ref,
    right_ref,
    psi_rows,
    left_rows,
    right_rows,
    near_ref,
    lefts_hbm,
    rights_hbm,
    lefts_ref,
    rights_ref,
    psis_ref,
    sems,
):
    owned = near_ref.shape[0]

    def split_left(i, carry):
        lefts_ref[i] = halves(pick(left_rows, i))
        return carry

    lax.fori_loop(0, lefts_ref.shape[0], split_left, 0, unroll=4)
    put_left = pltpu.make_async_copy(lefts_ref, lefts_hbm, sems.at[0])
    put_left.start()

    def split_right(i, carry):
        rights_ref[i] = doubled(pick(right_rows, i))
        return carry

    lax.fori_loop(0, rights_ref.shape[0], split_right, 0, unroll=4)
    put_right = pltpu.make_async_copy(rights_ref, rights_hbm, sems.at[1])
    put_right.start()

    def split_psi(i, carry):
        psis_ref[i] = doubled(pick(psi_rows, i))
        return carry

    lax.fori_loop(0, owned, split_psi, 0, unroll=4)
    near_ref[...] = jnp.zeros_like(near_ref)

    def term(k, carry):
        block = block_ref[k]
        moved = product(lefts_ref[left_ref[k]], psis_ref[block])
        near_ref[block] += product(halves(moved), rights_ref[right_ref[k]])
        return carry

    lax.fori_loop(0, block_ref.shape[0], term, 0, unroll=4)
    me = me_ref[0]
    for g in range(terms):
        spot = me * terms + g
        moved = product(lefts_ref[send_left_ref[spot]], psis_ref[send_block_ref[me]])
        moved = moved * send_live_ref[spot].astype(F32)
        near_ref[out_index_ref[spot]] += product(halves(moved), rights_ref[rindex_ref[spot]])
    put_left.wait()
    put_right.wait()


def add_terms(terms, order, me_ref, meta_ref, rindex_ref, out_index_ref, came, lefts_hbm, rights_hbm, acc, lefts_ref, rights_ref, left_sems, right_sems):
    sector = came[0].shape[0]
    senders = [peer(me_ref[0], step) for step in order]
    fetches = []
    for i, sender in enumerate(senders):
        mine = []
        for g in range(terms):
            lindex = meta_ref[sender * 2 * terms + g]
            rindex = rindex_ref[sender * terms + g]
            mine.append(
                pltpu.make_async_copy(
                    lefts_hbm.at[lindex], lefts_ref.at[i, pl.ds(g * sector, sector)], left_sems.at[i, g]
                )
            )
            mine.append(pltpu.make_async_copy(rights_hbm.at[rindex], rights_ref.at[i, g], right_sems.at[i, g]))
        for copy in mine:
            copy.start()
        fetches.append(mine)
    for i, sender in enumerate(senders):
        weight = doubled(came[i][...])
        for copy in fetches[i]:
            copy.wait()
        moved = product(lefts_ref[i], weight)
        for g in range(terms):
            live = meta_ref[sender * 2 * terms + terms + g].astype(F32)
            one = moved[g * sector : (g + 1) * sector] * live
            acc[out_index_ref[sender * terms + g]] += product(halves(one), rights_ref[i, g])


def remote_kernel(terms, order, me_ref, meta_ref, rindex_ref, out_index_ref, *rest):
    came, rest = rest[: len(order)], rest[len(order) :]
    lefts_hbm, rights_hbm, near_ref, acc, lefts_ref, rights_ref, left_sems, right_sems = rest
    acc[...] = near_ref[...]
    add_terms(terms, order, me_ref, meta_ref, rindex_ref, out_index_ref, came, lefts_hbm, rights_hbm, acc, lefts_ref, rights_ref, left_sems, right_sems)


def last_kernel(terms, order, me_ref, meta_ref, rindex_ref, out_index_ref, *rest):
    came, rest = rest[: len(order)], rest[len(order) :]
    lefts_hbm, rights_hbm, near_ref, psi_rows, hpsi_rows, sums_ref, acc, lefts_ref, rights_ref, left_sems, right_sems = rest
    sector = psi_rows.shape[1]
    acc[...] = near_ref[...]
    add_terms(terms, order, me_ref, meta_ref, rindex_ref, out_index_ref, came, lefts_hbm, rights_hbm, acc, lefts_ref, rights_ref, left_sems, right_sems)
    for b in range(acc.shape[0]):
        start = (b // SUB) * (SUB * sector) + b % SUB
        hpsi_rows[pl.ds(start, sector, stride=SUB), :] = acc[b]
    psi = psi_rows[...]
    corr = jnp.sum(psi * hpsi_rows[...], axis=0, keepdims=True)
    norm = jnp.sum(psi * psi, axis=0, keepdims=True)
    row = lax.broadcasted_iota(jnp.int32, sums_ref.shape, 0)
    sums_ref[...] = jnp.where(row == 0, corr, jnp.where(row == 1, norm, 0.0))


def residual_kernel(parts, *refs):
    hpsi_rows, psi_rows, out_ref = refs[parts:]
    total = refs[0][...]
    for part in refs[1:parts]:
        total = total + part[...]
    whole = jnp.sum(total, axis=1, keepdims=True)
    theta = whole[0:1] / (whole[1:2] + 1e-06)
    out_ref[...] = hpsi_rows[...] - theta * psi_rows[...]


def exchange(value, steps, peers):
    return [lax.ppermute(value, "renv", [(s, s ^ step) for s in range(peers)]) for step in steps]


def shards(
    psi,
    left_env,
    right_env,
    send_block,
    send_left,
    send_live,
    recv_right,
    recv_out,
    loc_block,
    loc_left,
    loc_right,
):
    peers = lax.axis_size("renv")
    owned = psi.shape[0]
    sector = math.isqrt(psi.shape[1])
    terms = send_left.shape[2]
    lefts = left_env.shape[0]
    rights = right_env.shape[0]
    psi_rows = as_rows(psi, sector)
    left_rows = as_rows(left_env, sector)
    right_rows = as_rows(right_env, sector)
    limit = pltpu.CompilerParams(vmem_limit_bytes=32 * 2**20)
    me = lax.axis_index("renv").astype(jnp.int32).reshape(1)
    mat = jax.ShapeDtypeStruct((sector, sector), F32)
    order = list(range(peers - 1, 0, -1))

    sent = pl.pallas_call(
        lambda *refs: gather_kernel(order, *refs),
        out_shape=[mat] * len(order),
        in_specs=[SMEM, SMEM, HBM],
        out_specs=[HBM] * len(order),
        scratch_shapes=[
            pltpu.VMEM(psi_rows.shape, F32),
            pltpu.VMEM((len(order), sector, sector), F32),
            pltpu.SemaphoreType.DMA,
            pltpu.SemaphoreType.DMA((len(order),)),
        ],
        compiler_params=limit,
        name="gather_blocks",
    )(me, send_block.reshape(-1), psi_rows)
    came = [lax.ppermute(block, "renv", [(s, s ^ step) for s in range(peers)]) for block, step in zip(sent, order)]

    meta = jnp.concatenate([send_left, send_live], axis=2).reshape(-1)
    every = lax.all_gather(meta, "renv")
    meta = lax.dynamic_slice_in_dim(every, me[0] * (2 * terms), 2 * terms, axis=1).reshape(-1)

    near, left_parts, right_parts = pl.pallas_call(
        lambda *refs: local_kernel(terms, *refs),
        out_shape=(
            jax.ShapeDtypeStruct((owned, sector, sector), F32),
            jax.ShapeDtypeStruct((lefts, sector, 2 * sector), BF16),
            jax.ShapeDtypeStruct((rights, 2 * sector, 2 * sector), BF16),
        ),
        in_specs=[SMEM] * 9 + [VMEM] * 3,
        out_specs=(VMEM, HBM, HBM),
        scratch_shapes=[
            pltpu.VMEM((lefts, sector, 2 * sector), BF16),
            pltpu.VMEM((rights, 2 * sector, 2 * sector), BF16),
            pltpu.VMEM((owned, 2 * sector, 2 * sector), BF16),
            pltpu.SemaphoreType.DMA((2,)),
        ],
        compiler_params=limit,
        cost_estimate=pl.CostEstimate(flops=2 * 10**9, bytes_accessed=13 * 2**20, transcendentals=0),
        name="local_terms",
    )(
        me,
        send_block.reshape(-1),
        send_left.reshape(-1),
        send_live.reshape(-1),
        recv_right.reshape(-1),
        recv_out.reshape(-1),
        loc_block,
        loc_left,
        loc_right,
        psi_rows,
        left_rows,
        right_rows,
    )

    width = 4
    groups = [(order[i : i + width], came[i : i + width]) for i in range(0, len(order), width)]
    groups.reverse()
    for number, (steps, blocks) in enumerate(groups):
        last = number == len(groups) - 1
        size = len(steps)
        scratch = [
            pltpu.VMEM((size, terms * sector, 2 * sector), BF16),
            pltpu.VMEM((size, terms, 2 * sector, 2 * sector), BF16),
            pltpu.SemaphoreType.DMA((size, terms)),
            pltpu.SemaphoreType.DMA((size, terms)),
        ]
        total = jax.ShapeDtypeStruct(near.shape, F32)
        operands = (me, meta, recv_right.reshape(-1), recv_out.reshape(-1), *blocks, left_parts, right_parts, near)
        specs = [SMEM] * 4 + [VMEM] * size + [HBM] * 2 + [VMEM]
        if not last:
            near = pl.pallas_call(
                lambda *refs, steps=steps: remote_kernel(terms, steps, *refs),
                out_shape=total,
                in_specs=specs,
                out_specs=VMEM,
                scratch_shapes=scratch,
                compiler_params=limit,
                cost_estimate=pl.CostEstimate(flops=2 * 10**8, bytes_accessed=4 * 2**20, transcendentals=0),
                name="remote_terms",
            )(*operands)
        else:
            hpsi_rows, sums = pl.pallas_call(
                lambda *refs, steps=steps: last_kernel(terms, steps, *refs),
                out_shape=(
                    jax.ShapeDtypeStruct((owned * sector, sector), F32),
                    jax.ShapeDtypeStruct((SUB, sector), F32),
                ),
                in_specs=specs + [VMEM],
                out_specs=(VMEM,) * 2,
                scratch_shapes=[pltpu.VMEM(near.shape, F32)] + scratch,
                compiler_params=limit,
                name="last_terms",
            )(*operands, psi_rows)

    stride = 1
    parts = [sums]
    while stride < peers:
        radix = min(4, peers // stride)
        if stride > 1:
            sums = sum(parts[1:], parts[0])
        parts = [sums] + exchange(sums, [digit * stride for digit in range(1, radix)], peers)
        stride *= radix
    residual_rows = pl.pallas_call(
        lambda *refs: residual_kernel(len(parts), *refs),
        out_shape=jax.ShapeDtypeStruct((owned * sector, sector), F32),
        in_specs=[VMEM] * (len(parts) + 2),
        out_specs=VMEM,
        compiler_params=limit,
        name="residual",
    )(*parts, hpsi_rows, psi_rows)
    return (from_rows(hpsi_rows, owned), from_rows(residual_rows, owned))


def solution(mesh):
    placed = (
        P(("groups", "renv"), None),
        P("groups", None),
        P(("groups", "renv"), None),
        P(("groups", "renv"), None),
        P(("groups", "renv"), None, None),
        P(("groups", "renv"), None, None),
        P(("groups", "renv"), None, None),
        P(("groups", "renv"), None, None),
        P(("groups", "renv")),
        P(("groups", "renv")),
        P(("groups", "renv")),
    )
    return jax.shard_map(
        shards,
        mesh=mesh,
        in_specs=placed,
        out_specs=(P(("groups", "renv"), None), P(("groups", "renv"), None)),
        check_vma=False,
    )
```

```python
import math

import jax
import jax.numpy as jnp
from jax import lax
from jax.experimental import pallas as pl
from jax.experimental.pallas import tpu as pltpu
from jax.sharding import PartitionSpec as P

F32 = jnp.float32
BF16 = jnp.bfloat16
SUB = 8
VMEM = pl.BlockSpec(memory_space=pltpu.VMEM)
SMEM = pl.BlockSpec(memory_space=pltpu.SMEM)
HBM = pl.BlockSpec(memory_space=pltpu.HBM)
MIB = 2**20


def as_rows(blocks, sector):
    count = blocks.shape[0]
    split = blocks.reshape(count // SUB, SUB, sector, sector)
    return split.transpose(0, 2, 1, 3).reshape(count * sector, sector)


def from_rows(rows, count):
    sector = rows.shape[1]
    split = rows.reshape(count // SUB, sector, SUB, sector)
    return split.transpose(0, 2, 1, 3).reshape(count, sector * sector)


def pick(ref, block):
    sector = ref.shape[1]
    start = (block // SUB) * (SUB * sector) + block % SUB
    return ref[pl.ds(start, sector, stride=SUB), :]


def halves(mat):
    high = mat.astype(BF16)
    low = (mat - high.astype(F32)).astype(BF16)
    return jnp.concatenate([high, low], axis=1)


def doubled(mat):
    both = halves(mat)
    return jnp.concatenate([both, both], axis=0)


def product(left, right):
    sector = right.shape[1] // 2
    wide = jnp.dot(left, right, preferred_element_type=F32)
    return wide[:, :sector] + wide[:, sector:]


def stacked(mat):
    high = mat.astype(BF16)
    low = (mat - high.astype(F32)).astype(BF16)
    rows = [jnp.concatenate([part, part], axis=1) for part in (high, low)]
    return jnp.concatenate(rows, axis=0)


def product_t(left, right):
    sector = right.shape[0] // 2
    wide = lax.dot_general(left, right, (((1,), (1,)), ((), ())), preferred_element_type=F32)
    return wide[:, :sector] + wide[:, sector:]


def roomy(mib):
    return pltpu.CompilerParams(vmem_limit_bytes=mib * MIB)


def gather_kernel(block_ref, psi_rows, out_hbm, stage, sems):
    puts = []
    for i in range(stage.shape[0]):
        stage[i] = pick(psi_rows, block_ref[i])
        put = pltpu.make_async_copy(stage.at[i], out_hbm.at[i], sems.at[i])
        put.start()
        puts.append(put)
    for put in puts:
        put.wait()


def local_kernel(block_ref, left_ref, right_ref, psi_rows, left_rows, right_rows, near_ref, sums_ref, rights_ref, psis_ref):
    def split_right(i, carry):
        rights_ref[i] = doubled(pick(right_rows, i))
        return carry

    lax.fori_loop(0, rights_ref.shape[0], split_right, 0, unroll=4)

    def split_psi(i, carry):
        psis_ref[i] = doubled(pick(psi_rows, i))
        return carry

    lax.fori_loop(0, psis_ref.shape[0], split_psi, 0, unroll=4)
    near_ref[...] = jnp.zeros_like(near_ref)

    def term(k, carry):
        block = block_ref[k]
        moved = product(halves(pick(left_rows, left_ref[k])), psis_ref[block])
        near_ref[block] += product(halves(moved), rights_ref[right_ref[k]])
        return carry

    lax.fori_loop(0, block_ref.shape[0], term, 0, unroll=4)
    corr = jnp.zeros((1, sums_ref.shape[1]), F32)
    norm = jnp.zeros((1, sums_ref.shape[1]), F32)
    for b in range(near_ref.shape[0]):
        mat = pick(psi_rows, b)
        corr += jnp.sum(mat * near_ref[b], axis=0, keepdims=True)
        norm += jnp.sum(mat * mat, axis=0, keepdims=True)
    row = lax.broadcasted_iota(jnp.int32, sums_ref.shape, 0)
    sums_ref[...] = jnp.where(row == 0, corr, jnp.where(row == 1, norm, 0.0))


def adjoint_kernel(terms, meta_ref, rindex_ref, out_index_ref, psi_rows, left_rows, right_rows, adjoint_ref, lefts_ref, rights_ref, psis_ref):
    sector = psi_rows.shape[1]

    def split_right(i, carry):
        rights_ref[i] = halves(pick(right_rows, i))
        return carry

    lax.fori_loop(0, rights_ref.shape[0], split_right, 0, unroll=4)

    def split_psi(i, carry):
        psis_ref[i] = stacked(pick(psi_rows, i))
        return carry

    lax.fori_loop(0, psis_ref.shape[0], split_psi, 0, unroll=4)

    def sender(i, carry):
        base = i * 2 * terms
        inner, weights = [], []
        for g in range(terms):
            left = halves(pick(left_rows, meta_ref[base + g]))
            lefts_ref[i, g * sector : (g + 1) * sector] = left
            weights += [left, left]
            live = meta_ref[base + terms + g].astype(F32)
            one = product_t(rights_ref[rindex_ref[i * terms + g]], psis_ref[out_index_ref[i * terms + g]])
            inner.append(halves(one * live))
        turned = product(jnp.concatenate(inner, axis=1), jnp.concatenate(weights, axis=0))
        adjoint_ref[i] = turned.T
        return carry

    lax.fori_loop(0, adjoint_ref.shape[0], sender, 0, unroll=2)


def overlap_kernel(came_ref, adjoint_ref, near_sums_ref, out_ref):
    def block(i, total):
        return total + jnp.sum((came_ref[i] * adjoint_ref[i]).reshape(-1, SUB, came_ref.shape[2]), axis=0)

    total = lax.fori_loop(0, came_ref.shape[0], block, jnp.zeros(out_ref.shape[1:], F32), unroll=4)
    corr = jnp.sum(total, axis=0, keepdims=True)
    row = lax.broadcasted_iota(jnp.int32, total.shape, 0)
    mine = near_sums_ref[...] + jnp.where(row == 0, corr, 0.0)
    for i in range(out_ref.shape[0]):
        out_ref[i] = mine


def remote_kernel(terms, meta_ref, rindex_ref, out_index_ref, came_ref, near_ref, lefts_ref, rights_ref, hpsi_rows, hpsi_hbm, acc, moved_ref, sem):
    count, sector, _ = came_ref.shape
    acc[...] = near_ref[...]

    def left_step(i, carry):
        moved = product(lefts_ref[i], doubled(came_ref[i]))
        for g in range(terms):
            live = meta_ref[i * 2 * terms + terms + g].astype(F32)
            moved_ref[i * terms + g] = halves(moved[g * sector : (g + 1) * sector] * live)
        return carry

    lax.fori_loop(0, count, left_step, 0, unroll=4)

    def right_step(t, carry):
        right = rights_ref[rindex_ref[t]]
        acc[out_index_ref[t]] += product(moved_ref[t], jnp.concatenate([right, right], axis=0))
        return carry

    lax.fori_loop(0, count * terms, right_step, 0, unroll=4)
    for b in range(acc.shape[0]):
        start = (b // SUB) * (SUB * sector) + b % SUB
        hpsi_rows[pl.ds(start, sector, stride=SUB), :] = acc[b]
    put = pltpu.make_async_copy(hpsi_rows, hpsi_hbm, sem)
    put.start()
    put.wait()


def residual_kernel(sums_ref, hpsi_rows, psi_rows, out_ref):
    total = jnp.sum(sums_ref[...], axis=0)
    whole = jnp.sum(total, axis=1, keepdims=True)
    theta = whole[0:1] / (whole[1:2] + 1e-06)
    out_ref[...] = hpsi_rows[...] - theta * psi_rows[...]


def shards(
    psi,
    left_env,
    right_env,
    send_block,
    send_left,
    send_live,
    recv_right,
    recv_out,
    loc_block,
    loc_left,
    loc_right,
):
    peers = lax.axis_size("renv")
    owned = psi.shape[0]
    sector = math.isqrt(psi.shape[1])
    slots = send_block.shape[1]
    terms = send_left.shape[2]
    count = peers * slots
    rights = right_env.shape[0]
    psi_rows = as_rows(psi, sector)
    left_rows = as_rows(left_env, sector)
    right_rows = as_rows(right_env, sector)
    rindex = recv_right.reshape(-1)
    out_index = recv_out.reshape(-1)
    blocks = jax.ShapeDtypeStruct((count, sector, sector), F32)
    rows = jax.ShapeDtypeStruct((owned * sector, sector), F32)
    mats = jax.ShapeDtypeStruct((owned, sector, sector), F32)
    tile = jax.ShapeDtypeStruct((SUB, sector), F32)

    sent = pl.pallas_call(
        gather_kernel,
        out_shape=blocks,
        in_specs=[SMEM, VMEM],
        out_specs=HBM,
        scratch_shapes=[pltpu.VMEM(blocks.shape, F32), pltpu.SemaphoreType.DMA((count,))],
        compiler_params=roomy(56),
        name="gather_blocks",
    )(send_block.reshape(-1), psi_rows)
    meta = jnp.concatenate([send_left, send_live], axis=2)
    sent, meta = lax.optimization_barrier((sent, meta))
    came = lax.all_to_all(sent.reshape(peers, slots, sector, sector), "renv", split_axis=0, concat_axis=0, tiled=True)
    came = came.reshape(count, sector, sector)
    meta = lax.all_to_all(meta, "renv", split_axis=0, concat_axis=0, tiled=True).reshape(-1)

    near, near_sums = pl.pallas_call(
        local_kernel,
        out_shape=(mats, tile),
        in_specs=[SMEM] * 3 + [VMEM] * 3,
        out_specs=(VMEM,) * 2,
        scratch_shapes=[
            pltpu.VMEM((rights, 2 * sector, 2 * sector), BF16),
            pltpu.VMEM((owned, 2 * sector, 2 * sector), BF16),
        ],
        compiler_params=roomy(56),
        cost_estimate=pl.CostEstimate(flops=4 * 10**9, bytes_accessed=6 * MIB, transcendentals=0),
        name="local_terms",
    )(loc_block, loc_left, loc_right, psi_rows, left_rows, right_rows)

    adjoint, left_parts, right_parts = pl.pallas_call(
        lambda *refs: adjoint_kernel(terms, *refs),
        out_shape=(
            blocks,
            jax.ShapeDtypeStruct((count, terms * sector, 2 * sector), BF16),
            jax.ShapeDtypeStruct((rights, sector, 2 * sector), BF16),
        ),
        in_specs=[SMEM] * 3 + [VMEM] * 3,
        out_specs=(VMEM,) * 3,
        scratch_shapes=[pltpu.VMEM((owned, 2 * sector, 2 * sector), BF16)],
        compiler_params=roomy(56),
        cost_estimate=pl.CostEstimate(flops=4 * 10**9, bytes_accessed=10 * MIB, transcendentals=0),
        name="adjoint_blocks",
    )(meta, rindex, out_index, psi_rows, left_rows, right_rows)

    sums = pl.pallas_call(
        overlap_kernel,
        out_shape=jax.ShapeDtypeStruct((peers, SUB, sector), F32),
        in_specs=[VMEM] * 3,
        out_specs=VMEM,
        compiler_params=roomy(24),
        name="overlap",
    )(came, adjoint, near_sums)
    sums = lax.all_to_all(sums, "renv", split_axis=0, concat_axis=0, tiled=True)

    hpsi_rows, hpsi = pl.pallas_call(
        lambda *refs: remote_kernel(terms, *refs),
        out_shape=(rows, rows),
        in_specs=[SMEM] * 3 + [VMEM] * 4,
        out_specs=(VMEM, HBM),
        scratch_shapes=[
            pltpu.VMEM(mats.shape, F32),
            pltpu.VMEM((count * terms, sector, 2 * sector), BF16),
            pltpu.SemaphoreType.DMA,
        ],
        compiler_params=roomy(56),
        cost_estimate=pl.CostEstimate(flops=4 * 10**9, bytes_accessed=6 * MIB, transcendentals=0),
        name="remote_terms",
    )(meta, rindex, out_index, came, near, left_parts, right_parts)

    residual_rows = pl.pallas_call(
        residual_kernel,
        out_shape=rows,
        in_specs=[VMEM] * 3,
        out_specs=VMEM,
        compiler_params=roomy(16),
        name="residual",
    )(sums, hpsi_rows, psi_rows)
    return (from_rows(hpsi, owned), from_rows(residual_rows, owned))


def solution(mesh):
    placed = (
        P(("groups", "renv"), None),
        P("groups", None),
        P(("groups", "renv"), None),
        P(("groups", "renv"), None),
        P(("groups", "renv"), None, None),
        P(("groups", "renv"), None, None),
        P(("groups", "renv"), None, None),
        P(("groups", "renv"), None, None),
        P(("groups", "renv")),
        P(("groups", "renv")),
        P(("groups", "renv")),
    )
    return jax.shard_map(
        shards,
        mesh=mesh,
        in_specs=placed,
        out_specs=(P(("groups", "renv"), None), P(("groups", "renv"), None)),
        check_vma=False,
    )
```

```python
import math

import jax
import jax.numpy as jnp
from jax import lax
from jax.experimental import pallas as pl
from jax.experimental.pallas import tpu as pltpu
from jax.sharding import PartitionSpec as P

F32 = jnp.float32
BF16 = jnp.bfloat16
SUB = 8
VMEM = pl.BlockSpec(memory_space=pltpu.VMEM)
SMEM = pl.BlockSpec(memory_space=pltpu.SMEM)
HBM = pl.BlockSpec(memory_space=pltpu.HBM)
MIB = 2**20


def as_rows(blocks, sector):
    count = blocks.shape[0]
    split = blocks.reshape(count // SUB, SUB, sector, sector)
    return split.transpose(0, 2, 1, 3).reshape(count * sector, sector)


def from_rows(rows, count):
    sector = rows.shape[1]
    split = rows.reshape(count // SUB, sector, SUB, sector)
    return split.transpose(0, 2, 1, 3).reshape(count, sector * sector)


def pick(ref, block):
    sector = ref.shape[1]
    start = (block // SUB) * (SUB * sector) + block % SUB
    return ref[pl.ds(start, sector, stride=SUB), :]


def halves(mat):
    high = mat.astype(BF16)
    low = (mat - high.astype(F32)).astype(BF16)
    return jnp.concatenate([high, low], axis=1)


def doubled(mat):
    both = halves(mat)
    return jnp.concatenate([both, both], axis=0)


def product(left, right):
    sector = right.shape[1] // 2
    wide = jnp.dot(left, right, preferred_element_type=F32)
    return wide[:, :sector] + wide[:, sector:]


def stacked(mat):
    high = mat.astype(BF16)
    low = (mat - high.astype(F32)).astype(BF16)
    rows = [jnp.concatenate([part, part], axis=1) for part in (high, low)]
    return jnp.concatenate(rows, axis=0)


def product_t(left, right):
    sector = right.shape[0] // 2
    wide = lax.dot_general(left, right, (((1,), (1,)), ((), ())), preferred_element_type=F32)
    return wide[:, :sector] + wide[:, sector:]


def twice(part):
    return jnp.concatenate([part, part], axis=0)


def roomy(mib):
    return pltpu.CompilerParams(vmem_limit_bytes=mib * MIB)


def gather_kernel(block_ref, psi_rows, out_hbm, stage, sems):
    puts = []
    for i in range(stage.shape[0]):
        stage[i] = pick(psi_rows, block_ref[i])
        put = pltpu.make_async_copy(stage.at[i], out_hbm.at[i], sems.at[i])
        put.start()
        puts.append(put)
    for put in puts:
        put.wait()


def turn_kernel(left_ref, live_ref, rindex_ref, out_index_ref, psi_rows, right_rows, meta_ref, turned_ref, rights_ref, psis_ref, stacks_ref):
    slots, terms, _ = left_ref.shape
    width = meta_ref.shape[2]
    lane = lax.broadcasted_iota(jnp.int32, (1, width), 1)

    def row(i, carry):
        values = jnp.zeros((1, width), jnp.int32)
        for g in range(terms):
            values = jnp.where(lane == g, left_ref[i % slots, g, i // slots], values)
            values = jnp.where(lane == terms + g, live_ref[i % slots, g, i // slots], values)
        meta_ref[i] = values
        return carry

    lax.fori_loop(0, meta_ref.shape[0], row, 0, unroll=4)

    def split_right(i, carry):
        rights_ref[i] = halves(pick(right_rows, i))
        return carry

    lax.fori_loop(0, rights_ref.shape[0], split_right, 0, unroll=4)

    def split_psi(i, carry):
        mat = pick(psi_rows, i)
        psis_ref[i] = halves(mat)
        stacks_ref[i] = stacked(mat)
        return carry

    lax.fori_loop(0, psis_ref.shape[0], split_psi, 0, unroll=4)

    def turn(i, carry):
        inner = []
        for g in range(terms):
            right = rights_ref[rindex_ref[i % slots, g, i // slots]]
            inner.append(halves(product_t(right, stacks_ref[out_index_ref[i % slots, g, i // slots]])))
        turned_ref[i] = jnp.concatenate(inner, axis=1)
        return carry

    lax.fori_loop(0, turned_ref.shape[0], turn, 0, unroll=4)


def local_kernel(block_ref, left_ref, right_ref, psi_rows, left_rows, psis_ref, rights_ref, near_ref, sums_ref, moved_ref):
    near_ref[...] = jnp.zeros_like(near_ref)

    def left_step(k, carry):
        moved = product(halves(pick(left_rows, left_ref[k])), twice(psis_ref[block_ref[k]]))
        moved_ref[k] = halves(moved)
        return carry

    lax.fori_loop(0, block_ref.shape[0], left_step, 0, unroll=8)

    def right_step(k, carry):
        near_ref[block_ref[k]] += product(moved_ref[k], twice(rights_ref[right_ref[k]]))
        return carry

    lax.fori_loop(0, block_ref.shape[0], right_step, 0, unroll=8)
    corr = jnp.zeros((1, sums_ref.shape[1]), F32)
    norm = jnp.zeros((1, sums_ref.shape[1]), F32)
    for b in range(near_ref.shape[0]):
        mat = pick(psi_rows, b)
        corr += jnp.sum(mat * near_ref[b], axis=0, keepdims=True)
        norm += jnp.sum(mat * mat, axis=0, keepdims=True)
    row = lax.broadcasted_iota(jnp.int32, sums_ref.shape, 0)
    sums_ref[...] = jnp.where(row == 0, corr, jnp.where(row == 1, norm, 0.0))


def adjoint_kernel(terms, meta_ref, left_rows, turned_ref, adjoint_ref, lefts_ref):
    sector = left_rows.shape[1]

    def sender(i, carry):
        weights = []
        for g in range(terms):
            live = meta_ref[i, 0, terms + g].astype(F32)
            left = halves(pick(left_rows, meta_ref[i, 0, g]) * live)
            lefts_ref[i, g * sector : (g + 1) * sector] = left
            weights.append(twice(left))
        adjoint_ref[i] = product(turned_ref[i], jnp.concatenate(weights, axis=0)).T
        return carry

    lax.fori_loop(0, adjoint_ref.shape[0], sender, 0, unroll=4)


def overlap_kernel(came_ref, adjoint_ref, near_sums_ref, out_ref):
    def block(i, total):
        return total + jnp.sum((came_ref[i] * adjoint_ref[i]).reshape(-1, SUB, came_ref.shape[2]), axis=0)

    total = lax.fori_loop(0, came_ref.shape[0], block, jnp.zeros(out_ref.shape[1:], F32), unroll=4)
    corr = jnp.sum(total, axis=0, keepdims=True)
    row = lax.broadcasted_iota(jnp.int32, total.shape, 0)
    mine = near_sums_ref[...] + jnp.where(row == 0, corr, 0.0)
    for i in range(out_ref.shape[0]):
        out_ref[i] = mine


def remote_kernel(rindex_ref, out_index_ref, came_ref, near_ref, lefts_ref, rights_ref, hpsi_rows, hpsi_hbm, acc, moved_ref, sem):
    count, sector, _ = came_ref.shape
    slots, terms, _ = rindex_ref.shape
    acc[...] = near_ref[...]

    def left_step(i, carry):
        moved_ref[i] = halves(product(lefts_ref[i], doubled(came_ref[i])))
        return carry

    lax.fori_loop(0, count, left_step, 0, unroll=4)

    def right_step(i, carry):
        for g in range(terms):
            right = rights_ref[rindex_ref[i % slots, g, i // slots]]
            acc[out_index_ref[i % slots, g, i // slots]] += product(moved_ref[i, g * sector : (g + 1) * sector], twice(right))
        return carry

    lax.fori_loop(0, count, right_step, 0, unroll=4)
    for b in range(acc.shape[0]):
        start = (b // SUB) * (SUB * sector) + b % SUB
        hpsi_rows[pl.ds(start, sector, stride=SUB), :] = acc[b]
    put = pltpu.make_async_copy(hpsi_rows, hpsi_hbm, sem)
    put.start()
    put.wait()


def residual_kernel(sums_ref, hpsi_rows, psi_rows, out_ref):
    total = jnp.sum(sums_ref[...], axis=0)
    whole = jnp.sum(total, axis=1, keepdims=True)
    theta = whole[0:1] / (whole[1:2] + 1e-06)
    out_ref[...] = hpsi_rows[...] - theta * psi_rows[...]


def shards(
    psi,
    left_env,
    right_env,
    send_block,
    send_left,
    send_live,
    recv_right,
    recv_out,
    loc_block,
    loc_left,
    loc_right,
):
    peers = lax.axis_size("renv")
    owned = psi.shape[0]
    sector = math.isqrt(psi.shape[1])
    slots = send_block.shape[1]
    terms = send_left.shape[2]
    count = peers * slots
    rights = right_env.shape[0]
    psi_rows = as_rows(psi, sector)
    left_rows = as_rows(left_env, sector)
    right_rows = as_rows(right_env, sector)
    by_slot = [index.transpose(1, 2, 0) for index in (send_left, send_live, recv_right, recv_out)]
    blocks = jax.ShapeDtypeStruct((count, sector, sector), F32)
    rows = jax.ShapeDtypeStruct((owned * sector, sector), F32)
    mats = jax.ShapeDtypeStruct((owned, sector, sector), F32)
    tile = jax.ShapeDtypeStruct((SUB, sector), F32)

    sent = pl.pallas_call(
        gather_kernel,
        out_shape=blocks,
        in_specs=[SMEM, VMEM],
        out_specs=HBM,
        scratch_shapes=[pltpu.VMEM(blocks.shape, F32), pltpu.SemaphoreType.DMA((count,))],
        compiler_params=roomy(56),
        name="gather_blocks",
    )(send_block.reshape(-1), psi_rows)
    came = lax.all_to_all(sent.reshape(peers, slots, sector, sector), "renv", split_axis=0, concat_axis=0, tiled=True)
    came = came.reshape(count, sector, sector)

    meta, turned, right_parts, psi_parts = pl.pallas_call(
        turn_kernel,
        out_shape=(
            jax.ShapeDtypeStruct((count, 1, sector), jnp.int32),
            jax.ShapeDtypeStruct((count, sector, terms * 2 * sector), BF16),
            jax.ShapeDtypeStruct((rights, sector, 2 * sector), BF16),
            jax.ShapeDtypeStruct((owned, sector, 2 * sector), BF16),
        ),
        in_specs=[SMEM] * 4 + [VMEM] * 2,
        out_specs=(VMEM,) * 4,
        scratch_shapes=[pltpu.VMEM((owned, 2 * sector, 2 * sector), BF16)],
        compiler_params=roomy(56),
        cost_estimate=pl.CostEstimate(flops=4 * 10**9, bytes_accessed=6 * MIB, transcendentals=0),
        name="turn",
    )(*by_slot, psi_rows, right_rows)
    meta = lax.all_to_all(meta, "renv", split_axis=0, concat_axis=0, tiled=True)

    near, near_sums = pl.pallas_call(
        local_kernel,
        out_shape=(mats, tile),
        in_specs=[SMEM] * 3 + [VMEM] * 4,
        out_specs=(VMEM,) * 2,
        scratch_shapes=[pltpu.VMEM((loc_block.shape[0], sector, 2 * sector), BF16)],
        compiler_params=roomy(56),
        cost_estimate=pl.CostEstimate(flops=4 * 10**9, bytes_accessed=6 * MIB, transcendentals=0),
        name="local_terms",
    )(loc_block, loc_left, loc_right, psi_rows, left_rows, psi_parts, right_parts)

    adjoint, left_parts = pl.pallas_call(
        lambda *refs: adjoint_kernel(terms, *refs),
        out_shape=(blocks, jax.ShapeDtypeStruct((count, terms * sector, 2 * sector), BF16)),
        in_specs=[SMEM] + [VMEM] * 2,
        out_specs=(VMEM,) * 2,
        compiler_params=roomy(48),
        cost_estimate=pl.CostEstimate(flops=4 * 10**9, bytes_accessed=10 * MIB, transcendentals=0),
        name="adjoint_blocks",
    )(meta, left_rows, turned)

    sums = pl.pallas_call(
        overlap_kernel,
        out_shape=jax.ShapeDtypeStruct((peers, SUB, sector), F32),
        in_specs=[VMEM] * 3,
        out_specs=VMEM,
        compiler_params=roomy(24),
        name="overlap",
    )(came, adjoint, near_sums)
    sums = lax.all_to_all(sums, "renv", split_axis=0, concat_axis=0, tiled=True)

    hpsi_rows, hpsi = pl.pallas_call(
        remote_kernel,
        out_shape=(rows, rows),
        in_specs=[SMEM] * 2 + [VMEM] * 4,
        out_specs=(VMEM, HBM),
        scratch_shapes=[
            pltpu.VMEM(mats.shape, F32),
            pltpu.VMEM((count, terms * sector, 2 * sector), BF16),
            pltpu.SemaphoreType.DMA,
        ],
        compiler_params=roomy(48),
        cost_estimate=pl.CostEstimate(flops=4 * 10**9, bytes_accessed=6 * MIB, transcendentals=0),
        name="remote_terms",
    )(*by_slot[2:], came, near, left_parts, right_parts)

    residual_rows = pl.pallas_call(
        residual_kernel,
        out_shape=rows,
        in_specs=[VMEM] * 3,
        out_specs=VMEM,
        compiler_params=roomy(16),
        name="residual",
    )(sums, hpsi_rows, psi_rows)
    return (from_rows(hpsi, owned), from_rows(residual_rows, owned))


def solution(mesh):
    placed = (
        P(("groups", "renv"), None),
        P("groups", None),
        P(("groups", "renv"), None),
        P(("groups", "renv"), None),
        P(("groups", "renv"), None, None),
        P(("groups", "renv"), None, None),
        P(("groups", "renv"), None, None),
        P(("groups", "renv"), None, None),
        P(("groups", "renv")),
        P(("groups", "renv")),
        P(("groups", "renv")),
    )
    return jax.shard_map(
        shards,
        mesh=mesh,
        in_specs=placed,
        out_specs=(P(("groups", "renv"), None), P(("groups", "renv"), None)),
        check_vma=False,
    )
```

```python
import math

import jax
import jax.numpy as jnp
from jax import lax
from jax.experimental import pallas as pl
from jax.experimental.pallas import tpu as pltpu
from jax.sharding import PartitionSpec as P

F32 = jnp.float32
BF16 = jnp.bfloat16
SUB = 8
VMEM = pl.BlockSpec(memory_space=pltpu.VMEM)
SMEM = pl.BlockSpec(memory_space=pltpu.SMEM)
HBM = pl.BlockSpec(memory_space=pltpu.HBM)
MIB = 2**20
LIGHT = pl.CostEstimate(flops=10**6, bytes_accessed=2**16, transcendentals=0)


def as_rows(blocks, sector):
    count = blocks.shape[0]
    split = blocks.reshape(count // SUB, SUB, sector, sector)
    return split.transpose(0, 2, 1, 3).reshape(count * sector, sector)


def from_rows(rows, count):
    sector = rows.shape[1]
    split = rows.reshape(count // SUB, sector, SUB, sector)
    return split.transpose(0, 2, 1, 3).reshape(count, sector * sector)


def pick(ref, block):
    sector = ref.shape[1]
    start = (block // SUB) * (SUB * sector) + block % SUB
    return ref[pl.ds(start, sector, stride=SUB), :]


def halves(mat):
    high = mat.astype(BF16)
    low = (mat - high.astype(F32)).astype(BF16)
    return jnp.concatenate([high, low], axis=1)


def doubled(mat):
    both = halves(mat)
    return jnp.concatenate([both, both], axis=0)


def product(left, right):
    sector = right.shape[1] // 2
    wide = jnp.dot(left, right, preferred_element_type=F32)
    return wide[:, :sector] + wide[:, sector:]


def stacked(mat):
    high = mat.astype(BF16)
    low = (mat - high.astype(F32)).astype(BF16)
    rows = [jnp.concatenate([part, part], axis=1) for part in (high, low)]
    return jnp.concatenate(rows, axis=0)


def product_t(left, right):
    sector = right.shape[0] // 2
    wide = lax.dot_general(left, right, (((1,), (1,)), ((), ())), preferred_element_type=F32)
    return wide[:, :sector] + wide[:, sector:]


def twice(part):
    return jnp.concatenate([part, part], axis=0)


def roomy(mib):
    return pltpu.CompilerParams(vmem_limit_bytes=mib * MIB)


def gather_kernel(block_ref, psi_rows, out_hbm, stage, sems):
    puts = []
    for i in range(stage.shape[0]):
        stage[i] = pick(psi_rows, block_ref[i])
        put = pltpu.make_async_copy(stage.at[i], out_hbm.at[i], sems.at[i])
        put.start()
        puts.append(put)
    for put in puts:
        put.wait()


def turn_kernel(sent_hbm, left_ref, live_ref, rindex_ref, out_index_ref, psi_rows, right_rows, meta_ref, turned_ref, rights_ref, psis_ref, stacks_ref):
    slots, terms, _ = left_ref.shape
    width = meta_ref.shape[2]
    lane = lax.broadcasted_iota(jnp.int32, (1, width), 1)

    def row(i, carry):
        values = jnp.zeros((1, width), jnp.int32)
        for g in range(terms):
            values = jnp.where(lane == g, left_ref[i % slots, g, i // slots], values)
            values = jnp.where(lane == terms + g, live_ref[i % slots, g, i // slots], values)
        meta_ref[i] = values
        return carry

    lax.fori_loop(0, meta_ref.shape[0], row, 0, unroll=4)

    def split_right(i, carry):
        rights_ref[i] = halves(pick(right_rows, i))
        return carry

    lax.fori_loop(0, rights_ref.shape[0], split_right, 0, unroll=4)

    def split_psi(i, carry):
        mat = pick(psi_rows, i)
        psis_ref[i] = halves(mat)
        stacks_ref[i] = stacked(mat)
        return carry

    lax.fori_loop(0, psis_ref.shape[0], split_psi, 0, unroll=4)

    def turn(i, carry):
        inner = []
        for g in range(terms):
            right = rights_ref[rindex_ref[i % slots, g, i // slots]]
            inner.append(halves(product_t(right, stacks_ref[out_index_ref[i % slots, g, i // slots]])))
        turned_ref[i] = jnp.concatenate(inner, axis=1)
        return carry

    lax.fori_loop(0, turned_ref.shape[0], turn, 0, unroll=4)


def local_kernel(block_ref, left_ref, right_ref, psi_rows, left_rows, psis_ref, rights_ref, near_ref, sums_ref, moved_ref):
    near_ref[...] = jnp.zeros_like(near_ref)

    def left_step(k, carry):
        moved = product(halves(pick(left_rows, left_ref[k])), twice(psis_ref[block_ref[k]]))
        moved_ref[k] = halves(moved)
        return carry

    lax.fori_loop(0, block_ref.shape[0], left_step, 0, unroll=8)

    def right_step(k, carry):
        near_ref[block_ref[k]] += product(moved_ref[k], twice(rights_ref[right_ref[k]]))
        return carry

    lax.fori_loop(0, block_ref.shape[0], right_step, 0, unroll=8)
    corr = jnp.zeros((1, sums_ref.shape[1]), F32)
    norm = jnp.zeros((1, sums_ref.shape[1]), F32)
    for b in range(near_ref.shape[0]):
        mat = pick(psi_rows, b)
        corr += jnp.sum(mat * near_ref[b], axis=0, keepdims=True)
        norm += jnp.sum(mat * mat, axis=0, keepdims=True)
    row = lax.broadcasted_iota(jnp.int32, sums_ref.shape, 0)
    sums_ref[...] = jnp.where(row == 0, corr, jnp.where(row == 1, norm, 0.0))


def adjoint_kernel(terms, meta_ref, left_rows, turned_ref, adjoint_ref, lefts_ref):
    sector = left_rows.shape[1]

    def sender(i, carry):
        weights = []
        for g in range(terms):
            live = meta_ref[i, 0, terms + g].astype(F32)
            left = halves(pick(left_rows, meta_ref[i, 0, g]) * live)
            lefts_ref[i, g * sector : (g + 1) * sector] = left
            weights.append(twice(left))
        adjoint_ref[i] = product(turned_ref[i], jnp.concatenate(weights, axis=0)).T
        return carry

    lax.fori_loop(0, adjoint_ref.shape[0], sender, 0, unroll=4)


def overlap_kernel(came_ref, adjoint_ref, near_sums_ref, out_ref):
    def block(i, total):
        return total + jnp.sum((came_ref[i] * adjoint_ref[i]).reshape(-1, SUB, came_ref.shape[2]), axis=0)

    total = lax.fori_loop(0, came_ref.shape[0], block, jnp.zeros(out_ref.shape[1:], F32), unroll=4)
    corr = jnp.sum(total, axis=0, keepdims=True)
    row = lax.broadcasted_iota(jnp.int32, total.shape, 0)
    mine = near_sums_ref[...] + jnp.where(row == 0, corr, 0.0)
    for i in range(out_ref.shape[0]):
        out_ref[i] = mine


def remote_kernel(rindex_ref, out_index_ref, came_ref, near_ref, lefts_ref, rights_ref, hpsi_rows, hpsi_hbm, acc, moved_ref, sem):
    count, sector, _ = came_ref.shape
    slots, terms, _ = rindex_ref.shape
    acc[...] = near_ref[...]

    def left_step(i, carry):
        moved_ref[i] = halves(product(lefts_ref[i], doubled(came_ref[i])))
        return carry

    lax.fori_loop(0, count, left_step, 0, unroll=4)

    def right_step(i, carry):
        for g in range(terms):
            right = rights_ref[rindex_ref[i % slots, g, i // slots]]
            acc[out_index_ref[i % slots, g, i // slots]] += product(moved_ref[i, g * sector : (g + 1) * sector], twice(right))
        return carry

    lax.fori_loop(0, count, right_step, 0, unroll=4)
    for b in range(acc.shape[0]):
        start = (b // SUB) * (SUB * sector) + b % SUB
        hpsi_rows[pl.ds(start, sector, stride=SUB), :] = acc[b]
    put = pltpu.make_async_copy(hpsi_rows, hpsi_hbm, sem)
    put.start()
    put.wait()


def residual_kernel(sums_ref, hpsi_rows, psi_rows, out_ref):
    total = jnp.sum(sums_ref[...], axis=0)
    whole = jnp.sum(total, axis=1, keepdims=True)
    theta = whole[0:1] / (whole[1:2] + 1e-06)
    out_ref[...] = hpsi_rows[...] - theta * psi_rows[...]


def shards(
    psi,
    left_env,
    right_env,
    send_block,
    send_left,
    send_live,
    recv_right,
    recv_out,
    loc_block,
    loc_left,
    loc_right,
):
    peers = lax.axis_size("renv")
    owned = psi.shape[0]
    sector = math.isqrt(psi.shape[1])
    slots = send_block.shape[1]
    terms = send_left.shape[2]
    count = peers * slots
    rights = right_env.shape[0]
    psi_rows = as_rows(psi, sector)
    left_rows = as_rows(left_env, sector)
    right_rows = as_rows(right_env, sector)
    by_slot = [index.transpose(1, 2, 0) for index in (send_left, send_live, recv_right, recv_out)]
    blocks = jax.ShapeDtypeStruct((count, sector, sector), F32)
    rows = jax.ShapeDtypeStruct((owned * sector, sector), F32)
    mats = jax.ShapeDtypeStruct((owned, sector, sector), F32)
    tile = jax.ShapeDtypeStruct((SUB, sector), F32)

    sent = pl.pallas_call(
        gather_kernel,
        out_shape=blocks,
        in_specs=[SMEM, VMEM],
        out_specs=HBM,
        scratch_shapes=[pltpu.VMEM(blocks.shape, F32), pltpu.SemaphoreType.DMA((count,))],
        compiler_params=roomy(56),
        name="gather_blocks",
    )(send_block.reshape(-1), psi_rows)
    came = lax.all_to_all(sent.reshape(peers, slots, sector, sector), "renv", split_axis=0, concat_axis=0, tiled=True)
    came = came.reshape(count, sector, sector)

    meta, turned, right_parts, psi_parts = pl.pallas_call(
        turn_kernel,
        out_shape=(
            jax.ShapeDtypeStruct((count, 1, sector), jnp.int32),
            jax.ShapeDtypeStruct((count, sector, terms * 2 * sector), BF16),
            jax.ShapeDtypeStruct((rights, sector, 2 * sector), BF16),
            jax.ShapeDtypeStruct((owned, sector, 2 * sector), BF16),
        ),
        in_specs=[HBM] + [SMEM] * 4 + [VMEM] * 2,
        out_specs=(VMEM,) * 4,
        scratch_shapes=[pltpu.VMEM((owned, 2 * sector, 2 * sector), BF16)],
        compiler_params=roomy(56),
        cost_estimate=LIGHT,
        name="turn",
    )(sent, *by_slot, psi_rows, right_rows)
    meta = lax.all_to_all(meta, "renv", split_axis=0, concat_axis=0, tiled=True)

    near, near_sums = pl.pallas_call(
        local_kernel,
        out_shape=(mats, tile),
        in_specs=[SMEM] * 3 + [VMEM] * 4,
        out_specs=(VMEM,) * 2,
        scratch_shapes=[pltpu.VMEM((loc_block.shape[0], sector, 2 * sector), BF16)],
        compiler_params=roomy(56),
        cost_estimate=LIGHT,
        name="local_terms",
    )(loc_block, loc_left, loc_right, psi_rows, left_rows, psi_parts, right_parts)

    adjoint, left_parts = pl.pallas_call(
        lambda *refs: adjoint_kernel(terms, *refs),
        out_shape=(blocks, jax.ShapeDtypeStruct((count, terms * sector, 2 * sector), BF16)),
        in_specs=[SMEM] + [VMEM] * 2,
        out_specs=(VMEM,) * 2,
        compiler_params=roomy(48),
        cost_estimate=LIGHT,
        name="adjoint_blocks",
    )(meta, left_rows, turned)

    sums = pl.pallas_call(
        overlap_kernel,
        out_shape=jax.ShapeDtypeStruct((peers, SUB, sector), F32),
        in_specs=[VMEM] * 3,
        out_specs=VMEM,
        compiler_params=roomy(24),
        name="overlap",
    )(came, adjoint, near_sums)
    sums = lax.all_to_all(sums, "renv", split_axis=0, concat_axis=0, tiled=True)

    hpsi_rows, hpsi = pl.pallas_call(
        remote_kernel,
        out_shape=(rows, rows),
        in_specs=[SMEM] * 2 + [VMEM] * 4,
        out_specs=(VMEM, HBM),
        scratch_shapes=[
            pltpu.VMEM(mats.shape, F32),
            pltpu.VMEM((count, terms * sector, 2 * sector), BF16),
            pltpu.SemaphoreType.DMA,
        ],
        compiler_params=roomy(48),
        cost_estimate=pl.CostEstimate(flops=4 * 10**9, bytes_accessed=6 * MIB, transcendentals=0),
        name="remote_terms",
    )(*by_slot[2:], came, near, left_parts, right_parts)

    residual_rows = pl.pallas_call(
        residual_kernel,
        out_shape=rows,
        in_specs=[VMEM] * 3,
        out_specs=VMEM,
        compiler_params=roomy(16),
        name="residual",
    )(sums, hpsi_rows, psi_rows)
    return (from_rows(hpsi, owned), from_rows(residual_rows, owned))


def solution(mesh):
    placed = (
        P(("groups", "renv"), None),
        P("groups", None),
        P(("groups", "renv"), None),
        P(("groups", "renv"), None),
        P(("groups", "renv"), None, None),
        P(("groups", "renv"), None, None),
        P(("groups", "renv"), None, None),
        P(("groups", "renv"), None, None),
        P(("groups", "renv")),
        P(("groups", "renv")),
        P(("groups", "renv")),
    )
    return jax.shard_map(
        shards,
        mesh=mesh,
        in_specs=placed,
        out_specs=(P(("groups", "renv"), None), P(("groups", "renv"), None)),
        check_vma=False,
    )
```

```python
import math

import jax
import jax.numpy as jnp
from jax import lax
from jax.experimental import pallas as pl
from jax.experimental.pallas import tpu as pltpu
from jax.sharding import PartitionSpec as P

F32 = jnp.float32
BF16 = jnp.bfloat16
SUB = 8
VMEM = pl.BlockSpec(memory_space=pltpu.VMEM)
SMEM = pl.BlockSpec(memory_space=pltpu.SMEM)
HBM = pl.BlockSpec(memory_space=pltpu.HBM)
MIB = 2**20
LIGHT = pl.CostEstimate(flops=10**6, bytes_accessed=2**16, transcendentals=0)


def as_rows(blocks, sector):
    count = blocks.shape[0]
    split = blocks.reshape(count // SUB, SUB, sector, sector)
    return split.transpose(0, 2, 1, 3).reshape(count * sector, sector)


def from_rows(rows, count):
    sector = rows.shape[1]
    split = rows.reshape(count // SUB, sector, SUB, sector)
    return split.transpose(0, 2, 1, 3).reshape(count, sector * sector)


def pick(ref, block):
    sector = ref.shape[1]
    start = (block // SUB) * (SUB * sector) + block % SUB
    return ref[pl.ds(start, sector, stride=SUB), :]


def halves(mat):
    high = mat.astype(BF16)
    low = (mat - high.astype(F32)).astype(BF16)
    return jnp.concatenate([high, low], axis=1)


def doubled(mat):
    both = halves(mat)
    return jnp.concatenate([both, both], axis=0)


def product(left, right):
    sector = right.shape[1] // 2
    wide = jnp.dot(left, right, preferred_element_type=F32)
    return wide[:, :sector] + wide[:, sector:]


def stacked(mat):
    high = mat.astype(BF16)
    low = (mat - high.astype(F32)).astype(BF16)
    rows = [jnp.concatenate([part, part], axis=1) for part in (high, low)]
    return jnp.concatenate(rows, axis=0)


def product_t(left, right):
    sector = right.shape[0] // 2
    wide = lax.dot_general(left, right, (((1,), (1,)), ((), ())), preferred_element_type=F32)
    return wide[:, :sector] + wide[:, sector:]


def twice(part):
    return jnp.concatenate([part, part], axis=0)


def roomy(mib):
    return pltpu.CompilerParams(vmem_limit_bytes=mib * MIB)


def gather_kernel(block_ref, psi_rows, out_hbm, stage, sems):
    puts = []
    for i in range(stage.shape[0]):
        stage[i] = pick(psi_rows, block_ref[i])
        put = pltpu.make_async_copy(stage.at[i], out_hbm.at[i], sems.at[i])
        put.start()
        puts.append(put)
    for put in puts:
        put.wait()


def index_kernel(sent_hbm, left_ref, live_ref, meta_ref):
    slots, terms, peers = left_ref.shape
    lane = lax.broadcasted_iota(jnp.int32, meta_ref.shape, 1)
    values = jnp.zeros(meta_ref.shape, jnp.int32)
    for i in range(peers * slots):
        for g in range(terms):
            at = i * 2 * terms + g
            values = jnp.where(lane == at, left_ref[i % slots, g, i // slots], values)
            values = jnp.where(lane == at + terms, live_ref[i % slots, g, i // slots], values)
    meta_ref[...] = values


def turn_kernel(sent_hbm, rindex_ref, out_index_ref, psi_rows, right_rows, turned_ref, rights_ref, psis_ref, stacks_ref):
    slots, terms, _ = rindex_ref.shape

    def split_right(i, carry):
        rights_ref[i] = halves(pick(right_rows, i))
        return carry

    lax.fori_loop(0, rights_ref.shape[0], split_right, 0, unroll=4)

    def split_psi(i, carry):
        mat = pick(psi_rows, i)
        psis_ref[i] = halves(mat)
        stacks_ref[i] = stacked(mat)
        return carry

    lax.fori_loop(0, psis_ref.shape[0], split_psi, 0, unroll=4)

    def turn(i, carry):
        inner = []
        for g in range(terms):
            right = rights_ref[rindex_ref[i % slots, g, i // slots]]
            inner.append(halves(product_t(right, stacks_ref[out_index_ref[i % slots, g, i // slots]])))
        turned_ref[i] = jnp.concatenate(inner, axis=1)
        return carry

    lax.fori_loop(0, turned_ref.shape[0], turn, 0, unroll=4)


def local_kernel(block_ref, left_ref, right_ref, psi_rows, left_rows, psis_ref, rights_ref, near_ref, sums_ref, moved_ref):
    near_ref[...] = jnp.zeros_like(near_ref)

    def left_step(k, carry):
        moved = product(halves(pick(left_rows, left_ref[k])), twice(psis_ref[block_ref[k]]))
        moved_ref[k] = halves(moved)
        return carry

    lax.fori_loop(0, block_ref.shape[0], left_step, 0, unroll=8)

    def right_step(k, carry):
        near_ref[block_ref[k]] += product(moved_ref[k], twice(rights_ref[right_ref[k]]))
        return carry

    lax.fori_loop(0, block_ref.shape[0], right_step, 0, unroll=8)
    corr = jnp.zeros((1, sums_ref.shape[1]), F32)
    norm = jnp.zeros((1, sums_ref.shape[1]), F32)
    for b in range(near_ref.shape[0]):
        mat = pick(psi_rows, b)
        corr += jnp.sum(mat * near_ref[b], axis=0, keepdims=True)
        norm += jnp.sum(mat * mat, axis=0, keepdims=True)
    row = lax.broadcasted_iota(jnp.int32, sums_ref.shape, 0)
    sums_ref[...] = jnp.where(row == 0, corr, jnp.where(row == 1, norm, 0.0))


def adjoint_kernel(slots, terms, me_ref, meta_ref, left_rows, turned_ref, adjoint_ref, lefts_ref):
    sector = left_rows.shape[1]

    def sender(i, carry):
        weights = []
        row = lax.bitwise_xor(i // slots, me_ref[0])
        base = (me_ref[0] * slots + i % slots) * 2 * terms
        for g in range(terms):
            live = meta_ref[row, base + terms + g].astype(F32)
            left = halves(pick(left_rows, meta_ref[row, base + g]) * live)
            lefts_ref[i, g * sector : (g + 1) * sector] = left
            weights.append(twice(left))
        adjoint_ref[i] = product(turned_ref[i], jnp.concatenate(weights, axis=0)).T
        return carry

    lax.fori_loop(0, adjoint_ref.shape[0], sender, 0, unroll=4)


def overlap_kernel(came_ref, adjoint_ref, near_sums_ref, out_ref):
    def block(i, total):
        return total + jnp.sum((came_ref[i] * adjoint_ref[i]).reshape(-1, SUB, came_ref.shape[2]), axis=0)

    total = lax.fori_loop(0, came_ref.shape[0], block, jnp.zeros(out_ref.shape[1:], F32), unroll=4)
    corr = jnp.sum(total, axis=0, keepdims=True)
    row = lax.broadcasted_iota(jnp.int32, total.shape, 0)
    mine = near_sums_ref[...] + jnp.where(row == 0, corr, 0.0)
    for i in range(out_ref.shape[0]):
        out_ref[i] = mine


def remote_kernel(rindex_ref, out_index_ref, came_ref, near_ref, lefts_ref, rights_ref, hpsi_rows, hpsi_hbm, acc, moved_ref, sem):
    count, sector, _ = came_ref.shape
    slots, terms, _ = rindex_ref.shape
    acc[...] = near_ref[...]

    def left_step(i, carry):
        moved_ref[i] = halves(product(lefts_ref[i], doubled(came_ref[i])))
        return carry

    lax.fori_loop(0, count, left_step, 0, unroll=4)

    def right_step(i, carry):
        for g in range(terms):
            right = rights_ref[rindex_ref[i % slots, g, i // slots]]
            acc[out_index_ref[i % slots, g, i // slots]] += product(moved_ref[i, g * sector : (g + 1) * sector], twice(right))
        return carry

    lax.fori_loop(0, count, right_step, 0, unroll=4)
    for b in range(acc.shape[0]):
        start = (b // SUB) * (SUB * sector) + b % SUB
        hpsi_rows[pl.ds(start, sector, stride=SUB), :] = acc[b]
    put = pltpu.make_async_copy(hpsi_rows, hpsi_hbm, sem)
    put.start()
    put.wait()


def residual_kernel(sums_ref, hpsi_rows, psi_rows, out_ref):
    total = jnp.sum(sums_ref[...], axis=0)
    whole = jnp.sum(total, axis=1, keepdims=True)
    theta = whole[0:1] / (whole[1:2] + 1e-06)
    out_ref[...] = hpsi_rows[...] - theta * psi_rows[...]


def shards(
    psi,
    left_env,
    right_env,
    send_block,
    send_left,
    send_live,
    recv_right,
    recv_out,
    loc_block,
    loc_left,
    loc_right,
):
    peers = lax.axis_size("renv")
    owned = psi.shape[0]
    sector = math.isqrt(psi.shape[1])
    slots = send_block.shape[1]
    terms = send_left.shape[2]
    count = peers * slots
    rights = right_env.shape[0]
    psi_rows = as_rows(psi, sector)
    left_rows = as_rows(left_env, sector)
    right_rows = as_rows(right_env, sector)
    me = lax.axis_index("renv").astype(jnp.int32).reshape(1)
    by_slot = [index.transpose(1, 2, 0) for index in (send_left, send_live, recv_right, recv_out)]
    blocks = jax.ShapeDtypeStruct((count, sector, sector), F32)
    rows = jax.ShapeDtypeStruct((owned * sector, sector), F32)
    mats = jax.ShapeDtypeStruct((owned, sector, sector), F32)
    tile = jax.ShapeDtypeStruct((SUB, sector), F32)

    sent = pl.pallas_call(
        gather_kernel,
        out_shape=blocks,
        in_specs=[SMEM, VMEM],
        out_specs=HBM,
        scratch_shapes=[pltpu.VMEM(blocks.shape, F32), pltpu.SemaphoreType.DMA((count,))],
        compiler_params=roomy(56),
        name="gather_blocks",
    )(send_block.reshape(-1), psi_rows)
    came = lax.all_to_all(sent.reshape(peers, slots, sector, sector), "renv", split_axis=0, concat_axis=0, tiled=True)
    came = came.reshape(count, sector, sector)

    lanes = -(-count * 2 * terms // 128) * 128
    meta = pl.pallas_call(
        index_kernel,
        out_shape=jax.ShapeDtypeStruct((1, lanes), jnp.int32),
        in_specs=[HBM] + [SMEM] * 2,
        out_specs=VMEM,
        compiler_params=roomy(56),
        cost_estimate=LIGHT,
        name="index_rows",
    )(sent, *by_slot[:2])
    step = 1
    while step < peers:
        meta = jnp.concatenate([meta, lax.ppermute(meta, "renv", [(s, s ^ step) for s in range(peers)])], axis=0)
        step *= 2

    turned, right_parts, psi_parts = pl.pallas_call(
        turn_kernel,
        out_shape=(
            jax.ShapeDtypeStruct((count, sector, terms * 2 * sector), BF16),
            jax.ShapeDtypeStruct((rights, sector, 2 * sector), BF16),
            jax.ShapeDtypeStruct((owned, sector, 2 * sector), BF16),
        ),
        in_specs=[HBM] + [SMEM] * 2 + [VMEM] * 2,
        out_specs=(VMEM,) * 3,
        scratch_shapes=[pltpu.VMEM((owned, 2 * sector, 2 * sector), BF16)],
        compiler_params=roomy(56),
        cost_estimate=LIGHT,
        name="turn",
    )(sent, *by_slot[2:], psi_rows, right_rows)

    near, near_sums = pl.pallas_call(
        local_kernel,
        out_shape=(mats, tile),
        in_specs=[SMEM] * 3 + [VMEM] * 4,
        out_specs=(VMEM,) * 2,
        scratch_shapes=[pltpu.VMEM((loc_block.shape[0], sector, 2 * sector), BF16)],
        compiler_params=roomy(56),
        cost_estimate=LIGHT,
        name="local_terms",
    )(loc_block, loc_left, loc_right, psi_rows, left_rows, psi_parts, right_parts)

    adjoint, left_parts = pl.pallas_call(
        lambda *refs: adjoint_kernel(slots, terms, *refs),
        out_shape=(blocks, jax.ShapeDtypeStruct((count, terms * sector, 2 * sector), BF16)),
        in_specs=[SMEM] * 2 + [VMEM] * 2,
        out_specs=(VMEM,) * 2,
        compiler_params=roomy(48),
        cost_estimate=LIGHT,
        name="adjoint_blocks",
    )(me, meta, left_rows, turned)

    sums = pl.pallas_call(
        overlap_kernel,
        out_shape=jax.ShapeDtypeStruct((peers, SUB, sector), F32),
        in_specs=[VMEM] * 3,
        out_specs=VMEM,
        compiler_params=roomy(24),
        name="overlap",
    )(came, adjoint, near_sums)
    sums = lax.all_to_all(sums, "renv", split_axis=0, concat_axis=0, tiled=True)

    hpsi_rows, hpsi = pl.pallas_call(
        remote_kernel,
        out_shape=(rows, rows),
        in_specs=[SMEM] * 2 + [VMEM] * 4,
        out_specs=(VMEM, HBM),
        scratch_shapes=[
            pltpu.VMEM(mats.shape, F32),
            pltpu.VMEM((count, terms * sector, 2 * sector), BF16),
            pltpu.SemaphoreType.DMA,
        ],
        compiler_params=roomy(48),
        cost_estimate=pl.CostEstimate(flops=4 * 10**9, bytes_accessed=6 * MIB, transcendentals=0),
        name="remote_terms",
    )(*by_slot[2:], came, near, left_parts, right_parts)

    residual_rows = pl.pallas_call(
        residual_kernel,
        out_shape=rows,
        in_specs=[VMEM] * 3,
        out_specs=VMEM,
        compiler_params=roomy(16),
        name="residual",
    )(sums, hpsi_rows, psi_rows)
    return (from_rows(hpsi, owned), from_rows(residual_rows, owned))


def solution(mesh):
    placed = (
        P(("groups", "renv"), None),
        P("groups", None),
        P(("groups", "renv"), None),
        P(("groups", "renv"), None),
        P(("groups", "renv"), None, None),
        P(("groups", "renv"), None, None),
        P(("groups", "renv"), None, None),
        P(("groups", "renv"), None, None),
        P(("groups", "renv")),
        P(("groups", "renv")),
        P(("groups", "renv")),
    )
    return jax.shard_map(
        shards,
        mesh=mesh,
        in_specs=placed,
        out_specs=(P(("groups", "renv"), None), P(("groups", "renv"), None)),
        check_vma=False,
    )
```

```python
import math

import jax
import jax.numpy as jnp
from jax import lax
from jax.experimental import pallas as pl
from jax.experimental.pallas import tpu as pltpu
from jax.sharding import PartitionSpec as P

F32 = jnp.float32
BF16 = jnp.bfloat16
SUB = 8
VMEM = pl.BlockSpec(memory_space=pltpu.VMEM)
SMEM = pl.BlockSpec(memory_space=pltpu.SMEM)
HBM = pl.BlockSpec(memory_space=pltpu.HBM)
MIB = 2**20
LIGHT = pl.CostEstimate(flops=10**6, bytes_accessed=2**16, transcendentals=0)


def as_rows(blocks, sector):
    count = blocks.shape[0]
    split = blocks.reshape(count // SUB, SUB, sector, sector)
    return split.transpose(0, 2, 1, 3).reshape(count * sector, sector)


def from_rows(rows, count):
    sector = rows.shape[1]
    split = rows.reshape(count // SUB, sector, SUB, sector)
    return split.transpose(0, 2, 1, 3).reshape(count, sector * sector)


def pick(ref, block):
    sector = ref.shape[1]
    start = (block // SUB) * (SUB * sector) + block % SUB
    return ref[pl.ds(start, sector, stride=SUB), :]


def halves(mat):
    high = mat.astype(BF16)
    low = (mat - high.astype(F32)).astype(BF16)
    return jnp.concatenate([high, low], axis=1)


def doubled(mat):
    both = halves(mat)
    return jnp.concatenate([both, both], axis=0)


def product(left, right):
    sector = right.shape[1] // 2
    wide = jnp.dot(left, right, preferred_element_type=F32)
    return wide[:, :sector] + wide[:, sector:]


def stacked(mat):
    high = mat.astype(BF16)
    low = (mat - high.astype(F32)).astype(BF16)
    rows = [jnp.concatenate([part, part], axis=1) for part in (high, low)]
    return jnp.concatenate(rows, axis=0)


def product_t(left, right):
    sector = right.shape[0] // 2
    wide = lax.dot_general(left, right, (((1,), (1,)), ((), ())), preferred_element_type=F32)
    return wide[:, :sector] + wide[:, sector:]


def twice(part):
    return jnp.concatenate([part, part], axis=0)


def roomy(mib):
    return pltpu.CompilerParams(vmem_limit_bytes=mib * MIB)


def gather_kernel(me_ref, block_ref, left_ref, live_ref, psi_rows, out_hbm, table_ref, stage, sems):
    slots, terms, _ = left_ref.shape
    puts = []
    for i in range(stage.shape[0]):
        stage[i] = pick(psi_rows, block_ref[i])
        put = pltpu.make_async_copy(stage.at[i], out_hbm.at[i], sems.at[i])
        put.start()
        puts.append(put)
    table_ref[...] = jnp.zeros(table_ref.shape, table_ref.dtype)
    lane = lax.broadcasted_iota(jnp.int32, (1, table_ref.shape[1]), 1)
    values = jnp.zeros(lane.shape, jnp.int32)
    for i in range(stage.shape[0]):
        for g in range(terms):
            at = i * 2 * terms + g
            values = jnp.where(lane == at, left_ref[i % slots, g, i // slots], values)
            values = jnp.where(lane == at + terms, live_ref[i % slots, g, i // slots], values)
    table_ref[pl.ds(me_ref[0], 1), :] = values
    for put in puts:
        put.wait()


def turn_kernel(sent_hbm, rindex_ref, out_index_ref, psi_rows, right_rows, turned_ref, rights_ref, psis_ref, stacks_ref):
    slots, terms, _ = rindex_ref.shape

    def split_right(i, carry):
        rights_ref[i] = halves(pick(right_rows, i))
        return carry

    lax.fori_loop(0, rights_ref.shape[0], split_right, 0, unroll=4)

    def split_psi(i, carry):
        mat = pick(psi_rows, i)
        psis_ref[i] = halves(mat)
        stacks_ref[i] = stacked(mat)
        return carry

    lax.fori_loop(0, psis_ref.shape[0], split_psi, 0, unroll=4)

    def turn(i, carry):
        inner = []
        for g in range(terms):
            right = rights_ref[rindex_ref[i % slots, g, i // slots]]
            inner.append(halves(product_t(right, stacks_ref[out_index_ref[i % slots, g, i // slots]])))
        turned_ref[i] = jnp.concatenate(inner, axis=1)
        return carry

    lax.fori_loop(0, turned_ref.shape[0], turn, 0, unroll=4)


def local_kernel(block_ref, left_ref, right_ref, psi_rows, left_rows, psis_ref, rights_ref, near_ref, sums_ref, moved_ref):
    near_ref[...] = jnp.zeros_like(near_ref)

    def left_step(k, carry):
        moved = product(halves(pick(left_rows, left_ref[k])), twice(psis_ref[block_ref[k]]))
        moved_ref[k] = halves(moved)
        return carry

    lax.fori_loop(0, block_ref.shape[0], left_step, 0, unroll=8)

    def right_step(k, carry):
        near_ref[block_ref[k]] += product(moved_ref[k], twice(rights_ref[right_ref[k]]))
        return carry

    lax.fori_loop(0, block_ref.shape[0], right_step, 0, unroll=8)
    corr = jnp.zeros((1, sums_ref.shape[1]), F32)
    norm = jnp.zeros((1, sums_ref.shape[1]), F32)
    for b in range(near_ref.shape[0]):
        mat = pick(psi_rows, b)
        corr += jnp.sum(mat * near_ref[b], axis=0, keepdims=True)
        norm += jnp.sum(mat * mat, axis=0, keepdims=True)
    row = lax.broadcasted_iota(jnp.int32, sums_ref.shape, 0)
    sums_ref[...] = jnp.where(row == 0, corr, jnp.where(row == 1, norm, 0.0))


def adjoint_kernel(slots, terms, me_ref, meta_ref, left_rows, turned_ref, adjoint_ref, lefts_ref):
    sector = left_rows.shape[1]

    def sender(i, carry):
        weights = []
        row = i // slots
        base = (me_ref[0] * slots + i % slots) * 2 * terms
        for g in range(terms):
            live = meta_ref[row, base + terms + g].astype(F32)
            left = halves(pick(left_rows, meta_ref[row, base + g]) * live)
            lefts_ref[i, g * sector : (g + 1) * sector] = left
            weights.append(twice(left))
        adjoint_ref[i] = product(turned_ref[i], jnp.concatenate(weights, axis=0)).T
        return carry

    lax.fori_loop(0, adjoint_ref.shape[0], sender, 0, unroll=4)


def overlap_kernel(came_ref, adjoint_ref, near_sums_ref, out_ref):
    def block(i, total):
        return total + jnp.sum((came_ref[i] * adjoint_ref[i]).reshape(-1, SUB, came_ref.shape[2]), axis=0)

    total = lax.fori_loop(0, came_ref.shape[0], block, jnp.zeros(out_ref.shape[1:], F32), unroll=4)
    corr = jnp.sum(total, axis=0, keepdims=True)
    row = lax.broadcasted_iota(jnp.int32, total.shape, 0)
    mine = near_sums_ref[...] + jnp.where(row == 0, corr, 0.0)
    for i in range(out_ref.shape[0]):
        out_ref[i] = mine


def remote_kernel(rindex_ref, out_index_ref, came_ref, near_ref, lefts_ref, rights_ref, hpsi_rows, hpsi_hbm, acc, moved_ref, sem):
    count, sector, _ = came_ref.shape
    slots, terms, _ = rindex_ref.shape
    acc[...] = near_ref[...]

    def left_step(i, carry):
        moved_ref[i] = halves(product(lefts_ref[i], doubled(came_ref[i])))
        return carry

    lax.fori_loop(0, count, left_step, 0, unroll=4)

    def right_step(i, carry):
        for g in range(terms):
            right = rights_ref[rindex_ref[i % slots, g, i // slots]]
            acc[out_index_ref[i % slots, g, i // slots]] += product(moved_ref[i, g * sector : (g + 1) * sector], twice(right))
        return carry

    lax.fori_loop(0, count, right_step, 0, unroll=4)
    for b in range(acc.shape[0]):
        start = (b // SUB) * (SUB * sector) + b % SUB
        hpsi_rows[pl.ds(start, sector, stride=SUB), :] = acc[b]
    put = pltpu.make_async_copy(hpsi_rows, hpsi_hbm, sem)
    put.start()
    put.wait()


def residual_kernel(sums_ref, hpsi_rows, psi_rows, out_ref):
    total = jnp.sum(sums_ref[...], axis=0)
    whole = jnp.sum(total, axis=1, keepdims=True)
    theta = whole[0:1] / (whole[1:2] + 1e-06)
    out_ref[...] = hpsi_rows[...] - theta * psi_rows[...]


def shards(
    psi,
    left_env,
    right_env,
    send_block,
    send_left,
    send_live,
    recv_right,
    recv_out,
    loc_block,
    loc_left,
    loc_right,
):
    peers = lax.axis_size("renv")
    owned = psi.shape[0]
    sector = math.isqrt(psi.shape[1])
    slots = send_block.shape[1]
    terms = send_left.shape[2]
    count = peers * slots
    rights = right_env.shape[0]
    psi_rows = as_rows(psi, sector)
    left_rows = as_rows(left_env, sector)
    right_rows = as_rows(right_env, sector)
    me = lax.axis_index("renv").astype(jnp.int32).reshape(1)
    by_slot = [index.transpose(1, 2, 0) for index in (send_left, send_live, recv_right, recv_out)]
    blocks = jax.ShapeDtypeStruct((count, sector, sector), F32)
    rows = jax.ShapeDtypeStruct((owned * sector, sector), F32)
    mats = jax.ShapeDtypeStruct((owned, sector, sector), F32)
    tile = jax.ShapeDtypeStruct((SUB, sector), F32)

    lanes = -(-count * 2 * terms // 128) * 128
    table = jax.ShapeDtypeStruct((-(-peers // 128) * 128, lanes), jnp.int32)
    sent, meta = pl.pallas_call(
        gather_kernel,
        out_shape=(blocks, table),
        in_specs=[SMEM] * 4 + [VMEM],
        out_specs=(HBM, VMEM),
        scratch_shapes=[pltpu.VMEM(blocks.shape, F32), pltpu.SemaphoreType.DMA((count,))],
        compiler_params=roomy(56),
        name="gather_blocks",
    )(me, send_block.reshape(-1), *by_slot[:2], psi_rows)
    meta = lax.psum(meta, "renv")
    came = lax.all_to_all(sent.reshape(peers, slots, sector, sector), "renv", split_axis=0, concat_axis=0, tiled=True)
    came = came.reshape(count, sector, sector)

    turned, right_parts, psi_parts = pl.pallas_call(
        turn_kernel,
        out_shape=(
            jax.ShapeDtypeStruct((count, sector, terms * 2 * sector), BF16),
            jax.ShapeDtypeStruct((rights, sector, 2 * sector), BF16),
            jax.ShapeDtypeStruct((owned, sector, 2 * sector), BF16),
        ),
        in_specs=[HBM] + [SMEM] * 2 + [VMEM] * 2,
        out_specs=(VMEM,) * 3,
        scratch_shapes=[pltpu.VMEM((owned, 2 * sector, 2 * sector), BF16)],
        compiler_params=roomy(56),
        cost_estimate=LIGHT,
        name="turn",
    )(sent, *by_slot[2:], psi_rows, right_rows)

    near, near_sums = pl.pallas_call(
        local_kernel,
        out_shape=(mats, tile),
        in_specs=[SMEM] * 3 + [VMEM] * 4,
        out_specs=(VMEM,) * 2,
        scratch_shapes=[pltpu.VMEM((loc_block.shape[0], sector, 2 * sector), BF16)],
        compiler_params=roomy(56),
        cost_estimate=LIGHT,
        name="local_terms",
    )(loc_block, loc_left, loc_right, psi_rows, left_rows, psi_parts, right_parts)

    adjoint, left_parts = pl.pallas_call(
        lambda *refs: adjoint_kernel(slots, terms, *refs),
        out_shape=(blocks, jax.ShapeDtypeStruct((count, terms * sector, 2 * sector), BF16)),
        in_specs=[SMEM] * 2 + [VMEM] * 2,
        out_specs=(VMEM,) * 2,
        compiler_params=roomy(48),
        cost_estimate=LIGHT,
        name="adjoint_blocks",
    )(me, meta, left_rows, turned)

    sums = pl.pallas_call(
        overlap_kernel,
        out_shape=jax.ShapeDtypeStruct((peers, SUB, sector), F32),
        in_specs=[VMEM] * 3,
        out_specs=VMEM,
        compiler_params=roomy(24),
        name="overlap",
    )(came, adjoint, near_sums)
    sums = lax.all_to_all(sums, "renv", split_axis=0, concat_axis=0, tiled=True)

    hpsi_rows, hpsi = pl.pallas_call(
        remote_kernel,
        out_shape=(rows, rows),
        in_specs=[SMEM] * 2 + [VMEM] * 4,
        out_specs=(VMEM, HBM),
        scratch_shapes=[
            pltpu.VMEM(mats.shape, F32),
            pltpu.VMEM((count, terms * sector, 2 * sector), BF16),
            pltpu.SemaphoreType.DMA,
        ],
        compiler_params=roomy(48),
        cost_estimate=pl.CostEstimate(flops=4 * 10**9, bytes_accessed=6 * MIB, transcendentals=0),
        name="remote_terms",
    )(*by_slot[2:], came, near, left_parts, right_parts)

    residual_rows = pl.pallas_call(
        residual_kernel,
        out_shape=rows,
        in_specs=[VMEM] * 3,
        out_specs=VMEM,
        compiler_params=roomy(16),
        name="residual",
    )(sums, hpsi_rows, psi_rows)
    return (from_rows(hpsi, owned), from_rows(residual_rows, owned))


def solution(mesh):
    placed = (
        P(("groups", "renv"), None),
        P("groups", None),
        P(("groups", "renv"), None),
        P(("groups", "renv"), None),
        P(("groups", "renv"), None, None),
        P(("groups", "renv"), None, None),
        P(("groups", "renv"), None, None),
        P(("groups", "renv"), None, None),
        P(("groups", "renv")),
        P(("groups", "renv")),
        P(("groups", "renv")),
    )
    return jax.shard_map(
        shards,
        mesh=mesh,
        in_specs=placed,
        out_specs=(P(("groups", "renv"), None), P(("groups", "renv"), None)),
        check_vma=False,
    )
```

```python
import math

import jax
import jax.numpy as jnp
from jax import lax
from jax.experimental import pallas as pl
from jax.experimental.pallas import tpu as pltpu
from jax.sharding import PartitionSpec as P

F32 = jnp.float32
BF16 = jnp.bfloat16
SUB = 8
VMEM = pl.BlockSpec(memory_space=pltpu.VMEM)
SMEM = pl.BlockSpec(memory_space=pltpu.SMEM)
HBM = pl.BlockSpec(memory_space=pltpu.HBM)
MIB = 2**20
LIGHT = pl.CostEstimate(flops=10**6, bytes_accessed=2**16, transcendentals=0)


def as_rows(blocks, sector):
    count = blocks.shape[0]
    split = blocks.reshape(count // SUB, SUB, sector, sector)
    return split.transpose(0, 2, 1, 3).reshape(count * sector, sector)


def from_rows(rows, count):
    sector = rows.shape[1]
    split = rows.reshape(count // SUB, sector, SUB, sector)
    return split.transpose(0, 2, 1, 3).reshape(count, sector * sector)


def pick(ref, block):
    sector = ref.shape[1]
    start = (block // SUB) * (SUB * sector) + block % SUB
    return ref[pl.ds(start, sector, stride=SUB), :]


def halves(mat):
    high = mat.astype(BF16)
    low = (mat - high.astype(F32)).astype(BF16)
    return jnp.concatenate([high, low], axis=1)


def doubled(mat):
    both = halves(mat)
    return jnp.concatenate([both, both], axis=0)


def product(left, right):
    sector = right.shape[1] // 2
    wide = jnp.dot(left, right, preferred_element_type=F32)
    return wide[:, :sector] + wide[:, sector:]


def stacked(mat):
    high = mat.astype(BF16)
    low = (mat - high.astype(F32)).astype(BF16)
    rows = [jnp.concatenate([part, part], axis=1) for part in (high, low)]
    return jnp.concatenate(rows, axis=0)


def product_t(left, right):
    sector = right.shape[0] // 2
    wide = lax.dot_general(left, right, (((1,), (1,)), ((), ())), preferred_element_type=F32)
    return wide[:, :sector] + wide[:, sector:]


def twice(part):
    return jnp.concatenate([part, part], axis=0)


def roomy(mib):
    return pltpu.CompilerParams(vmem_limit_bytes=mib * MIB)


def gather_kernel(block_ref, left_ref, live_ref, psi_rows, out_hbm, stage, sems):
    slots, terms, _ = left_ref.shape
    sector = psi_rows.shape[1]
    lane = lax.broadcasted_iota(jnp.int32, (SUB, sector), 1)
    puts = []
    for i in range(stage.shape[0]):
        stage[i, :sector] = pick(psi_rows, block_ref[i])
        values = jnp.zeros(lane.shape, jnp.int32)
        for g in range(terms):
            values = jnp.where(lane == g, left_ref[i % slots, g, i // slots], values)
            values = jnp.where(lane == terms + g, live_ref[i % slots, g, i // slots], values)
        stage[i, sector:] = values.astype(F32)
        put = pltpu.make_async_copy(stage.at[i], out_hbm.at[i], sems.at[i])
        put.start()
        puts.append(put)
    for put in puts:
        put.wait()


def turn_kernel(sent_hbm, rindex_ref, out_index_ref, psi_rows, right_rows, turned_ref, rights_ref, psis_ref, stacks_ref):
    slots, terms, _ = rindex_ref.shape
    sector = psi_rows.shape[1]

    def split_right(i, carry):
        mat = pick(right_rows, i)
        rights_ref[i] = halves(mat)
        stacks_ref[i] = stacked(mat)
        return carry

    lax.fori_loop(0, rights_ref.shape[0], split_right, 0, unroll=4)

    def split_psi(i, carry):
        psis_ref[i] = halves(pick(psi_rows, i))
        return carry

    lax.fori_loop(0, psis_ref.shape[0], split_psi, 0, unroll=4)

    def turn(i, carry):
        for g in range(terms):
            right = stacks_ref[rindex_ref[i % slots, g, i // slots]]
            psi = psis_ref[out_index_ref[i % slots, g, i // slots]]
            turned_ref[i, g * sector : (g + 1) * sector] = product_t(psi, right)
        return carry

    lax.fori_loop(0, turned_ref.shape[0], turn, 0, unroll=4)


def local_kernel(block_ref, left_ref, right_ref, psi_rows, left_rows, psis_ref, rights_ref, near_ref, sums_ref, lefts_ref, moved_ref):
    near_ref[...] = jnp.zeros_like(near_ref)

    def split_left(i, carry):
        lefts_ref[i] = halves(pick(left_rows, i))
        return carry

    lax.fori_loop(0, lefts_ref.shape[0], split_left, 0, unroll=8)

    def left_step(k, carry):
        moved_ref[k] = halves(product(lefts_ref[left_ref[k]], twice(psis_ref[block_ref[k]])))
        return carry

    lax.fori_loop(0, block_ref.shape[0], left_step, 0, unroll=8)

    def right_step(k, carry):
        near_ref[block_ref[k]] += product(moved_ref[k], twice(rights_ref[right_ref[k]]))
        return carry

    lax.fori_loop(0, block_ref.shape[0], right_step, 0, unroll=8)
    corr = jnp.zeros((1, sums_ref.shape[1]), F32)
    norm = jnp.zeros((1, sums_ref.shape[1]), F32)
    for b in range(near_ref.shape[0]):
        mat = pick(psi_rows, b)
        corr += jnp.sum(mat * near_ref[b], axis=0, keepdims=True)
        norm += jnp.sum(mat * mat, axis=0, keepdims=True)
    row = lax.broadcasted_iota(jnp.int32, sums_ref.shape, 0)
    sums_ref[...] = jnp.where(row == 0, corr, jnp.where(row == 1, norm, 0.0))


def arrive_kernel(
    terms, came_ref, turned_hbm, lefts_hbm, before_ref, moved_ref, sums_ref, marks, lefts_ref, turned_ref, mark_sem, left_sems, turned_sems
):
    count, height, sector = came_ref.shape
    get_marks = pltpu.make_async_copy(came_ref.at[:, pl.ds(sector, height - sector)], marks, mark_sem)
    get_marks.start()

    def fetch_turned(i):
        return pltpu.make_async_copy(turned_hbm.at[i], turned_ref.at[i], turned_sems.at[i])

    def fetch_left(i, g):
        source = lefts_hbm.at[marks[i, 0, g].astype(jnp.int32)]
        return pltpu.make_async_copy(source, lefts_ref.at[i, pl.ds(g * sector, sector)], left_sems.at[i, g])

    get_marks.wait()

    def start(i, carry):
        for g in range(terms):
            fetch_left(i, g).start()
        fetch_turned(i).start()
        return carry

    lax.fori_loop(0, count, start, 0, unroll=4)

    def block(i, total):
        for g in range(terms):
            fetch_left(i, g).wait()
        fetch_turned(i).wait()
        moved = product(lefts_ref[i], doubled(came_ref[i, :sector]))
        for g in range(terms):
            part = slice(g * sector, (g + 1) * sector)
            one = moved[part] * marks[i, 0, terms + g]
            moved_ref[i, part] = halves(one)
            total += jnp.sum((one * turned_ref[i, part]).reshape(-1, SUB, sector), axis=0)
        return total

    total = lax.fori_loop(0, count, block, jnp.zeros((SUB, sector), F32), unroll=4)
    corr = jnp.sum(total, axis=0, keepdims=True)
    row = lax.broadcasted_iota(jnp.int32, total.shape, 0)
    mine = before_ref[0] + jnp.where(row == 0, corr, 0.0)
    for i in range(sums_ref.shape[0]):
        sums_ref[i] = mine


def remote_kernel(sums_hbm, rindex_ref, out_index_ref, moved_ref, near_ref, rights_ref, hpsi_rows, hpsi_hbm, acc, sem):
    slots, terms, _ = rindex_ref.shape
    sector = rights_ref.shape[1]
    acc[...] = near_ref[...]

    def right_step(i, carry):
        for g in range(terms):
            right = rights_ref[rindex_ref[i % slots, g, i // slots]]
            acc[out_index_ref[i % slots, g, i // slots]] += product(moved_ref[i, g * sector : (g + 1) * sector], twice(right))
        return carry

    lax.fori_loop(0, moved_ref.shape[0], right_step, 0, unroll=4)
    for b in range(acc.shape[0]):
        start = (b // SUB) * (SUB * sector) + b % SUB
        hpsi_rows[pl.ds(start, sector, stride=SUB), :] = acc[b]
    put = pltpu.make_async_copy(hpsi_rows, hpsi_hbm, sem)
    put.start()
    put.wait()


def residual_kernel(sums_ref, hpsi_rows, psi_rows, out_ref):
    total = jnp.sum(sums_ref[...], axis=0)
    whole = jnp.sum(total, axis=1, keepdims=True)
    theta = whole[0:1] / (whole[1:2] + 1e-06)
    out_ref[...] = hpsi_rows[...] - theta * psi_rows[...]


def shards(
    psi,
    left_env,
    right_env,
    send_block,
    send_left,
    send_live,
    recv_right,
    recv_out,
    loc_block,
    loc_left,
    loc_right,
):
    peers = lax.axis_size("renv")
    owned = psi.shape[0]
    sector = math.isqrt(psi.shape[1])
    slots = send_block.shape[1]
    terms = send_left.shape[2]
    count = peers * slots
    lefts = left_env.shape[0]
    rights = right_env.shape[0]
    height = sector + SUB
    psi_rows = as_rows(psi, sector)
    left_rows = as_rows(left_env, sector)
    right_rows = as_rows(right_env, sector)
    by_slot = [index.transpose(1, 2, 0) for index in (send_left, send_live, recv_right, recv_out)]
    blocks = jax.ShapeDtypeStruct((count, height, sector), F32)
    rows = jax.ShapeDtypeStruct((owned * sector, sector), F32)
    mats = jax.ShapeDtypeStruct((owned, sector, sector), F32)
    tile = jax.ShapeDtypeStruct((SUB, sector), F32)

    sent = pl.pallas_call(
        gather_kernel,
        out_shape=blocks,
        in_specs=[SMEM] * 3 + [VMEM],
        out_specs=HBM,
        scratch_shapes=[pltpu.VMEM(blocks.shape, F32), pltpu.SemaphoreType.DMA((count,))],
        compiler_params=roomy(56),
        name="gather_blocks",
    )(send_block.reshape(-1), *by_slot[:2], psi_rows)
    came = lax.all_to_all(sent.reshape(peers, slots, height, sector), "renv", split_axis=0, concat_axis=0, tiled=True)
    came = came.reshape(count, height, sector)

    turned, right_parts, psi_parts = pl.pallas_call(
        turn_kernel,
        out_shape=(
            jax.ShapeDtypeStruct((count, terms * sector, sector), F32),
            jax.ShapeDtypeStruct((rights, sector, 2 * sector), BF16),
            jax.ShapeDtypeStruct((owned, sector, 2 * sector), BF16),
        ),
        in_specs=[HBM] + [SMEM] * 2 + [VMEM] * 2,
        out_specs=(VMEM,) * 3,
        scratch_shapes=[pltpu.VMEM((rights, 2 * sector, 2 * sector), BF16)],
        compiler_params=roomy(56),
        cost_estimate=LIGHT,
        name="turn",
    )(sent, *by_slot[2:], psi_rows, right_rows)

    near, before, left_parts = pl.pallas_call(
        local_kernel,
        out_shape=(mats, tile, jax.ShapeDtypeStruct((lefts, sector, 2 * sector), BF16)),
        in_specs=[SMEM] * 3 + [VMEM] * 4,
        out_specs=(VMEM,) * 3,
        scratch_shapes=[pltpu.VMEM((loc_block.shape[0], sector, 2 * sector), BF16)],
        compiler_params=roomy(56),
        cost_estimate=LIGHT,
        name="local_terms",
    )(loc_block, loc_left, loc_right, psi_rows, left_rows, psi_parts, right_parts)

    chunk = math.gcd(count, 16)
    sums = before[None]
    moved = []
    for first in range(0, count, chunk):
        part = slice(first, first + chunk) if count > chunk else slice(None)
        kept, sums = pl.pallas_call(
            lambda *refs: arrive_kernel(terms, *refs),
            out_shape=(
                jax.ShapeDtypeStruct((chunk, terms * sector, 2 * sector), BF16),
                jax.ShapeDtypeStruct((peers, SUB, sector), F32),
            ),
            in_specs=[VMEM, HBM, HBM, VMEM],
            out_specs=(VMEM,) * 2,
            scratch_shapes=[
                pltpu.SMEM((chunk, SUB, sector), F32),
                pltpu.VMEM((chunk, terms * sector, 2 * sector), BF16),
                pltpu.VMEM((chunk, terms * sector, sector), F32),
                pltpu.SemaphoreType.DMA,
                pltpu.SemaphoreType.DMA((chunk, terms)),
                pltpu.SemaphoreType.DMA((chunk,)),
            ],
            compiler_params=roomy(48),
            name="arrive",
        )(came[part], turned[part], left_parts, sums)
        moved.append(kept)
    moved = moved[0] if len(moved) == 1 else jnp.concatenate(moved, axis=0)
    totals = lax.all_to_all(sums, "renv", split_axis=0, concat_axis=0, tiled=True)

    hpsi_rows, hpsi = pl.pallas_call(
        remote_kernel,
        out_shape=(rows, rows),
        in_specs=[HBM] + [SMEM] * 2 + [VMEM] * 3,
        out_specs=(VMEM, HBM),
        scratch_shapes=[pltpu.VMEM(mats.shape, F32), pltpu.SemaphoreType.DMA],
        compiler_params=roomy(48),
        cost_estimate=pl.CostEstimate(flops=4 * 10**9, bytes_accessed=6 * MIB, transcendentals=0),
        name="remote_terms",
    )(sums, *by_slot[2:], moved, near, right_parts)

    residual_rows = pl.pallas_call(
        residual_kernel,
        out_shape=rows,
        in_specs=[VMEM] * 3,
        out_specs=VMEM,
        compiler_params=roomy(16),
        name="residual",
    )(totals, hpsi_rows, psi_rows)
    return (from_rows(hpsi, owned), from_rows(residual_rows, owned))


def solution(mesh):
    placed = (
        P(("groups", "renv"), None),
        P("groups", None),
        P(("groups", "renv"), None),
        P(("groups", "renv"), None),
        P(("groups", "renv"), None, None),
        P(("groups", "renv"), None, None),
        P(("groups", "renv"), None, None),
        P(("groups", "renv"), None, None),
        P(("groups", "renv")),
        P(("groups", "renv")),
        P(("groups", "renv")),
    )
    return jax.shard_map(
        shards,
        mesh=mesh,
        in_specs=placed,
        out_specs=(P(("groups", "renv"), None), P(("groups", "renv"), None)),
        check_vma=False,
    )
```

```python
import math

import jax
import jax.numpy as jnp
from jax import lax
from jax.experimental import pallas as pl
from jax.experimental.pallas import tpu as pltpu
from jax.sharding import PartitionSpec as P

F32 = jnp.float32
BF16 = jnp.bfloat16
SUB = 8
VMEM = pl.BlockSpec(memory_space=pltpu.VMEM)
SMEM = pl.BlockSpec(memory_space=pltpu.SMEM)
HBM = pl.BlockSpec(memory_space=pltpu.HBM)
MIB = 2**20
LIGHT = pl.CostEstimate(flops=10**6, bytes_accessed=2**16, transcendentals=0)


def as_rows(blocks, sector):
    count = blocks.shape[0]
    split = blocks.reshape(count // SUB, SUB, sector, sector)
    return split.transpose(0, 2, 1, 3).reshape(count * sector, sector)


def from_rows(rows, count):
    sector = rows.shape[1]
    split = rows.reshape(count // SUB, sector, SUB, sector)
    return split.transpose(0, 2, 1, 3).reshape(count, sector * sector)


def pick(ref, block):
    sector = ref.shape[1]
    start = (block // SUB) * (SUB * sector) + block % SUB
    return ref[pl.ds(start, sector, stride=SUB), :]


def halves(mat):
    high = mat.astype(BF16)
    low = (mat - high.astype(F32)).astype(BF16)
    return jnp.concatenate([high, low], axis=1)


def doubled(mat):
    both = halves(mat)
    return jnp.concatenate([both, both], axis=0)


def product(left, right):
    sector = right.shape[1] // 2
    wide = jnp.dot(left, right, preferred_element_type=F32)
    return wide[:, :sector] + wide[:, sector:]


def stacked(mat):
    high = mat.astype(BF16)
    low = (mat - high.astype(F32)).astype(BF16)
    rows = [jnp.concatenate([part, part], axis=1) for part in (high, low)]
    return jnp.concatenate(rows, axis=0)


def product_t(left, right):
    sector = right.shape[0] // 2
    wide = lax.dot_general(left, right, (((1,), (1,)), ((), ())), preferred_element_type=F32)
    return wide[:, :sector] + wide[:, sector:]


def twice(part):
    return jnp.concatenate([part, part], axis=0)


def roomy(mib):
    return pltpu.CompilerParams(vmem_limit_bytes=mib * MIB)


def gather_kernel(block_ref, left_ref, live_ref, psi_rows, out_hbm, stage, sems):
    slots, terms, _ = left_ref.shape
    sector = psi_rows.shape[1]
    lane = lax.broadcasted_iota(jnp.int32, (SUB, sector), 1)
    puts = []
    for i in range(stage.shape[0]):
        stage[i, :sector] = pick(psi_rows, block_ref[i])
        values = jnp.zeros(lane.shape, jnp.int32)
        for g in range(terms):
            values = jnp.where(lane == g, left_ref[i % slots, g, i // slots], values)
            values = jnp.where(lane == terms + g, live_ref[i % slots, g, i // slots], values)
        stage[i, sector:] = values.astype(F32)
        put = pltpu.make_async_copy(stage.at[i], out_hbm.at[i], sems.at[i])
        put.start()
        puts.append(put)
    for put in puts:
        put.wait()


def prepare_kernel(
    sent_hbm,
    rindex_ref,
    out_index_ref,
    block_ref,
    left_ref,
    right_ref,
    psi_rows,
    right_rows,
    left_rows,
    turned_ref,
    parts_ref,
    near_ref,
    psis_ref,
    stacks_ref,
    moved_ref,
):
    slots, terms, _ = rindex_ref.shape
    sector = psi_rows.shape[1]

    rights = right_rows.shape[0] // sector
    lefts = left_rows.shape[0] // sector

    def split_right(i, carry):
        mat = pick(right_rows, i)
        parts_ref[lefts + i] = halves(mat)
        stacks_ref[i] = stacked(mat)
        return carry

    lax.fori_loop(0, rights, split_right, 0, unroll=4)

    def split_psi(i, carry):
        psis_ref[i] = halves(pick(psi_rows, i))
        return carry

    lax.fori_loop(0, psis_ref.shape[0], split_psi, 0, unroll=4)

    def turn(i, carry):
        for g in range(terms):
            right = stacks_ref[rindex_ref[i % slots, g, i // slots]]
            psi = psis_ref[out_index_ref[i % slots, g, i // slots]]
            turned_ref[i, g * sector : (g + 1) * sector] = product_t(psi, right)
        turned_ref[i, terms * sector :] = jnp.zeros((SUB, sector), F32)
        return carry

    slabs = near_ref.shape[0] // terms
    senders = turned_ref.shape[0] - slabs
    lax.fori_loop(0, senders, turn, 0, unroll=4)

    def split_left(i, carry):
        parts_ref[i] = halves(pick(left_rows, i))
        return carry

    lax.fori_loop(0, lefts, split_left, 0, unroll=8)

    def left_step(k, carry):
        moved_ref[k] = halves(product(parts_ref[left_ref[k]], twice(psis_ref[block_ref[k]])))
        return carry

    lax.fori_loop(0, block_ref.shape[0], left_step, 0, unroll=8)
    near_ref[...] = jnp.zeros_like(near_ref)

    def right_step(k, carry):
        near_ref[block_ref[k]] += product(moved_ref[k], twice(parts_ref[lefts + right_ref[k]]))
        return carry

    lax.fori_loop(0, block_ref.shape[0], right_step, 0, unroll=8)
    corr = jnp.zeros((1, sector), F32)
    norm = jnp.zeros((1, sector), F32)
    for b in range(near_ref.shape[0]):
        mat = pick(psi_rows, b)
        turned_ref[senders + b // terms, (b % terms) * sector : (b % terms + 1) * sector] = near_ref[b]
        corr += jnp.sum(mat * near_ref[b], axis=0, keepdims=True)
        norm += jnp.sum(mat * mat, axis=0, keepdims=True)
    row = lax.broadcasted_iota(jnp.int32, (SUB, sector), 0)
    turned_ref[0, terms * sector :] = jnp.where(row == 0, corr, jnp.where(row == 1, norm, 0.0))


def arrive_kernel(terms, came_ref, turned_hbm, parts_hbm, moved_ref, sums_ref, marks, turned_ref, lefts_ref, sems):
    count, height, sector = came_ref.shape
    get_marks = pltpu.make_async_copy(came_ref.at[:, pl.ds(sector, height - sector)], marks, sems.at[0])
    get_lefts = pltpu.make_async_copy(parts_hbm.at[pl.ds(0, lefts_ref.shape[0])], lefts_ref, sems.at[1])
    get_turned = pltpu.make_async_copy(turned_hbm.at[pl.ds(0, count)], turned_ref, sems.at[2])
    get_marks.start()
    get_lefts.start()
    get_turned.start()
    get_marks.wait()
    get_lefts.wait()
    get_turned.wait()

    def block(i, total):
        stack = [lefts_ref[marks[i, 0, g].astype(jnp.int32)] for g in range(terms)]
        moved = product(jnp.concatenate(stack, axis=0), doubled(came_ref[i, :sector]))
        for g in range(terms):
            part = slice(g * sector, (g + 1) * sector)
            one = moved[part] * marks[i, 0, terms + g]
            moved_ref[i, part] = halves(one)
            total += jnp.sum((one * turned_ref[i, part]).reshape(-1, SUB, sector), axis=0)
        return total

    total = lax.fori_loop(0, count, block, jnp.zeros((SUB, sector), F32), unroll=4)
    corr = jnp.sum(total, axis=0, keepdims=True)
    row = lax.broadcasted_iota(jnp.int32, total.shape, 0)
    mine = turned_ref[0, terms * sector :] + jnp.where(row == 0, corr, 0.0)
    for i in range(sums_ref.shape[0]):
        sums_ref[i] = mine


def remote_kernel(rindex_ref, out_index_ref, moved_ref, turned_hbm, parts_hbm, hpsi_rows, hpsi_hbm, acc, rights_ref, sems):
    slots, terms, _ = rindex_ref.shape
    senders, height, _ = moved_ref.shape
    sector = height // terms
    rights = rights_ref.shape[0]
    rights_hbm = parts_hbm.at[pl.ds(parts_hbm.shape[0] - rights, rights)]
    get_rights = pltpu.make_async_copy(rights_hbm, rights_ref, sems.at[0])
    get_rights.start()
    slabs = []
    for k in range(acc.shape[0] // height):
        near = turned_hbm.at[senders + k, pl.ds(0, height)]
        slabs.append(pltpu.make_async_copy(near, acc.at[pl.ds(k * height, height)], sems.at[1 + k]))
        slabs[k].start()
    get_rights.wait()
    for copy in slabs:
        copy.wait()

    def right_step(i, carry):
        for g in range(terms):
            right = rights_ref[rindex_ref[i % slots, g, i // slots]]
            spot = pl.multiple_of(out_index_ref[i % slots, g, i // slots] * sector, sector)
            acc[pl.ds(spot, sector)] += product(moved_ref[i, g * sector : (g + 1) * sector], twice(right))
        return carry

    lax.fori_loop(0, senders, right_step, 0, unroll=4)
    for b in range(acc.shape[0] // sector):
        start = (b // SUB) * (SUB * sector) + b % SUB
        hpsi_rows[pl.ds(start, sector, stride=SUB), :] = acc[b * sector : (b + 1) * sector]
    put = pltpu.make_async_copy(hpsi_rows, hpsi_hbm, sems.at[0])
    put.start()
    put.wait()


def residual_kernel(sums_ref, hpsi_rows, psi_rows, out_ref):
    total = jnp.sum(sums_ref[...], axis=0)
    whole = jnp.sum(total, axis=1, keepdims=True)
    theta = whole[0:1] / (whole[1:2] + 1e-06)
    out_ref[...] = hpsi_rows[...] - theta * psi_rows[...]


def shards(
    psi,
    left_env,
    right_env,
    send_block,
    send_left,
    send_live,
    recv_right,
    recv_out,
    loc_block,
    loc_left,
    loc_right,
):
    peers = lax.axis_size("renv")
    owned = psi.shape[0]
    sector = math.isqrt(psi.shape[1])
    slots = send_block.shape[1]
    terms = send_left.shape[2]
    count = peers * slots
    lefts = left_env.shape[0]
    rights = right_env.shape[0]
    height = sector + SUB
    psi_rows = as_rows(psi, sector)
    left_rows = as_rows(left_env, sector)
    right_rows = as_rows(right_env, sector)
    by_slot = [index.transpose(1, 2, 0) for index in (send_left, send_live, recv_right, recv_out)]
    blocks = jax.ShapeDtypeStruct((count, height, sector), F32)
    rows = jax.ShapeDtypeStruct((owned * sector, sector), F32)

    sent = pl.pallas_call(
        gather_kernel,
        out_shape=blocks,
        in_specs=[SMEM] * 3 + [VMEM],
        out_specs=HBM,
        scratch_shapes=[pltpu.VMEM(blocks.shape, F32), pltpu.SemaphoreType.DMA((count,))],
        compiler_params=roomy(56),
        name="gather_blocks",
    )(send_block.reshape(-1), *by_slot[:2], psi_rows)
    came = lax.all_to_all(sent.reshape(peers, slots, height, sector), "renv", split_axis=0, concat_axis=0, tiled=True)
    came = came.reshape(count, height, sector)

    slabs = owned // terms
    turned, parts = pl.pallas_call(
        prepare_kernel,
        out_shape=(
            jax.ShapeDtypeStruct((count + slabs, terms * sector + SUB, sector), F32),
            jax.ShapeDtypeStruct((lefts + rights, sector, 2 * sector), BF16),
        ),
        in_specs=[HBM] + [SMEM] * 5 + [VMEM] * 3,
        out_specs=(VMEM,) * 2,
        scratch_shapes=[
            pltpu.VMEM((owned, sector, sector), F32),
            pltpu.VMEM((owned, sector, 2 * sector), BF16),
            pltpu.VMEM((rights, 2 * sector, 2 * sector), BF16),
            pltpu.VMEM((loc_block.shape[0], sector, 2 * sector), BF16),
        ],
        compiler_params=roomy(56),
        cost_estimate=LIGHT,
        name="prepare",
    )(sent, *by_slot[2:], loc_block, loc_left, loc_right, psi_rows, right_rows, left_rows)

    chunk = math.gcd(count, 16)
    moved = []
    sums = 0.0
    for first in range(0, count, chunk):
        part = slice(first, first + chunk) if count > chunk else slice(None)
        kept, share = pl.pallas_call(
            lambda *refs: arrive_kernel(terms, *refs),
            out_shape=(
                jax.ShapeDtypeStruct((chunk, terms * sector, 2 * sector), BF16),
                jax.ShapeDtypeStruct((peers, SUB, sector), F32),
            ),
            in_specs=[VMEM] + [HBM] * 2,
            out_specs=(VMEM,) * 2,
            scratch_shapes=[
                pltpu.SMEM((chunk, SUB, sector), F32),
                pltpu.VMEM((chunk, terms * sector + SUB, sector), F32),
                pltpu.VMEM((lefts, sector, 2 * sector), BF16),
                pltpu.SemaphoreType.DMA((3,)),
            ],
            compiler_params=roomy(50),
            name="arrive",
        )(came[part], turned if count == chunk else turned[part], parts)
        moved.append(kept)
        sums = share if count == chunk else sums + share
    moved = moved[0] if len(moved) == 1 else jnp.concatenate(moved, axis=0)
    totals = lax.all_to_all(sums, "renv", split_axis=0, concat_axis=0, tiled=True)

    hpsi_rows, hpsi = pl.pallas_call(
        remote_kernel,
        out_shape=(rows, rows),
        in_specs=[SMEM] * 2 + [VMEM] + [HBM] * 2,
        out_specs=(VMEM, HBM),
        scratch_shapes=[
            pltpu.VMEM(rows.shape, F32),
            pltpu.VMEM((rights, sector, 2 * sector), BF16),
            pltpu.SemaphoreType.DMA((1 + slabs,)),
        ],
        compiler_params=roomy(50),
        cost_estimate=pl.CostEstimate(flops=4 * 10**9, bytes_accessed=6 * MIB, transcendentals=0),
        name="remote_terms",
    )(*by_slot[2:], moved, turned, parts)

    residual_rows = pl.pallas_call(
        residual_kernel,
        out_shape=rows,
        in_specs=[VMEM] * 3,
        out_specs=VMEM,
        compiler_params=roomy(16),
        name="residual",
    )(totals, hpsi_rows, psi_rows)
    return (from_rows(hpsi, owned), from_rows(residual_rows, owned))


def solution(mesh):
    placed = (
        P(("groups", "renv"), None),
        P("groups", None),
        P(("groups", "renv"), None),
        P(("groups", "renv"), None),
        P(("groups", "renv"), None, None),
        P(("groups", "renv"), None, None),
        P(("groups", "renv"), None, None),
        P(("groups", "renv"), None, None),
        P(("groups", "renv")),
        P(("groups", "renv")),
        P(("groups", "renv")),
    )
    return jax.shard_map(
        shards,
        mesh=mesh,
        in_specs=placed,
        out_specs=(P(("groups", "renv"), None), P(("groups", "renv"), None)),
        check_vma=False,
    )
```

```python
import math

import jax
import jax.numpy as jnp
from jax import lax
from jax.experimental import pallas as pl
from jax.experimental.pallas import tpu as pltpu
from jax.sharding import PartitionSpec as P

F32 = jnp.float32
BF16 = jnp.bfloat16
SUB = 8
VMEM = pl.BlockSpec(memory_space=pltpu.VMEM)
SMEM = pl.BlockSpec(memory_space=pltpu.SMEM)
HBM = pl.BlockSpec(memory_space=pltpu.HBM)
MIB = 2**20
LIGHT = pl.CostEstimate(flops=10**6, bytes_accessed=2**16, transcendentals=0)


def as_rows(blocks, sector):
    count = blocks.shape[0]
    split = blocks.reshape(count // SUB, SUB, sector, sector)
    return split.transpose(0, 2, 1, 3).reshape(count * sector, sector)


def from_rows(rows, count):
    sector = rows.shape[1]
    split = rows.reshape(count // SUB, sector, SUB, sector)
    return split.transpose(0, 2, 1, 3).reshape(count, sector * sector)


def pick(ref, block):
    sector = ref.shape[1]
    start = (block // SUB) * (SUB * sector) + block % SUB
    return ref[pl.ds(start, sector, stride=SUB), :]


def halves(mat):
    high = mat.astype(BF16)
    low = (mat - high.astype(F32)).astype(BF16)
    return jnp.concatenate([high, low], axis=1)


def doubled(mat):
    both = halves(mat)
    return jnp.concatenate([both, both], axis=0)


def product(left, right):
    sector = right.shape[1] // 2
    wide = jnp.dot(left, right, preferred_element_type=F32)
    return wide[:, :sector] + wide[:, sector:]


def stacked(mat):
    high = mat.astype(BF16)
    low = (mat - high.astype(F32)).astype(BF16)
    rows = [jnp.concatenate([part, part], axis=1) for part in (high, low)]
    return jnp.concatenate(rows, axis=0)


def product_t(left, right):
    sector = right.shape[0] // 2
    wide = lax.dot_general(left, right, (((1,), (1,)), ((), ())), preferred_element_type=F32)
    return wide[:, :sector] + wide[:, sector:]


def twice(part):
    return jnp.concatenate([part, part], axis=0)


def roomy(mib):
    return pltpu.CompilerParams(vmem_limit_bytes=mib * MIB)


def gather_kernel(block_ref, left_ref, live_ref, psi_rows, out_hbm, stage, sems):
    slots, terms, _ = left_ref.shape
    sector = psi_rows.shape[1]
    lane = lax.broadcasted_iota(jnp.int32, (SUB, sector), 1)
    puts = []
    for i in range(stage.shape[0]):
        stage[i, :sector] = pick(psi_rows, block_ref[i])
        values = jnp.zeros(lane.shape, jnp.int32)
        for g in range(terms):
            values = jnp.where(lane == g, left_ref[i % slots, g, i // slots], values)
            values = jnp.where(lane == terms + g, live_ref[i % slots, g, i // slots], values)
        stage[i, sector:] = values.astype(F32)
        put = pltpu.make_async_copy(stage.at[i], out_hbm.at[i], sems.at[i])
        put.start()
        puts.append(put)
    for put in puts:
        put.wait()


def prepare_kernel(
    sent_hbm,
    rindex_ref,
    out_index_ref,
    block_ref,
    left_ref,
    right_ref,
    psi_rows,
    right_rows,
    left_rows,
    turned_ref,
    parts_ref,
    near_ref,
    psis_ref,
    stacks_ref,
    moved_ref,
):
    slots, terms, _ = rindex_ref.shape
    sector = psi_rows.shape[1]

    rights = right_rows.shape[0] // sector
    lefts = left_rows.shape[0] // sector

    def split_right(i, carry):
        mat = pick(right_rows, i)
        parts_ref[lefts + i] = halves(mat)
        stacks_ref[i] = stacked(mat)
        return carry

    lax.fori_loop(0, rights, split_right, 0, unroll=4)

    def split_psi(i, carry):
        psis_ref[i] = halves(pick(psi_rows, i))
        return carry

    lax.fori_loop(0, psis_ref.shape[0], split_psi, 0, unroll=4)

    def turn(i, carry):
        for g in range(terms):
            right = stacks_ref[rindex_ref[i % slots, g, i // slots]]
            psi = psis_ref[out_index_ref[i % slots, g, i // slots]]
            turned_ref[i, g * sector : (g + 1) * sector] = product_t(psi, right)
        turned_ref[i, terms * sector :] = jnp.zeros((SUB, sector), F32)
        return carry

    slabs = near_ref.shape[0] // terms
    senders = turned_ref.shape[0] - slabs
    lax.fori_loop(0, senders, turn, 0, unroll=4)

    def split_left(i, carry):
        parts_ref[i] = halves(pick(left_rows, i))
        return carry

    lax.fori_loop(0, lefts, split_left, 0, unroll=8)

    def left_step(k, carry):
        moved_ref[k] = halves(product(parts_ref[left_ref[k]], twice(psis_ref[block_ref[k]])))
        return carry

    lax.fori_loop(0, block_ref.shape[0], left_step, 0, unroll=8)
    near_ref[...] = jnp.zeros_like(near_ref)

    def right_step(k, carry):
        near_ref[block_ref[k]] += product(moved_ref[k], twice(parts_ref[lefts + right_ref[k]]))
        return carry

    lax.fori_loop(0, block_ref.shape[0], right_step, 0, unroll=8)
    corr = jnp.zeros((1, sector), F32)
    norm = jnp.zeros((1, sector), F32)
    for b in range(near_ref.shape[0]):
        mat = pick(psi_rows, b)
        turned_ref[senders + b // terms, (b % terms) * sector : (b % terms + 1) * sector] = near_ref[b]
        corr += jnp.sum(mat * near_ref[b], axis=0, keepdims=True)
        norm += jnp.sum(mat * mat, axis=0, keepdims=True)
    row = lax.broadcasted_iota(jnp.int32, (SUB, sector), 0)
    turned_ref[0, terms * sector :] = jnp.where(row == 0, corr, jnp.where(row == 1, norm, 0.0))


def arrive_kernel(terms, came_ref, turned_hbm, parts_hbm, moved_ref, sums_ref, marks, turned_ref, lefts_ref, sems):
    count, height, sector = came_ref.shape
    get_marks = pltpu.make_async_copy(came_ref.at[:, pl.ds(sector, height - sector)], marks, sems.at[0])
    get_lefts = pltpu.make_async_copy(parts_hbm.at[pl.ds(0, lefts_ref.shape[0])], lefts_ref, sems.at[1])
    get_turned = pltpu.make_async_copy(turned_hbm.at[pl.ds(0, count)], turned_ref, sems.at[2])
    get_marks.start()
    get_lefts.start()
    get_turned.start()
    get_marks.wait()
    get_lefts.wait()
    get_turned.wait()

    def block(i, total):
        stack = [lefts_ref[marks[i, 0, g].astype(jnp.int32)] for g in range(terms)]
        moved = product(jnp.concatenate(stack, axis=0), doubled(came_ref[i, :sector]))
        for g in range(terms):
            part = slice(g * sector, (g + 1) * sector)
            one = moved[part] * marks[i, 0, terms + g]
            moved_ref[i, part] = halves(one)
            total += jnp.sum((one * turned_ref[i, part]).reshape(-1, SUB, sector), axis=0)
        return total

    total = lax.fori_loop(0, count, block, jnp.zeros((SUB, sector), F32), unroll=4)
    corr = jnp.sum(total, axis=0, keepdims=True)
    row = lax.broadcasted_iota(jnp.int32, total.shape, 0)
    mine = turned_ref[0, terms * sector :] + jnp.where(row == 0, corr, 0.0)
    for i in range(sums_ref.shape[0]):
        sums_ref[i] = mine


def remote_kernel(sums_hbm, rindex_ref, out_index_ref, moved_ref, turned_hbm, parts_hbm, hpsi_rows, acc, near_ref, rights_ref, sems):
    slots, terms, _ = rindex_ref.shape
    senders, height, _ = moved_ref.shape
    sector = height // terms
    rights = rights_ref.shape[0]
    get_rights = pltpu.make_async_copy(parts_hbm.at[pl.ds(parts_hbm.shape[0] - rights, rights)], rights_ref, sems.at[0])
    get_rights.start()
    slabs = []
    for k in range(acc.shape[0] // height):
        near = turned_hbm.at[senders + k, pl.ds(0, height)]
        slabs.append(pltpu.make_async_copy(near, near_ref.at[pl.ds(k * height, height)], sems.at[1 + k]))
        slabs[k].start()
    acc[...] = jnp.zeros_like(acc)
    get_rights.wait()

    def right_step(i, carry):
        for g in range(terms):
            right = rights_ref[rindex_ref[i % slots, g, i // slots]]
            spot = pl.multiple_of(out_index_ref[i % slots, g, i // slots] * sector, sector)
            acc[pl.ds(spot, sector)] += product(moved_ref[i, g * sector : (g + 1) * sector], twice(right))
        return carry

    lax.fori_loop(0, senders, right_step, 0, unroll=4)
    for copy in slabs:
        copy.wait()
    for b in range(acc.shape[0] // sector):
        start = (b // SUB) * (SUB * sector) + b % SUB
        part = slice(b * sector, (b + 1) * sector)
        hpsi_rows[pl.ds(start, sector, stride=SUB), :] = acc[part] + near_ref[part]


def residual_kernel(sums_ref, hpsi_rows, psi_rows, hpsi_hbm, out_ref, sem):
    put = pltpu.make_async_copy(hpsi_rows, hpsi_hbm, sem)
    put.start()
    total = jnp.sum(sums_ref[...], axis=0)
    whole = jnp.sum(total, axis=1, keepdims=True)
    theta = whole[0:1] / (whole[1:2] + 1e-06)
    out_ref[...] = hpsi_rows[...] - theta * psi_rows[...]
    put.wait()


def shards(
    psi,
    left_env,
    right_env,
    send_block,
    send_left,
    send_live,
    recv_right,
    recv_out,
    loc_block,
    loc_left,
    loc_right,
):
    peers = lax.axis_size("renv")
    owned = psi.shape[0]
    sector = math.isqrt(psi.shape[1])
    slots = send_block.shape[1]
    terms = send_left.shape[2]
    count = peers * slots
    lefts = left_env.shape[0]
    rights = right_env.shape[0]
    height = sector + SUB
    psi_rows = as_rows(psi, sector)
    left_rows = as_rows(left_env, sector)
    right_rows = as_rows(right_env, sector)
    by_slot = [index.transpose(1, 2, 0) for index in (send_left, send_live, recv_right, recv_out)]
    blocks = jax.ShapeDtypeStruct((count, height, sector), F32)
    rows = jax.ShapeDtypeStruct((owned * sector, sector), F32)

    sent = pl.pallas_call(
        gather_kernel,
        out_shape=blocks,
        in_specs=[SMEM] * 3 + [VMEM],
        out_specs=HBM,
        scratch_shapes=[pltpu.VMEM(blocks.shape, F32), pltpu.SemaphoreType.DMA((count,))],
        compiler_params=roomy(56),
        name="gather_blocks",
    )(send_block.reshape(-1), *by_slot[:2], psi_rows)
    came = lax.all_to_all(sent.reshape(peers, slots, height, sector), "renv", split_axis=0, concat_axis=0, tiled=True)
    came = came.reshape(count, height, sector)

    slabs = owned // terms
    turned, parts = pl.pallas_call(
        prepare_kernel,
        out_shape=(
            jax.ShapeDtypeStruct((count + slabs, terms * sector + SUB, sector), F32),
            jax.ShapeDtypeStruct((lefts + rights, sector, 2 * sector), BF16),
        ),
        in_specs=[HBM] + [SMEM] * 5 + [VMEM] * 3,
        out_specs=(VMEM,) * 2,
        scratch_shapes=[
            pltpu.VMEM((owned, sector, sector), F32),
            pltpu.VMEM((owned, sector, 2 * sector), BF16),
            pltpu.VMEM((rights, 2 * sector, 2 * sector), BF16),
            pltpu.VMEM((loc_block.shape[0], sector, 2 * sector), BF16),
        ],
        compiler_params=roomy(56),
        cost_estimate=LIGHT,
        name="prepare",
    )(sent, *by_slot[2:], loc_block, loc_left, loc_right, psi_rows, right_rows, left_rows)

    near_by = math.gcd(peers, 4)
    chunk = math.gcd(count, 16)
    moved = []
    sums = 0.0
    for first in range(0, count, chunk):
        part = slice(first, first + chunk) if count > chunk else slice(None)
        kept, share = pl.pallas_call(
            lambda *refs: arrive_kernel(terms, *refs),
            out_shape=(
                jax.ShapeDtypeStruct((chunk, terms * sector, 2 * sector), BF16),
                jax.ShapeDtypeStruct((near_by, SUB, sector), F32),
            ),
            in_specs=[VMEM] + [HBM] * 2,
            out_specs=(VMEM,) * 2,
            scratch_shapes=[
                pltpu.SMEM((chunk, SUB, sector), F32),
                pltpu.VMEM((chunk, terms * sector + SUB, sector), F32),
                pltpu.VMEM((lefts, sector, 2 * sector), BF16),
                pltpu.SemaphoreType.DMA((3,)),
            ],
            compiler_params=roomy(50),
            name="arrive",
        )(came[part], turned if count == chunk else turned[part], parts)
        moved.append(kept)
        sums = share if count == chunk else sums + share
    moved = moved[0] if len(moved) == 1 else jnp.concatenate(moved, axis=0)
    together = [list(range(first, first + near_by)) for first in range(0, peers, near_by)]
    across = [list(range(first, peers, near_by)) for first in range(near_by)]
    totals = lax.all_to_all(sums, "renv", split_axis=0, concat_axis=0, tiled=True, axis_index_groups=together)
    first_sums = jnp.sum(totals, axis=0)
    totals = jnp.broadcast_to(first_sums[None], (peers // near_by, SUB, sector))
    totals = lax.all_to_all(totals, "renv", split_axis=0, concat_axis=0, tiled=True, axis_index_groups=across)

    hpsi_rows = pl.pallas_call(
        remote_kernel,
        out_shape=rows,
        in_specs=[HBM] + [SMEM] * 2 + [VMEM] + [HBM] * 2,
        out_specs=VMEM,
        scratch_shapes=[
            pltpu.VMEM(rows.shape, F32),
            pltpu.VMEM(rows.shape, F32),
            pltpu.VMEM((rights, sector, 2 * sector), BF16),
            pltpu.SemaphoreType.DMA((1 + slabs,)),
        ],
        compiler_params=roomy(50),
        cost_estimate=pl.CostEstimate(flops=4 * 10**9, bytes_accessed=6 * MIB, transcendentals=0),
        name="remote_terms",
    )(first_sums, *by_slot[2:], moved, turned, parts)

    hpsi, residual_rows = pl.pallas_call(
        residual_kernel,
        out_shape=(rows, rows),
        in_specs=[VMEM] * 3,
        out_specs=(HBM, VMEM),
        scratch_shapes=[pltpu.SemaphoreType.DMA],
        compiler_params=roomy(16),
        name="residual",
    )(totals, hpsi_rows, psi_rows)
    return (from_rows(hpsi, owned), from_rows(residual_rows, owned))


def solution(mesh):
    placed = (
        P(("groups", "renv"), None),
        P("groups", None),
        P(("groups", "renv"), None),
        P(("groups", "renv"), None),
        P(("groups", "renv"), None, None),
        P(("groups", "renv"), None, None),
        P(("groups", "renv"), None, None),
        P(("groups", "renv"), None, None),
        P(("groups", "renv")),
        P(("groups", "renv")),
        P(("groups", "renv")),
    )
    return jax.shard_map(
        shards,
        mesh=mesh,
        in_specs=placed,
        out_specs=(P(("groups", "renv"), None), P(("groups", "renv"), None)),
        check_vma=False,
    )
```

```python
import functools
import math

import jax
import jax.numpy as jnp
from jax import lax
from jax.experimental import pallas as pl
from jax.experimental.pallas import tpu as pltpu
from jax.sharding import PartitionSpec as P

F32 = jnp.float32
BF16 = jnp.bfloat16
SUB = 8
VMEM = pl.BlockSpec(memory_space=pltpu.VMEM)
SMEM = pl.BlockSpec(memory_space=pltpu.SMEM)
HBM = pl.BlockSpec(memory_space=pltpu.HBM)
MIB = 2**20
LIGHT = pl.CostEstimate(flops=10**6, bytes_accessed=2**16, transcendentals=0)


def as_rows(blocks, sector):
    count = blocks.shape[0]
    split = blocks.reshape(count // SUB, SUB, sector, sector)
    return split.transpose(0, 2, 1, 3).reshape(count * sector, sector)


def from_rows(rows, count):
    sector = rows.shape[1]
    split = rows.reshape(count // SUB, sector, SUB, sector)
    return split.transpose(0, 2, 1, 3).reshape(count, sector * sector)


def pick(ref, block):
    sector = ref.shape[1]
    start = (block // SUB) * (SUB * sector) + block % SUB
    return ref[pl.ds(start, sector, stride=SUB), :]


def halves(mat):
    high = mat.astype(BF16)
    low = (mat - high.astype(F32)).astype(BF16)
    return jnp.concatenate([high, low], axis=1)


def doubled(mat):
    both = halves(mat)
    return jnp.concatenate([both, both], axis=0)


def product(left, right):
    sector = right.shape[1] // 2
    wide = jnp.dot(left, right, preferred_element_type=F32)
    return wide[:, :sector] + wide[:, sector:]


def stacked(mat):
    high = mat.astype(BF16)
    low = (mat - high.astype(F32)).astype(BF16)
    rows = [jnp.concatenate([part, part], axis=1) for part in (high, low)]
    return jnp.concatenate(rows, axis=0)


def product_t(left, right):
    sector = right.shape[0] // 2
    wide = lax.dot_general(left, right, (((1,), (1,)), ((), ())), preferred_element_type=F32)
    return wide[:, :sector] + wide[:, sector:]


def twice(part):
    return jnp.concatenate([part, part], axis=0)


def roomy(mib):
    return pltpu.CompilerParams(vmem_limit_bytes=mib * MIB)


def gather_kernel(block_ref, left_ref, live_ref, psi_rows, out_hbm, stage, sems):
    slots, terms, _ = left_ref.shape
    sector = psi_rows.shape[1]
    lane = lax.broadcasted_iota(jnp.int32, (SUB, sector), 1)
    puts = []
    for i in range(stage.shape[0]):
        stage[i, :sector] = pick(psi_rows, block_ref[i])
        values = jnp.zeros(lane.shape, jnp.int32)
        for g in range(terms):
            values = jnp.where(lane == g, left_ref[i % slots, g, i // slots], values)
            values = jnp.where(lane == terms + g, live_ref[i % slots, g, i // slots], values)
        stage[i, sector:] = values.astype(F32)
        put = pltpu.make_async_copy(stage.at[i], out_hbm.at[i], sems.at[i])
        put.start()
        puts.append(put)
    for put in puts:
        put.wait()


def prepare_kernel(
    sent_hbm,
    rindex_ref,
    out_index_ref,
    block_ref,
    left_ref,
    right_ref,
    psi_rows,
    right_rows,
    left_rows,
    turned_ref,
    parts_ref,
    near_ref,
    psis_ref,
    stacks_ref,
    moved_ref,
):
    slots, terms, _ = rindex_ref.shape
    sector = psi_rows.shape[1]

    rights = right_rows.shape[0] // sector
    lefts = left_rows.shape[0] // sector

    def split_right(i, carry):
        mat = pick(right_rows, i)
        parts_ref[lefts + i] = halves(mat)
        stacks_ref[i] = stacked(mat)
        return carry

    lax.fori_loop(0, rights, split_right, 0, unroll=4)

    def split_psi(i, carry):
        psis_ref[i] = halves(pick(psi_rows, i))
        return carry

    lax.fori_loop(0, psis_ref.shape[0], split_psi, 0, unroll=4)

    def turn(i, carry):
        for g in range(terms):
            right = stacks_ref[rindex_ref[i % slots, g, i // slots]]
            psi = psis_ref[out_index_ref[i % slots, g, i // slots]]
            turned_ref[i, g * sector : (g + 1) * sector] = product_t(psi, right)
        turned_ref[i, terms * sector :] = jnp.zeros((SUB, sector), F32)
        return carry

    slabs = near_ref.shape[0] // terms
    senders = turned_ref.shape[0] - slabs
    lax.fori_loop(0, senders, turn, 0, unroll=4)

    def split_left(i, carry):
        parts_ref[i] = halves(pick(left_rows, i))
        return carry

    lax.fori_loop(0, lefts, split_left, 0, unroll=8)

    def left_step(k, carry):
        moved_ref[k] = halves(product(parts_ref[left_ref[k]], twice(psis_ref[block_ref[k]])))
        return carry

    lax.fori_loop(0, block_ref.shape[0], left_step, 0, unroll=8)
    near_ref[...] = jnp.zeros_like(near_ref)

    def right_step(k, carry):
        near_ref[block_ref[k]] += product(moved_ref[k], twice(parts_ref[lefts + right_ref[k]]))
        return carry

    lax.fori_loop(0, block_ref.shape[0], right_step, 0, unroll=8)
    corr = jnp.zeros((1, sector), F32)
    norm = jnp.zeros((1, sector), F32)
    for b in range(near_ref.shape[0]):
        mat = pick(psi_rows, b)
        turned_ref[senders + b // terms, (b % terms) * sector : (b % terms + 1) * sector] = near_ref[b]
        corr += jnp.sum(mat * near_ref[b], axis=0, keepdims=True)
        norm += jnp.sum(mat * mat, axis=0, keepdims=True)
    row = lax.broadcasted_iota(jnp.int32, (SUB, sector), 0)
    turned_ref[0, terms * sector :] = jnp.where(row == 0, corr, jnp.where(row == 1, norm, 0.0))


def arrive_kernel(terms, bounds, came_ref, turned_hbm, parts_hbm, *rest):
    moved_refs, rest = rest[: len(bounds) - 1], rest[len(bounds) - 1 :]
    rights_ref, sums_ref, marks, turned_ref, lefts_ref, sems = rest
    count, height, sector = came_ref.shape
    get_marks = pltpu.make_async_copy(came_ref.at[:, pl.ds(sector, height - sector)], marks, sems.at[0])
    get_lefts = pltpu.make_async_copy(parts_hbm.at[pl.ds(0, lefts_ref.shape[0])], lefts_ref, sems.at[1])
    get_turned = pltpu.make_async_copy(turned_hbm.at[pl.ds(0, count)], turned_ref, sems.at[2])
    get_rights = pltpu.make_async_copy(parts_hbm.at[pl.ds(lefts_ref.shape[0], rights_ref.shape[0])], rights_ref, sems.at[3])
    get_marks.start()
    get_lefts.start()
    get_turned.start()
    get_rights.start()
    get_marks.wait()
    get_lefts.wait()
    get_turned.wait()

    def block(first, moved_ref, i, total):
        stack = [lefts_ref[marks[i, 0, g].astype(jnp.int32)] for g in range(terms)]
        moved = product(jnp.concatenate(stack, axis=0), doubled(came_ref[i, :sector]))
        for g in range(terms):
            part = slice(g * sector, (g + 1) * sector)
            one = moved[part] * marks[i, 0, terms + g]
            moved_ref[i - first, part] = halves(one)
            total += jnp.sum((one * turned_ref[i, part]).reshape(-1, SUB, sector), axis=0)
        return total

    total = jnp.zeros((SUB, sector), F32)
    for first, last, moved_ref in zip(bounds[:-1], bounds[1:], moved_refs):
        total = lax.fori_loop(first, last, functools.partial(block, first, moved_ref), total, unroll=4)
    corr = jnp.sum(total, axis=0, keepdims=True)
    row = lax.broadcasted_iota(jnp.int32, total.shape, 0)
    sums_ref[...] = turned_ref[0, terms * sector :] + jnp.where(row == 0, corr, 0.0)
    get_rights.wait()


def remote_kernel(first, final, size, order_hbm, rindex_ref, out_index_ref, moved_ref, rights_ref, *rest):
    slots, terms, peers = rindex_ref.shape
    senders = slots * peers
    height = moved_ref.shape[1]
    sector = height // terms
    before, rest = (rest[:1], rest[1:]) if first else ((), rest)
    if final:
        turned_hbm, out_ref, acc, near_ref, sems = rest
        slabs = []
        for k in range(size // height):
            near = turned_hbm.at[senders + k, pl.ds(0, height)]
            slabs.append(pltpu.make_async_copy(near, near_ref.at[pl.ds(k * height, height)], sems.at[k]))
            slabs[k].start()
    else:
        (acc,) = rest
    acc[...] = before[0][...] if before else jnp.zeros_like(acc)

    def right_step(k, carry):
        i = first + k
        for g in range(terms):
            right = rights_ref[rindex_ref[i % slots, g, i // slots]]
            spot = pl.multiple_of(out_index_ref[i % slots, g, i // slots] * sector, sector)
            acc[pl.ds(spot, sector)] += product(moved_ref[k, g * sector : (g + 1) * sector], twice(right))
        return carry

    lax.fori_loop(0, moved_ref.shape[0], right_step, 0, unroll=4)
    if final:
        for copy in slabs:
            copy.wait()
        for b in range(size // sector):
            start = (b // SUB) * (SUB * sector) + b % SUB
            part = slice(b * sector, (b + 1) * sector)
            out_ref[pl.ds(start, sector, stride=SUB), :] = acc[part] + near_ref[part]


def residual_kernel(sums_ref, hpsi_rows, psi_rows, hpsi_hbm, out_ref, sem):
    put = pltpu.make_async_copy(hpsi_rows, hpsi_hbm, sem)
    put.start()
    whole = jnp.sum(sums_ref[...], axis=1, keepdims=True)
    theta = whole[0:1] / (whole[1:2] + 1e-06)
    out_ref[...] = hpsi_rows[...] - theta * psi_rows[...]
    put.wait()


def shards(
    psi,
    left_env,
    right_env,
    send_block,
    send_left,
    send_live,
    recv_right,
    recv_out,
    loc_block,
    loc_left,
    loc_right,
):
    peers = lax.axis_size("renv")
    owned = psi.shape[0]
    sector = math.isqrt(psi.shape[1])
    slots = send_block.shape[1]
    terms = send_left.shape[2]
    count = peers * slots
    lefts = left_env.shape[0]
    rights = right_env.shape[0]
    height = sector + SUB
    psi_rows = as_rows(psi, sector)
    left_rows = as_rows(left_env, sector)
    right_rows = as_rows(right_env, sector)
    by_slot = [index.transpose(1, 2, 0) for index in (send_left, send_live, recv_right, recv_out)]
    blocks = jax.ShapeDtypeStruct((count, height, sector), F32)
    rows = jax.ShapeDtypeStruct((owned * sector, sector), F32)

    sent = pl.pallas_call(
        gather_kernel,
        out_shape=blocks,
        in_specs=[SMEM] * 3 + [VMEM],
        out_specs=HBM,
        scratch_shapes=[pltpu.VMEM(blocks.shape, F32), pltpu.SemaphoreType.DMA((count,))],
        compiler_params=roomy(56),
        name="gather_blocks",
    )(send_block.reshape(-1), *by_slot[:2], psi_rows)
    came = lax.all_to_all(sent.reshape(peers, slots, height, sector), "renv", split_axis=0, concat_axis=0, tiled=True)
    came = came.reshape(count, height, sector)

    slabs = owned // terms
    turned, parts = pl.pallas_call(
        prepare_kernel,
        out_shape=(
            jax.ShapeDtypeStruct((count + slabs, terms * sector + SUB, sector), F32),
            jax.ShapeDtypeStruct((lefts + rights, sector, 2 * sector), BF16),
        ),
        in_specs=[HBM] + [SMEM] * 5 + [VMEM] * 3,
        out_specs=(VMEM,) * 2,
        scratch_shapes=[
            pltpu.VMEM((owned, sector, sector), F32),
            pltpu.VMEM((owned, sector, 2 * sector), BF16),
            pltpu.VMEM((rights, 2 * sector, 2 * sector), BF16),
            pltpu.VMEM((loc_block.shape[0], sector, 2 * sector), BF16),
        ],
        compiler_params=roomy(56),
        cost_estimate=LIGHT,
        name="prepare",
    )(sent, *by_slot[2:], loc_block, loc_left, loc_right, psi_rows, right_rows, left_rows)

    rounds = max(peers.bit_length() - 1, 1)
    chunk = math.gcd(count, 16)
    share_of = max(rounds * chunk // count, 1)
    bounds = [chunk * i // share_of for i in range(share_of + 1)]
    pieces = []
    sums = 0.0
    for base in range(0, count, chunk):
        part = slice(base, base + chunk)
        *kept, right_parts, share = pl.pallas_call(
            lambda *refs: arrive_kernel(terms, bounds, *refs),
            out_shape=(
                *(
                    jax.ShapeDtypeStruct((last - first, terms * sector, 2 * sector), BF16)
                    for first, last in zip(bounds[:-1], bounds[1:])
                ),
                jax.ShapeDtypeStruct((rights, sector, 2 * sector), BF16),
                jax.ShapeDtypeStruct((SUB, sector), F32),
            ),
            in_specs=[VMEM] + [HBM] * 2,
            out_specs=(VMEM,) * (share_of + 2),
            scratch_shapes=[
                pltpu.SMEM((chunk, SUB, sector), F32),
                pltpu.VMEM((chunk, terms * sector + SUB, sector), F32),
                pltpu.VMEM((lefts, sector, 2 * sector), BF16),
                pltpu.SemaphoreType.DMA((4,)),
            ],
            compiler_params=roomy(48),
            name="arrive",
        )(came if count == chunk else came[part], turned if count == chunk else turned[part], parts)
        pieces += [(base + first, moved) for first, moved in zip(bounds, kept)]
        sums = share if count == chunk else sums + share

    hpsi_rows = None
    for number in range(max(rounds, len(pieces))):
        got = None
        if number < rounds:
            step = 1 << number
            got = lax.ppermute(sums, "renv", [(s, s ^ step) for s in range(peers)])
        if number < len(pieces):
            first, moved = pieces[number]
            final = number == len(pieces) - 1
            hpsi_rows = pl.pallas_call(
                lambda *refs, first=first, final=final: remote_kernel(first, final, owned * sector, *refs),
                out_shape=rows,
                in_specs=[HBM] + [SMEM] * 2 + [VMEM] * (3 if first else 2) + [HBM] * final,
                out_specs=VMEM,
                scratch_shapes=[
                    pltpu.VMEM(rows.shape, F32),
                    pltpu.VMEM(rows.shape, F32),
                    pltpu.SemaphoreType.DMA((slabs,)),
                ]
                * final,
                input_output_aliases={} if final or not first else {5: 0},
                compiler_params=roomy(50),
                cost_estimate=pl.CostEstimate(flops=10**9, bytes_accessed=2 * MIB, transcendentals=0),
                name=f"remote_terms_{number}",
            )(sums, *by_slot[2:], moved, right_parts, *([hpsi_rows] if first else []), *([turned] if final else []))
        if got is not None:
            sums = sums + got

    hpsi, residual_rows = pl.pallas_call(
        residual_kernel,
        out_shape=(rows, rows),
        in_specs=[VMEM] * 3,
        out_specs=(HBM, VMEM),
        scratch_shapes=[pltpu.SemaphoreType.DMA],
        compiler_params=roomy(16),
        name="residual",
    )(sums, hpsi_rows, psi_rows)
    return (from_rows(hpsi, owned), from_rows(residual_rows, owned))


def solution(mesh):
    placed = (
        P(("groups", "renv"), None),
        P("groups", None),
        P(("groups", "renv"), None),
        P(("groups", "renv"), None),
        P(("groups", "renv"), None, None),
        P(("groups", "renv"), None, None),
        P(("groups", "renv"), None, None),
        P(("groups", "renv"), None, None),
        P(("groups", "renv")),
        P(("groups", "renv")),
        P(("groups", "renv")),
    )
    return jax.shard_map(
        shards,
        mesh=mesh,
        in_specs=placed,
        out_specs=(P(("groups", "renv"), None), P(("groups", "renv"), None)),
        check_vma=False,
    )
```

```python
import math

import jax
import jax.numpy as jnp
from jax import lax
from jax.experimental import pallas as pl
from jax.experimental.pallas import tpu as pltpu
from jax.sharding import PartitionSpec as P

F32 = jnp.float32
BF16 = jnp.bfloat16
SUB = 8
VMEM = pl.BlockSpec(memory_space=pltpu.VMEM)
SMEM = pl.BlockSpec(memory_space=pltpu.SMEM)
HBM = pl.BlockSpec(memory_space=pltpu.HBM)
MIB = 2**20
LIGHT = pl.CostEstimate(flops=10**6, bytes_accessed=2**16, transcendentals=0)


def as_rows(blocks, sector):
    count = blocks.shape[0]
    split = blocks.reshape(count // SUB, SUB, sector, sector)
    return split.transpose(0, 2, 1, 3).reshape(count * sector, sector)


def from_rows(rows, count):
    sector = rows.shape[1]
    split = rows.reshape(count // SUB, sector, SUB, sector)
    return split.transpose(0, 2, 1, 3).reshape(count, sector * sector)


def pick(ref, block):
    sector = ref.shape[1]
    start = (block // SUB) * (SUB * sector) + block % SUB
    return ref[pl.ds(start, sector, stride=SUB), :]


def halves(mat):
    high = mat.astype(BF16)
    low = (mat - high.astype(F32)).astype(BF16)
    return jnp.concatenate([high, low], axis=1)


def doubled(mat):
    both = halves(mat)
    return jnp.concatenate([both, both], axis=0)


def product(left, right):
    sector = right.shape[1] // 2
    wide = jnp.dot(left, right, preferred_element_type=F32)
    return wide[:, :sector] + wide[:, sector:]


def stacked(mat):
    high = mat.astype(BF16)
    low = (mat - high.astype(F32)).astype(BF16)
    rows = [jnp.concatenate([part, part], axis=1) for part in (high, low)]
    return jnp.concatenate(rows, axis=0)


def product_t(left, right):
    sector = right.shape[0] // 2
    wide = lax.dot_general(left, right, (((1,), (1,)), ((), ())), preferred_element_type=F32)
    return wide[:, :sector] + wide[:, sector:]


def twice(part):
    return jnp.concatenate([part, part], axis=0)


def roomy(mib):
    return pltpu.CompilerParams(vmem_limit_bytes=mib * MIB)


def gather_kernel(block_ref, left_ref, live_ref, psi_rows, out_hbm, stage, sems):
    slots, terms, _ = left_ref.shape
    sector = psi_rows.shape[1]
    lane = lax.broadcasted_iota(jnp.int32, (SUB, sector), 1)
    puts = []
    for i in range(stage.shape[0]):
        stage[i, :sector] = pick(psi_rows, block_ref[i])
        values = jnp.zeros(lane.shape, jnp.int32)
        for g in range(terms):
            values = jnp.where(lane == g, left_ref[i % slots, g, i // slots], values)
            values = jnp.where(lane == terms + g, live_ref[i % slots, g, i // slots], values)
        stage[i, sector:] = values.astype(F32)
        put = pltpu.make_async_copy(stage.at[i], out_hbm.at[i], sems.at[i])
        put.start()
        puts.append(put)
    for put in puts:
        put.wait()


def prepare_kernel(
    sent_hbm,
    rindex_ref,
    out_index_ref,
    block_ref,
    left_ref,
    right_ref,
    psi_rows,
    right_rows,
    left_rows,
    turned_ref,
    parts_ref,
    near_ref,
    psis_ref,
    stacks_ref,
    moved_ref,
):
    slots, terms, _ = rindex_ref.shape
    sector = psi_rows.shape[1]

    rights = right_rows.shape[0] // sector
    lefts = left_rows.shape[0] // sector

    def split_right(i, carry):
        mat = pick(right_rows, i)
        parts_ref[lefts + i] = halves(mat)
        stacks_ref[i] = stacked(mat)
        return carry

    lax.fori_loop(0, rights, split_right, 0, unroll=4)

    def split_psi(i, carry):
        psis_ref[i] = halves(pick(psi_rows, i))
        return carry

    lax.fori_loop(0, psis_ref.shape[0], split_psi, 0, unroll=4)

    def turn(i, carry):
        for g in range(terms):
            right = stacks_ref[rindex_ref[i % slots, g, i // slots]]
            psi = psis_ref[out_index_ref[i % slots, g, i // slots]]
            turned_ref[i, g * sector : (g + 1) * sector] = product_t(psi, right)
        turned_ref[i, terms * sector :] = jnp.zeros((SUB, sector), F32)
        return carry

    slabs = near_ref.shape[0] // terms
    senders = turned_ref.shape[0] - slabs
    lax.fori_loop(0, senders, turn, 0, unroll=4)

    def split_left(i, carry):
        parts_ref[i] = halves(pick(left_rows, i))
        return carry

    lax.fori_loop(0, lefts, split_left, 0, unroll=8)

    def left_step(k, carry):
        moved_ref[k] = halves(product(parts_ref[left_ref[k]], twice(psis_ref[block_ref[k]])))
        return carry

    lax.fori_loop(0, block_ref.shape[0], left_step, 0, unroll=8)
    near_ref[...] = jnp.zeros_like(near_ref)

    def right_step(k, carry):
        near_ref[block_ref[k]] += product(moved_ref[k], twice(parts_ref[lefts + right_ref[k]]))
        return carry

    lax.fori_loop(0, block_ref.shape[0], right_step, 0, unroll=8)
    corr = jnp.zeros((1, sector), F32)
    norm = jnp.zeros((1, sector), F32)
    for b in range(near_ref.shape[0]):
        mat = pick(psi_rows, b)
        turned_ref[senders + b // terms, (b % terms) * sector : (b % terms + 1) * sector] = near_ref[b]
        corr += jnp.sum(mat * near_ref[b], axis=0, keepdims=True)
        norm += jnp.sum(mat * mat, axis=0, keepdims=True)
    row = lax.broadcasted_iota(jnp.int32, (SUB, sector), 0)
    turned_ref[0, terms * sector :] = jnp.where(row == 0, corr, jnp.where(row == 1, norm, 0.0))


def arrive_kernel(terms, came_ref, turned_hbm, parts_hbm, moved_ref, sums_ref, marks, turned_ref, lefts_ref, sems):
    count, height, sector = came_ref.shape
    get_marks = pltpu.make_async_copy(came_ref.at[:, pl.ds(sector, height - sector)], marks, sems.at[0])
    get_lefts = pltpu.make_async_copy(parts_hbm.at[pl.ds(0, lefts_ref.shape[0])], lefts_ref, sems.at[1])
    get_turned = pltpu.make_async_copy(turned_hbm.at[pl.ds(0, count)], turned_ref, sems.at[2])
    get_marks.start()
    get_lefts.start()
    get_turned.start()
    get_marks.wait()
    get_lefts.wait()
    get_turned.wait()

    def block(i, total):
        stack = [lefts_ref[marks[i, 0, g].astype(jnp.int32)] for g in range(terms)]
        moved = product(jnp.concatenate(stack, axis=0), doubled(came_ref[i, :sector]))
        for g in range(terms):
            part = slice(g * sector, (g + 1) * sector)
            one = moved[part] * marks[i, 0, terms + g]
            moved_ref[i, part] = halves(one)
            total += jnp.sum((one * turned_ref[i, part]).reshape(-1, SUB, sector), axis=0)
        return total

    total = lax.fori_loop(0, count, block, jnp.zeros((SUB, sector), F32), unroll=16)
    corr = jnp.sum(total, axis=0, keepdims=True)
    row = lax.broadcasted_iota(jnp.int32, total.shape, 0)
    mine = turned_ref[0, terms * sector :] + jnp.where(row == 0, corr, 0.0)
    folded = mine + pltpu.roll(mine, sector // 2, 1)
    lane = lax.broadcasted_iota(jnp.int32, (1, sector), 1)
    shared = jnp.where(lane < sector // 2, folded[0:1], folded[1:2])
    for i in range(sums_ref.shape[0]):
        sums_ref[i] = shared


def remote_kernel(rindex_ref, out_index_ref, moved_ref, turned_hbm, parts_hbm, hpsi_rows, acc, near_ref, rights_ref, sems):
    slots, terms, _ = rindex_ref.shape
    senders, height, _ = moved_ref.shape
    sector = height // terms
    rights = rights_ref.shape[0]
    get_rights = pltpu.make_async_copy(parts_hbm.at[pl.ds(parts_hbm.shape[0] - rights, rights)], rights_ref, sems.at[0])
    get_rights.start()
    slabs = []
    for k in range(acc.shape[0] // height):
        near = turned_hbm.at[senders + k, pl.ds(0, height)]
        slabs.append(pltpu.make_async_copy(near, near_ref.at[pl.ds(k * height, height)], sems.at[1 + k]))
        slabs[k].start()
    acc[...] = jnp.zeros_like(acc)
    get_rights.wait()

    def right_step(i, carry):
        for g in range(terms):
            right = rights_ref[rindex_ref[i % slots, g, i // slots]]
            spot = pl.multiple_of(out_index_ref[i % slots, g, i // slots] * sector, sector)
            acc[pl.ds(spot, sector)] += product(moved_ref[i, g * sector : (g + 1) * sector], twice(right))
        return carry

    lax.fori_loop(0, senders, right_step, 0, unroll=4)
    for copy in slabs:
        copy.wait()
    for b in range(acc.shape[0] // sector):
        start = (b // SUB) * (SUB * sector) + b % SUB
        part = slice(b * sector, (b + 1) * sector)
        hpsi_rows[pl.ds(start, sector, stride=SUB), :] = acc[part] + near_ref[part]


def residual_kernel(sums_ref, hpsi_rows, psi_rows, hpsi_hbm, out_ref, sem):
    put = pltpu.make_async_copy(hpsi_rows, hpsi_hbm, sem)
    put.start()
    total = jnp.sum(sums_ref[...], axis=0)
    lane = lax.broadcasted_iota(jnp.int32, total.shape, 1)
    first = lane < total.shape[1] // 2
    corr = jnp.sum(jnp.where(first, total, 0.0), axis=1, keepdims=True)
    norm = jnp.sum(jnp.where(first, 0.0, total), axis=1, keepdims=True)
    theta = corr / (norm + 1e-06)
    out_ref[...] = hpsi_rows[...] - theta * psi_rows[...]
    put.wait()


def shards(
    psi,
    left_env,
    right_env,
    send_block,
    send_left,
    send_live,
    recv_right,
    recv_out,
    loc_block,
    loc_left,
    loc_right,
):
    peers = lax.axis_size("renv")
    owned = psi.shape[0]
    sector = math.isqrt(psi.shape[1])
    slots = send_block.shape[1]
    terms = send_left.shape[2]
    count = peers * slots
    lefts = left_env.shape[0]
    rights = right_env.shape[0]
    height = sector + SUB
    psi_rows = as_rows(psi, sector)
    left_rows = as_rows(left_env, sector)
    right_rows = as_rows(right_env, sector)
    by_slot = [index.transpose(1, 2, 0) for index in (send_left, send_live, recv_right, recv_out)]
    blocks = jax.ShapeDtypeStruct((count, height, sector), F32)
    rows = jax.ShapeDtypeStruct((owned * sector, sector), F32)

    sent = pl.pallas_call(
        gather_kernel,
        out_shape=blocks,
        in_specs=[SMEM] * 3 + [VMEM],
        out_specs=HBM,
        scratch_shapes=[pltpu.VMEM(blocks.shape, F32), pltpu.SemaphoreType.DMA((count,))],
        compiler_params=roomy(56),
        name="gather_blocks",
    )(send_block.reshape(-1), *by_slot[:2], psi_rows)
    came = lax.all_to_all(sent.reshape(peers, slots, height, sector), "renv", split_axis=0, concat_axis=0, tiled=True)
    came = came.reshape(count, height, sector)

    slabs = owned // terms
    turned, parts = pl.pallas_call(
        prepare_kernel,
        out_shape=(
            jax.ShapeDtypeStruct((count + slabs, terms * sector + SUB, sector), F32),
            jax.ShapeDtypeStruct((lefts + rights, sector, 2 * sector), BF16),
        ),
        in_specs=[HBM] + [SMEM] * 5 + [VMEM] * 3,
        out_specs=(VMEM,) * 2,
        scratch_shapes=[
            pltpu.VMEM((owned, sector, sector), F32),
            pltpu.VMEM((owned, sector, 2 * sector), BF16),
            pltpu.VMEM((rights, 2 * sector, 2 * sector), BF16),
            pltpu.VMEM((loc_block.shape[0], sector, 2 * sector), BF16),
        ],
        compiler_params=roomy(56),
        cost_estimate=LIGHT,
        name="prepare",
    )(sent, *by_slot[2:], loc_block, loc_left, loc_right, psi_rows, right_rows, left_rows)

    chunk = math.gcd(count, 16)
    moved = []
    sums = 0.0
    for first in range(0, count, chunk):
        part = slice(first, first + chunk) if count > chunk else slice(None)
        kept, share = pl.pallas_call(
            lambda *refs: arrive_kernel(terms, *refs),
            out_shape=(
                jax.ShapeDtypeStruct((chunk, terms * sector, 2 * sector), BF16),
                jax.ShapeDtypeStruct((peers, 1, sector), F32),
            ),
            in_specs=[VMEM] + [HBM] * 2,
            out_specs=(VMEM,) * 2,
            scratch_shapes=[
                pltpu.SMEM((chunk, SUB, sector), F32),
                pltpu.VMEM((chunk, terms * sector + SUB, sector), F32),
                pltpu.VMEM((lefts, sector, 2 * sector), BF16),
                pltpu.SemaphoreType.DMA((3,)),
            ],
            compiler_params=roomy(50),
            name="arrive",
        )(came[part], turned if count == chunk else turned[part], parts)
        moved.append(kept)
        sums = share if count == chunk else sums + share
    moved = moved[0] if len(moved) == 1 else jnp.concatenate(moved, axis=0)
    totals = lax.all_to_all(sums, "renv", split_axis=0, concat_axis=0, tiled=True)

    hpsi_rows = pl.pallas_call(
        remote_kernel,
        out_shape=rows,
        in_specs=[SMEM] * 2 + [VMEM] + [HBM] * 2,
        out_specs=VMEM,
        scratch_shapes=[
            pltpu.VMEM(rows.shape, F32),
            pltpu.VMEM(rows.shape, F32),
            pltpu.VMEM((rights, sector, 2 * sector), BF16),
            pltpu.SemaphoreType.DMA((1 + slabs,)),
        ],
        compiler_params=roomy(50),
        cost_estimate=pl.CostEstimate(flops=4 * 10**9, bytes_accessed=6 * MIB, transcendentals=0),
        name="remote_terms",
    )(*by_slot[2:], moved, turned, parts)

    hpsi, residual_rows = pl.pallas_call(
        residual_kernel,
        out_shape=(rows, rows),
        in_specs=[VMEM] * 3,
        out_specs=(HBM, VMEM),
        scratch_shapes=[pltpu.SemaphoreType.DMA],
        compiler_params=roomy(16),
        name="residual",
    )(totals, hpsi_rows, psi_rows)
    return (from_rows(hpsi, owned), from_rows(residual_rows, owned))


def solution(mesh):
    placed = (
        P(("groups", "renv"), None),
        P("groups", None),
        P(("groups", "renv"), None),
        P(("groups", "renv"), None),
        P(("groups", "renv"), None, None),
        P(("groups", "renv"), None, None),
        P(("groups", "renv"), None, None),
        P(("groups", "renv"), None, None),
        P(("groups", "renv")),
        P(("groups", "renv")),
        P(("groups", "renv")),
    )
    return jax.shard_map(
        shards,
        mesh=mesh,
        in_specs=placed,
        out_specs=(P(("groups", "renv"), None), P(("groups", "renv"), None)),
        check_vma=False,
    )
```

```python
import math

import jax
import jax.numpy as jnp
from jax import lax
from jax.experimental import pallas as pl
from jax.experimental.pallas import tpu as pltpu
from jax.sharding import PartitionSpec as P

F32 = jnp.float32
BF16 = jnp.bfloat16
SUB = 8
VMEM = pl.BlockSpec(memory_space=pltpu.VMEM)
SMEM = pl.BlockSpec(memory_space=pltpu.SMEM)
HBM = pl.BlockSpec(memory_space=pltpu.HBM)
MIB = 2**20
LIGHT = pl.CostEstimate(flops=10**6, bytes_accessed=2**16, transcendentals=0)


def as_rows(blocks, sector):
    count = blocks.shape[0]
    split = blocks.reshape(count // SUB, SUB, sector, sector)
    return split.transpose(0, 2, 1, 3).reshape(count * sector, sector)


def from_rows(rows, count):
    sector = rows.shape[1]
    split = rows.reshape(count // SUB, sector, SUB, sector)
    return split.transpose(0, 2, 1, 3).reshape(count, sector * sector)


def pick(ref, block):
    sector = ref.shape[1]
    start = (block // SUB) * (SUB * sector) + block % SUB
    return ref[pl.ds(start, sector, stride=SUB), :]


def halves(mat):
    high = mat.astype(BF16)
    low = (mat - high.astype(F32)).astype(BF16)
    return jnp.concatenate([high, low], axis=1)


def doubled(mat):
    both = halves(mat)
    return jnp.concatenate([both, both], axis=0)


def product(left, right):
    sector = right.shape[1] // 2
    wide = jnp.dot(left, right, preferred_element_type=F32)
    return wide[:, :sector] + wide[:, sector:]


def stacked(mat):
    high = mat.astype(BF16)
    low = (mat - high.astype(F32)).astype(BF16)
    rows = [jnp.concatenate([part, part], axis=1) for part in (high, low)]
    return jnp.concatenate(rows, axis=0)


def product_t(left, right):
    sector = right.shape[0] // 2
    wide = lax.dot_general(left, right, (((1,), (1,)), ((), ())), preferred_element_type=F32)
    return wide[:, :sector] + wide[:, sector:]


def twice(part):
    return jnp.concatenate([part, part], axis=0)


def roomy(mib):
    return pltpu.CompilerParams(vmem_limit_bytes=mib * MIB)


def gather_kernel(block_ref, left_ref, live_ref, psi_rows, out_hbm, stage, sems):
    slots, terms, _ = left_ref.shape
    sector = psi_rows.shape[1]
    lane = lax.broadcasted_iota(jnp.int32, (SUB, sector), 1)
    puts = []
    for i in range(stage.shape[0]):
        stage[i, :sector] = pick(psi_rows, block_ref[i])
        values = jnp.zeros(lane.shape, jnp.int32)
        for g in range(terms):
            values = jnp.where(lane == g, left_ref[i % slots, g, i // slots], values)
            values = jnp.where(lane == terms + g, live_ref[i % slots, g, i // slots], values)
        stage[i, sector:] = values.astype(F32)
        put = pltpu.make_async_copy(stage.at[i], out_hbm.at[i], sems.at[i])
        put.start()
        puts.append(put)
    for put in puts:
        put.wait()


def prepare_kernel(
    sent_hbm,
    rindex_ref,
    out_index_ref,
    block_ref,
    left_ref,
    right_ref,
    psi_rows,
    right_rows,
    left_rows,
    turned_ref,
    parts_ref,
    near_ref,
    psis_ref,
    stacks_ref,
    moved_ref,
):
    slots, terms, _ = rindex_ref.shape
    sector = psi_rows.shape[1]

    rights = right_rows.shape[0] // sector
    lefts = left_rows.shape[0] // sector

    def split_right(i, carry):
        mat = pick(right_rows, i)
        parts_ref[lefts + i] = halves(mat)
        stacks_ref[i] = stacked(mat)
        return carry

    lax.fori_loop(0, rights, split_right, 0, unroll=4)

    def split_psi(i, carry):
        psis_ref[i] = halves(pick(psi_rows, i))
        return carry

    lax.fori_loop(0, psis_ref.shape[0], split_psi, 0, unroll=4)

    def turn(i, carry):
        for g in range(terms):
            right = stacks_ref[rindex_ref[i % slots, g, i // slots]]
            psi = psis_ref[out_index_ref[i % slots, g, i // slots]]
            turned_ref[i, g * sector : (g + 1) * sector] = product_t(psi, right)
        turned_ref[i, terms * sector :] = jnp.zeros((SUB, sector), F32)
        return carry

    slabs = near_ref.shape[0] // terms
    senders = turned_ref.shape[0] - slabs
    lax.fori_loop(0, senders, turn, 0, unroll=4)

    def split_left(i, carry):
        parts_ref[i] = halves(pick(left_rows, i))
        return carry

    lax.fori_loop(0, lefts, split_left, 0, unroll=8)

    def left_step(k, carry):
        moved_ref[k] = halves(product(parts_ref[left_ref[k]], twice(psis_ref[block_ref[k]])))
        return carry

    lax.fori_loop(0, block_ref.shape[0], left_step, 0, unroll=8)
    near_ref[...] = jnp.zeros_like(near_ref)

    def right_step(k, carry):
        near_ref[block_ref[k]] += product(moved_ref[k], twice(parts_ref[lefts + right_ref[k]]))
        return carry

    lax.fori_loop(0, block_ref.shape[0], right_step, 0, unroll=8)
    corr = jnp.zeros((1, sector), F32)
    norm = jnp.zeros((1, sector), F32)
    for b in range(near_ref.shape[0]):
        mat = pick(psi_rows, b)
        turned_ref[senders + b // terms, (b % terms) * sector : (b % terms + 1) * sector] = near_ref[b]
        corr += jnp.sum(mat * near_ref[b], axis=0, keepdims=True)
        norm += jnp.sum(mat * mat, axis=0, keepdims=True)
    row = lax.broadcasted_iota(jnp.int32, (SUB, sector), 0)
    turned_ref[0, terms * sector :] = jnp.where(row == 0, corr, jnp.where(row == 1, norm, 0.0))


def arrive_kernel(terms, came_ref, turned_hbm, parts_hbm, moved_ref, sums_ref, marks, turned_ref, lefts_ref, weights_ref, sems):
    count, height, sector = came_ref.shape
    get_marks = pltpu.make_async_copy(came_ref.at[:, pl.ds(sector, height - sector)], marks, sems.at[0])
    get_lefts = pltpu.make_async_copy(parts_hbm.at[pl.ds(0, lefts_ref.shape[0])], lefts_ref, sems.at[1])
    quarter = count // math.gcd(count, 4)
    spans = [pl.ds(first, quarter) for first in range(0, count, quarter)]
    get_turned = [
        pltpu.make_async_copy(turned_hbm.at[span], turned_ref.at[span], sems.at[2 + k]) for k, span in enumerate(spans)
    ]
    for copy in (get_marks, get_lefts, *get_turned):
        copy.start()

    def split(i, carry):
        weights_ref[i] = doubled(came_ref[i, :sector])
        return carry

    lax.fori_loop(0, count, split, 0, unroll=4)
    get_marks.wait()
    get_lefts.wait()

    def block(i, total):
        stack = [lefts_ref[marks[i, 0, g].astype(jnp.int32)] for g in range(terms)]
        moved = product(jnp.concatenate(stack, axis=0), weights_ref[i])
        for g in range(terms):
            part = slice(g * sector, (g + 1) * sector)
            one = moved[part] * marks[i, 0, terms + g]
            moved_ref[i, part] = halves(one)
            total += jnp.sum((one * turned_ref[i, part]).reshape(-1, SUB, sector), axis=0)
        return total

    total = jnp.zeros((SUB, sector), F32)
    for k, copy in enumerate(get_turned):
        copy.wait()
        total = lax.fori_loop(k * quarter, (k + 1) * quarter, block, total, unroll=4)
    corr = jnp.sum(total, axis=0, keepdims=True)
    row = lax.broadcasted_iota(jnp.int32, total.shape, 0)
    mine = turned_ref[0, terms * sector :] + jnp.where(row == 0, corr, 0.0)
    folded = mine + pltpu.roll(mine, sector // 2, 1)
    lane = lax.broadcasted_iota(jnp.int32, (1, sector), 1)
    shared = jnp.where(lane < sector // 2, folded[0:1], folded[1:2])
    for i in range(sums_ref.shape[0]):
        sums_ref[i] = shared


def remote_kernel(rindex_ref, out_index_ref, moved_ref, turned_hbm, parts_hbm, hpsi_rows, hpsi_hbm, acc, near_ref, rights_ref, sems):
    slots, terms, _ = rindex_ref.shape
    senders, height, _ = moved_ref.shape
    sector = height // terms
    rights = rights_ref.shape[0]
    get_rights = pltpu.make_async_copy(parts_hbm.at[pl.ds(parts_hbm.shape[0] - rights, rights)], rights_ref, sems.at[0])
    get_rights.start()
    slabs = []
    for k in range(acc.shape[0] // height):
        near = turned_hbm.at[senders + k, pl.ds(0, height)]
        slabs.append(pltpu.make_async_copy(near, near_ref.at[pl.ds(k * height, height)], sems.at[1 + k]))
        slabs[k].start()
    acc[...] = jnp.zeros_like(acc)
    get_rights.wait()

    def right_step(i, carry):
        for g in range(terms):
            right = rights_ref[rindex_ref[i % slots, g, i // slots]]
            spot = pl.multiple_of(out_index_ref[i % slots, g, i // slots] * sector, sector)
            acc[pl.ds(spot, sector)] += product(moved_ref[i, g * sector : (g + 1) * sector], twice(right))
        return carry

    lax.fori_loop(0, senders, right_step, 0, unroll=4)
    for copy in slabs:
        copy.wait()
    for b in range(acc.shape[0] // sector):
        start = (b // SUB) * (SUB * sector) + b % SUB
        part = slice(b * sector, (b + 1) * sector)
        hpsi_rows[pl.ds(start, sector, stride=SUB), :] = acc[part] + near_ref[part]
    put = pltpu.make_async_copy(hpsi_rows, hpsi_hbm, sems.at[0])
    put.start()
    put.wait()


def residual_kernel(sums_ref, hpsi_rows, psi_rows, out_ref):
    total = jnp.sum(sums_ref[...], axis=0)
    lane = lax.broadcasted_iota(jnp.int32, total.shape, 1)
    first = lane < total.shape[1] // 2
    corr = jnp.sum(jnp.where(first, total, 0.0), axis=1, keepdims=True)
    norm = jnp.sum(jnp.where(first, 0.0, total), axis=1, keepdims=True)
    theta = corr / (norm + 1e-06)
    out_ref[...] = hpsi_rows[...] - theta * psi_rows[...]


def shards(
    psi,
    left_env,
    right_env,
    send_block,
    send_left,
    send_live,
    recv_right,
    recv_out,
    loc_block,
    loc_left,
    loc_right,
):
    peers = lax.axis_size("renv")
    owned = psi.shape[0]
    sector = math.isqrt(psi.shape[1])
    slots = send_block.shape[1]
    terms = send_left.shape[2]
    count = peers * slots
    lefts = left_env.shape[0]
    rights = right_env.shape[0]
    height = sector + SUB
    psi_rows = as_rows(psi, sector)
    left_rows = as_rows(left_env, sector)
    right_rows = as_rows(right_env, sector)
    by_slot = [index.transpose(1, 2, 0) for index in (send_left, send_live, recv_right, recv_out)]
    blocks = jax.ShapeDtypeStruct((count, height, sector), F32)
    rows = jax.ShapeDtypeStruct((owned * sector, sector), F32)

    sent = pl.pallas_call(
        gather_kernel,
        out_shape=blocks,
        in_specs=[SMEM] * 3 + [VMEM],
        out_specs=HBM,
        scratch_shapes=[pltpu.VMEM(blocks.shape, F32), pltpu.SemaphoreType.DMA((count,))],
        compiler_params=roomy(56),
        name="gather_blocks",
    )(send_block.reshape(-1), *by_slot[:2], psi_rows)
    came = lax.all_to_all(sent.reshape(peers, slots, height, sector), "renv", split_axis=0, concat_axis=0, tiled=True)
    came = came.reshape(count, height, sector)

    slabs = owned // terms
    turned, parts = pl.pallas_call(
        prepare_kernel,
        out_shape=(
            jax.ShapeDtypeStruct((count + slabs, terms * sector + SUB, sector), F32),
            jax.ShapeDtypeStruct((lefts + rights, sector, 2 * sector), BF16),
        ),
        in_specs=[HBM] + [SMEM] * 5 + [VMEM] * 3,
        out_specs=(VMEM,) * 2,
        scratch_shapes=[
            pltpu.VMEM((owned, sector, sector), F32),
            pltpu.VMEM((owned, sector, 2 * sector), BF16),
            pltpu.VMEM((rights, 2 * sector, 2 * sector), BF16),
            pltpu.VMEM((loc_block.shape[0], sector, 2 * sector), BF16),
        ],
        compiler_params=roomy(56),
        cost_estimate=LIGHT,
        name="prepare",
    )(sent, *by_slot[2:], loc_block, loc_left, loc_right, psi_rows, right_rows, left_rows)

    chunk = math.gcd(count, 16)
    moved = []
    sums = 0.0
    for first in range(0, count, chunk):
        part = slice(first, first + chunk) if count > chunk else slice(None)
        kept, share = pl.pallas_call(
            lambda *refs: arrive_kernel(terms, *refs),
            out_shape=(
                jax.ShapeDtypeStruct((chunk, terms * sector, 2 * sector), BF16),
                jax.ShapeDtypeStruct((peers, 1, sector), F32),
            ),
            in_specs=[VMEM] + [HBM] * 2,
            out_specs=(VMEM,) * 2,
            scratch_shapes=[
                pltpu.SMEM((chunk, SUB, sector), F32),
                pltpu.VMEM((chunk, terms * sector + SUB, sector), F32),
                pltpu.VMEM((lefts, sector, 2 * sector), BF16),
                pltpu.VMEM((chunk, 2 * sector, 2 * sector), BF16),
                pltpu.SemaphoreType.DMA((6,)),
            ],
            compiler_params=roomy(50),
            name="arrive",
        )(came[part], turned if count == chunk else turned[part], parts)
        moved.append(kept)
        sums = share if count == chunk else sums + share
    moved = moved[0] if len(moved) == 1 else jnp.concatenate(moved, axis=0)
    totals = lax.all_to_all(sums, "renv", split_axis=0, concat_axis=0, tiled=True)

    hpsi_rows, hpsi = pl.pallas_call(
        remote_kernel,
        out_shape=(rows, rows),
        in_specs=[SMEM] * 2 + [VMEM] + [HBM] * 2,
        out_specs=(VMEM, HBM),
        scratch_shapes=[
            pltpu.VMEM(rows.shape, F32),
            pltpu.VMEM(rows.shape, F32),
            pltpu.VMEM((rights, sector, 2 * sector), BF16),
            pltpu.SemaphoreType.DMA((1 + slabs,)),
        ],
        compiler_params=roomy(50),
        cost_estimate=pl.CostEstimate(flops=4 * 10**9, bytes_accessed=6 * MIB, transcendentals=0),
        name="remote_terms",
    )(*by_slot[2:], moved, turned, parts)

    residual_rows = pl.pallas_call(
        residual_kernel,
        out_shape=rows,
        in_specs=[VMEM] * 3,
        out_specs=VMEM,
        compiler_params=roomy(16),
        name="residual",
    )(totals, hpsi_rows, psi_rows)
    return (from_rows(hpsi, owned), from_rows(residual_rows, owned))


def solution(mesh):
    placed = (
        P(("groups", "renv"), None),
        P("groups", None),
        P(("groups", "renv"), None),
        P(("groups", "renv"), None),
        P(("groups", "renv"), None, None),
        P(("groups", "renv"), None, None),
        P(("groups", "renv"), None, None),
        P(("groups", "renv"), None, None),
        P(("groups", "renv")),
        P(("groups", "renv")),
        P(("groups", "renv")),
    )
    return jax.shard_map(
        shards,
        mesh=mesh,
        in_specs=placed,
        out_specs=(P(("groups", "renv"), None), P(("groups", "renv"), None)),
        check_vma=False,
    )
```

```python
import math

import jax
import jax.numpy as jnp
from jax import lax
from jax.experimental import pallas as pl
from jax.experimental.pallas import tpu as pltpu
from jax.sharding import PartitionSpec as P

F32 = jnp.float32
BF16 = jnp.bfloat16
SUB = 8
VMEM = pl.BlockSpec(memory_space=pltpu.VMEM)
SMEM = pl.BlockSpec(memory_space=pltpu.SMEM)
HBM = pl.BlockSpec(memory_space=pltpu.HBM)
MIB = 2**20
LIGHT = pl.CostEstimate(flops=10**6, bytes_accessed=2**16, transcendentals=0)


def as_rows(blocks, sector):
    count = blocks.shape[0]
    split = blocks.reshape(count // SUB, SUB, sector, sector)
    return split.transpose(0, 2, 1, 3).reshape(count * sector, sector)


def from_rows(rows, count):
    sector = rows.shape[1]
    split = rows.reshape(count // SUB, sector, SUB, sector)
    return split.transpose(0, 2, 1, 3).reshape(count, sector * sector)


def pick(ref, block):
    sector = ref.shape[1]
    start = (block // SUB) * (SUB * sector) + block % SUB
    return ref[pl.ds(start, sector, stride=SUB), :]


def halves(mat):
    high = mat.astype(BF16)
    low = (mat - high.astype(F32)).astype(BF16)
    return jnp.concatenate([high, low], axis=1)


def doubled(mat):
    both = halves(mat)
    return jnp.concatenate([both, both], axis=0)


def product(left, right):
    sector = right.shape[1] // 2
    wide = jnp.dot(left, right, preferred_element_type=F32)
    return wide[:, :sector] + wide[:, sector:]


def stacked(mat):
    high = mat.astype(BF16)
    low = (mat - high.astype(F32)).astype(BF16)
    rows = [jnp.concatenate([part, part], axis=1) for part in (high, low)]
    return jnp.concatenate(rows, axis=0)


def product_t(left, right):
    sector = right.shape[0] // 2
    wide = lax.dot_general(left, right, (((1,), (1,)), ((), ())), preferred_element_type=F32)
    return wide[:, :sector] + wide[:, sector:]


def twice(part):
    return jnp.concatenate([part, part], axis=0)


def roomy(mib):
    return pltpu.CompilerParams(vmem_limit_bytes=mib * MIB)


def member(position, peers):
    bits = peers.bit_length() - 1
    if peers != 1 << bits:
        return position
    return sum(((position >> k) & 1) << (bits - 1 - k) for k in range(bits))


def gather_kernel(block_ref, left_ref, live_ref, psi_rows, out_hbm, stage, sems):
    slots, terms, peers = left_ref.shape
    sector = psi_rows.shape[1]
    lane = lax.broadcasted_iota(jnp.int32, (SUB, sector), 1)
    puts = []
    for i in range(stage.shape[0]):
        slot, peer = i % slots, member(i // slots, peers)
        stage[i, :sector] = pick(psi_rows, block_ref[peer * slots + slot])
        values = jnp.zeros(lane.shape, jnp.int32)
        for g in range(terms):
            values = jnp.where(lane == g, left_ref[slot, g, peer], values)
            values = jnp.where(lane == terms + g, live_ref[slot, g, peer], values)
        stage[i, sector:] = values.astype(F32)
        put = pltpu.make_async_copy(stage.at[i], out_hbm.at[i], sems.at[i])
        put.start()
        puts.append(put)
    for put in puts:
        put.wait()


def prepare_kernel(
    sent_hbm,
    rindex_ref,
    out_index_ref,
    block_ref,
    left_ref,
    right_ref,
    psi_rows,
    right_rows,
    left_rows,
    turned_ref,
    parts_ref,
    near_ref,
    psis_ref,
    stacks_ref,
    moved_ref,
):
    slots, terms, peers = rindex_ref.shape
    sector = psi_rows.shape[1]

    rights = right_rows.shape[0] // sector
    lefts = left_rows.shape[0] // sector

    def split_right(i, carry):
        mat = pick(right_rows, i)
        parts_ref[lefts + i] = halves(mat)
        stacks_ref[i] = stacked(mat)
        return carry

    lax.fori_loop(0, rights, split_right, 0, unroll=4)

    def split_psi(i, carry):
        psis_ref[i] = halves(pick(psi_rows, i))
        return carry

    lax.fori_loop(0, psis_ref.shape[0], split_psi, 0, unroll=4)

    def turn(i, carry):
        slot, peer = i % slots, member(i // slots, peers)
        for g in range(terms):
            right = stacks_ref[rindex_ref[slot, g, peer]]
            psi = psis_ref[out_index_ref[slot, g, peer]]
            turned_ref[i, g * sector : (g + 1) * sector] = product_t(psi, right)
        turned_ref[i, terms * sector :] = jnp.zeros((SUB, sector), F32)
        return carry

    slabs = near_ref.shape[0] // terms
    senders = turned_ref.shape[0] - slabs
    lax.fori_loop(0, senders, turn, 0, unroll=4)

    def split_left(i, carry):
        parts_ref[i] = halves(pick(left_rows, i))
        return carry

    lax.fori_loop(0, lefts, split_left, 0, unroll=8)

    def left_step(k, carry):
        moved_ref[k] = halves(product(parts_ref[left_ref[k]], twice(psis_ref[block_ref[k]])))
        return carry

    lax.fori_loop(0, block_ref.shape[0], left_step, 0, unroll=8)
    near_ref[...] = jnp.zeros_like(near_ref)

    def right_step(k, carry):
        near_ref[block_ref[k]] += product(moved_ref[k], twice(parts_ref[lefts + right_ref[k]]))
        return carry

    lax.fori_loop(0, block_ref.shape[0], right_step, 0, unroll=8)
    corr = jnp.zeros((1, sector), F32)
    norm = jnp.zeros((1, sector), F32)
    for b in range(near_ref.shape[0]):
        mat = pick(psi_rows, b)
        turned_ref[senders + b // terms, (b % terms) * sector : (b % terms + 1) * sector] = near_ref[b]
        corr += jnp.sum(mat * near_ref[b], axis=0, keepdims=True)
        norm += jnp.sum(mat * mat, axis=0, keepdims=True)
    row = lax.broadcasted_iota(jnp.int32, (SUB, sector), 0)
    turned_ref[0, terms * sector :] = jnp.where(row == 0, corr, jnp.where(row == 1, norm, 0.0))


def arrive_kernel(terms, came_ref, turned_hbm, parts_hbm, moved_ref, sums_ref, marks, turned_ref, lefts_ref, weights_ref, sems):
    count, height, sector = came_ref.shape
    get_marks = pltpu.make_async_copy(came_ref.at[:, pl.ds(sector, height - sector)], marks, sems.at[0])
    get_lefts = pltpu.make_async_copy(parts_hbm.at[pl.ds(0, lefts_ref.shape[0])], lefts_ref, sems.at[1])
    quarter = count // math.gcd(count, 4)
    spans = [pl.ds(first, quarter) for first in range(0, count, quarter)]
    get_turned = [
        pltpu.make_async_copy(turned_hbm.at[span], turned_ref.at[span], sems.at[2 + k]) for k, span in enumerate(spans)
    ]
    for copy in (get_marks, get_lefts, *get_turned):
        copy.start()

    def split(i, carry):
        weights_ref[i] = doubled(came_ref[i, :sector])
        return carry

    lax.fori_loop(0, count, split, 0, unroll=4)
    get_marks.wait()
    get_lefts.wait()

    def block(i, total):
        stack = [lefts_ref[marks[i, 0, g].astype(jnp.int32)] for g in range(terms)]
        moved = product(jnp.concatenate(stack, axis=0), weights_ref[i])
        for g in range(terms):
            part = slice(g * sector, (g + 1) * sector)
            one = moved[part] * marks[i, 0, terms + g]
            moved_ref[i, part] = halves(one)
            total += jnp.sum((one * turned_ref[i, part]).reshape(-1, SUB, sector), axis=0)
        return total

    total = jnp.zeros((SUB, sector), F32)
    for k, copy in enumerate(get_turned):
        copy.wait()
        total = lax.fori_loop(k * quarter, (k + 1) * quarter, block, total, unroll=4)
    corr = jnp.sum(total, axis=0, keepdims=True)
    row = lax.broadcasted_iota(jnp.int32, total.shape, 0)
    mine = turned_ref[0, terms * sector :] + jnp.where(row == 0, corr, 0.0)
    folded = mine + pltpu.roll(mine, sector // 2, 1)
    lane = lax.broadcasted_iota(jnp.int32, (1, sector), 1)
    shared = jnp.where(lane < sector // 2, folded[0:1], folded[1:2])
    for i in range(sums_ref.shape[0]):
        sums_ref[i] = shared


def remote_kernel(rindex_ref, out_index_ref, moved_ref, turned_hbm, parts_hbm, hpsi_rows, hpsi_hbm, acc, near_ref, rights_ref, sems):
    slots, terms, peers = rindex_ref.shape
    senders, height, _ = moved_ref.shape
    sector = height // terms
    rights = rights_ref.shape[0]
    get_rights = pltpu.make_async_copy(parts_hbm.at[pl.ds(parts_hbm.shape[0] - rights, rights)], rights_ref, sems.at[0])
    get_rights.start()
    slabs = []
    for k in range(acc.shape[0] // height):
        near = turned_hbm.at[senders + k, pl.ds(0, height)]
        slabs.append(pltpu.make_async_copy(near, near_ref.at[pl.ds(k * height, height)], sems.at[1 + k]))
        slabs[k].start()
    acc[...] = jnp.zeros_like(acc)
    get_rights.wait()

    def right_step(i, carry):
        slot, peer = i % slots, member(i // slots, peers)
        for g in range(terms):
            right = rights_ref[rindex_ref[slot, g, peer]]
            spot = pl.multiple_of(out_index_ref[slot, g, peer] * sector, sector)
            acc[pl.ds(spot, sector)] += product(moved_ref[i, g * sector : (g + 1) * sector], twice(right))
        return carry

    lax.fori_loop(0, senders, right_step, 0, unroll=4)
    for copy in slabs:
        copy.wait()
    for b in range(acc.shape[0] // sector):
        start = (b // SUB) * (SUB * sector) + b % SUB
        part = slice(b * sector, (b + 1) * sector)
        hpsi_rows[pl.ds(start, sector, stride=SUB), :] = acc[part] + near_ref[part]
    put = pltpu.make_async_copy(hpsi_rows, hpsi_hbm, sems.at[0])
    put.start()
    put.wait()


def residual_kernel(sums_ref, hpsi_rows, psi_rows, out_ref):
    total = jnp.sum(sums_ref[...], axis=0)
    lane = lax.broadcasted_iota(jnp.int32, total.shape, 1)
    first = lane < total.shape[1] // 2
    corr = jnp.sum(jnp.where(first, total, 0.0), axis=1, keepdims=True)
    norm = jnp.sum(jnp.where(first, 0.0, total), axis=1, keepdims=True)
    theta = corr / (norm + 1e-06)
    out_ref[...] = hpsi_rows[...] - theta * psi_rows[...]


def shards(
    psi,
    left_env,
    right_env,
    send_block,
    send_left,
    send_live,
    recv_right,
    recv_out,
    loc_block,
    loc_left,
    loc_right,
):
    peers = lax.axis_size("renv")
    owned = psi.shape[0]
    sector = math.isqrt(psi.shape[1])
    slots = send_block.shape[1]
    terms = send_left.shape[2]
    count = peers * slots
    lefts = left_env.shape[0]
    rights = right_env.shape[0]
    height = sector + SUB
    psi_rows = as_rows(psi, sector)
    left_rows = as_rows(left_env, sector)
    right_rows = as_rows(right_env, sector)
    by_slot = [index.transpose(1, 2, 0) for index in (send_left, send_live, recv_right, recv_out)]
    blocks = jax.ShapeDtypeStruct((count, height, sector), F32)
    rows = jax.ShapeDtypeStruct((owned * sector, sector), F32)

    sent = pl.pallas_call(
        gather_kernel,
        out_shape=blocks,
        in_specs=[SMEM] * 3 + [VMEM],
        out_specs=HBM,
        scratch_shapes=[pltpu.VMEM(blocks.shape, F32), pltpu.SemaphoreType.DMA((count,))],
        compiler_params=roomy(56),
        name="gather_blocks",
    )(send_block.reshape(-1), *by_slot[:2], psi_rows)
    came = lax.all_to_all(
        sent.reshape(peers, slots, height, sector),
        "renv",
        split_axis=0,
        concat_axis=0,
        tiled=True,
        axis_index_groups=[[member(position, peers) for position in range(peers)]],
    )
    came = came.reshape(count, height, sector)

    slabs = owned // terms
    turned, parts = pl.pallas_call(
        prepare_kernel,
        out_shape=(
            jax.ShapeDtypeStruct((count + slabs, terms * sector + SUB, sector), F32),
            jax.ShapeDtypeStruct((lefts + rights, sector, 2 * sector), BF16),
        ),
        in_specs=[HBM] + [SMEM] * 5 + [VMEM] * 3,
        out_specs=(VMEM,) * 2,
        scratch_shapes=[
            pltpu.VMEM((owned, sector, sector), F32),
            pltpu.VMEM((owned, sector, 2 * sector), BF16),
            pltpu.VMEM((rights, 2 * sector, 2 * sector), BF16),
            pltpu.VMEM((loc_block.shape[0], sector, 2 * sector), BF16),
        ],
        compiler_params=roomy(56),
        cost_estimate=LIGHT,
        name="prepare",
    )(sent, *by_slot[2:], loc_block, loc_left, loc_right, psi_rows, right_rows, left_rows)

    chunk = math.gcd(count, 16)
    moved = []
    sums = 0.0
    for first in range(0, count, chunk):
        part = slice(first, first + chunk) if count > chunk else slice(None)
        kept, share = pl.pallas_call(
            lambda *refs: arrive_kernel(terms, *refs),
            out_shape=(
                jax.ShapeDtypeStruct((chunk, terms * sector, 2 * sector), BF16),
                jax.ShapeDtypeStruct((peers, 1, sector), F32),
            ),
            in_specs=[VMEM] + [HBM] * 2,
            out_specs=(VMEM,) * 2,
            scratch_shapes=[
                pltpu.SMEM((chunk, SUB, sector), F32),
                pltpu.VMEM((chunk, terms * sector + SUB, sector), F32),
                pltpu.VMEM((lefts, sector, 2 * sector), BF16),
                pltpu.VMEM((chunk, 2 * sector, 2 * sector), BF16),
                pltpu.SemaphoreType.DMA((6,)),
            ],
            compiler_params=roomy(50),
            name="arrive",
        )(came[part], turned if count == chunk else turned[part], parts)
        moved.append(kept)
        sums = share if count == chunk else sums + share
    moved = moved[0] if len(moved) == 1 else jnp.concatenate(moved, axis=0)
    totals = lax.all_to_all(sums, "renv", split_axis=0, concat_axis=0, tiled=True)

    hpsi_rows, hpsi = pl.pallas_call(
        remote_kernel,
        out_shape=(rows, rows),
        in_specs=[SMEM] * 2 + [VMEM] + [HBM] * 2,
        out_specs=(VMEM, HBM),
        scratch_shapes=[
            pltpu.VMEM(rows.shape, F32),
            pltpu.VMEM(rows.shape, F32),
            pltpu.VMEM((rights, sector, 2 * sector), BF16),
            pltpu.SemaphoreType.DMA((1 + slabs,)),
        ],
        compiler_params=roomy(50),
        cost_estimate=pl.CostEstimate(flops=4 * 10**9, bytes_accessed=6 * MIB, transcendentals=0),
        name="remote_terms",
    )(*by_slot[2:], moved, turned, parts)

    residual_rows = pl.pallas_call(
        residual_kernel,
        out_shape=rows,
        in_specs=[VMEM] * 3,
        out_specs=VMEM,
        compiler_params=roomy(16),
        name="residual",
    )(totals, hpsi_rows, psi_rows)
    return (from_rows(hpsi, owned), from_rows(residual_rows, owned))


def solution(mesh):
    placed = (
        P(("groups", "renv"), None),
        P("groups", None),
        P(("groups", "renv"), None),
        P(("groups", "renv"), None),
        P(("groups", "renv"), None, None),
        P(("groups", "renv"), None, None),
        P(("groups", "renv"), None, None),
        P(("groups", "renv"), None, None),
        P(("groups", "renv")),
        P(("groups", "renv")),
        P(("groups", "renv")),
    )
    return jax.shard_map(
        shards,
        mesh=mesh,
        in_specs=placed,
        out_specs=(P(("groups", "renv"), None), P(("groups", "renv"), None)),
        check_vma=False,
    )
```

```python
import math

import jax
import jax.numpy as jnp
from jax import lax
from jax.experimental import pallas as pl
from jax.experimental.pallas import tpu as pltpu
from jax.sharding import PartitionSpec as P

F32 = jnp.float32
BF16 = jnp.bfloat16
SUB = 8
VMEM = pl.BlockSpec(memory_space=pltpu.VMEM)
SMEM = pl.BlockSpec(memory_space=pltpu.SMEM)
HBM = pl.BlockSpec(memory_space=pltpu.HBM)
MIB = 2**20
LIGHT = pl.CostEstimate(flops=10**6, bytes_accessed=2**16, transcendentals=0)


def as_rows(blocks, sector):
    count = blocks.shape[0]
    split = blocks.reshape(count // SUB, SUB, sector, sector)
    return split.transpose(0, 2, 1, 3).reshape(count * sector, sector)


def from_rows(rows, count):
    sector = rows.shape[1]
    split = rows.reshape(count // SUB, sector, SUB, sector)
    return split.transpose(0, 2, 1, 3).reshape(count, sector * sector)


def pick(ref, block):
    sector = ref.shape[1]
    start = (block // SUB) * (SUB * sector) + block % SUB
    return ref[pl.ds(start, sector, stride=SUB), :]


def halves(mat):
    high = mat.astype(BF16)
    low = (mat - high.astype(F32)).astype(BF16)
    return jnp.concatenate([high, low], axis=1)


def doubled(mat):
    both = halves(mat)
    return jnp.concatenate([both, both], axis=0)


def product(left, right):
    sector = right.shape[1] // 2
    wide = jnp.dot(left, right, preferred_element_type=F32)
    return wide[:, :sector] + wide[:, sector:]


def stacked(mat):
    high = mat.astype(BF16)
    low = (mat - high.astype(F32)).astype(BF16)
    rows = [jnp.concatenate([part, part], axis=1) for part in (high, low)]
    return jnp.concatenate(rows, axis=0)


def product_t(left, right):
    sector = right.shape[0] // 2
    wide = lax.dot_general(left, right, (((1,), (1,)), ((), ())), preferred_element_type=F32)
    return wide[:, :sector] + wide[:, sector:]


def twice(part):
    return jnp.concatenate([part, part], axis=0)


def roomy(mib):
    return pltpu.CompilerParams(vmem_limit_bytes=mib * MIB)


def member(position, peers):
    quarter = peers // 4
    if peers % 4:
        return position
    part = position // quarter
    return position + quarter * (2 * (part == 1) - (part == 2) - (part == 3))


def gather_kernel(block_ref, left_ref, live_ref, psi_rows, out_hbm, stage, sems):
    slots, terms, peers = left_ref.shape
    sector = psi_rows.shape[1]
    lane = lax.broadcasted_iota(jnp.int32, (SUB, sector), 1)
    puts = []
    for i in range(stage.shape[0]):
        slot, peer = i % slots, member(i // slots, peers)
        stage[i, :sector] = pick(psi_rows, block_ref[peer * slots + slot])
        values = jnp.zeros(lane.shape, jnp.int32)
        for g in range(terms):
            values = jnp.where(lane == g, left_ref[slot, g, peer], values)
            values = jnp.where(lane == terms + g, live_ref[slot, g, peer], values)
        stage[i, sector:] = values.astype(F32)
        put = pltpu.make_async_copy(stage.at[i], out_hbm.at[i], sems.at[i])
        put.start()
        puts.append(put)
    for put in puts:
        put.wait()


def prepare_kernel(
    sent_hbm,
    rindex_ref,
    out_index_ref,
    block_ref,
    left_ref,
    right_ref,
    psi_rows,
    right_rows,
    left_rows,
    turned_ref,
    parts_ref,
    near_ref,
    psis_ref,
    stacks_ref,
    moved_ref,
):
    slots, terms, peers = rindex_ref.shape
    sector = psi_rows.shape[1]

    rights = right_rows.shape[0] // sector
    lefts = left_rows.shape[0] // sector

    def split_right(i, carry):
        mat = pick(right_rows, i)
        parts_ref[lefts + i] = halves(mat)
        stacks_ref[i] = stacked(mat)
        return carry

    lax.fori_loop(0, rights, split_right, 0, unroll=4)

    def split_psi(i, carry):
        psis_ref[i] = halves(pick(psi_rows, i))
        return carry

    lax.fori_loop(0, psis_ref.shape[0], split_psi, 0, unroll=4)

    def turn(i, carry):
        slot, peer = i % slots, member(i // slots, peers)
        for g in range(terms):
            right = stacks_ref[rindex_ref[slot, g, peer]]
            psi = psis_ref[out_index_ref[slot, g, peer]]
            turned_ref[i, g * sector : (g + 1) * sector] = product_t(psi, right)
        turned_ref[i, terms * sector :] = jnp.zeros((SUB, sector), F32)
        return carry

    slabs = near_ref.shape[0] // terms
    senders = turned_ref.shape[0] - slabs
    lax.fori_loop(0, senders, turn, 0, unroll=4)

    def split_left(i, carry):
        parts_ref[i] = halves(pick(left_rows, i))
        return carry

    lax.fori_loop(0, lefts, split_left, 0, unroll=8)

    def left_step(k, carry):
        moved_ref[k] = halves(product(parts_ref[left_ref[k]], twice(psis_ref[block_ref[k]])))
        return carry

    lax.fori_loop(0, block_ref.shape[0], left_step, 0, unroll=8)
    near_ref[...] = jnp.zeros_like(near_ref)

    def right_step(k, carry):
        near_ref[block_ref[k]] += product(moved_ref[k], twice(parts_ref[lefts + right_ref[k]]))
        return carry

    lax.fori_loop(0, block_ref.shape[0], right_step, 0, unroll=8)
    corr = jnp.zeros((1, sector), F32)
    norm = jnp.zeros((1, sector), F32)
    for b in range(near_ref.shape[0]):
        mat = pick(psi_rows, b)
        turned_ref[senders + b // terms, (b % terms) * sector : (b % terms + 1) * sector] = near_ref[b]
        corr += jnp.sum(mat * near_ref[b], axis=0, keepdims=True)
        norm += jnp.sum(mat * mat, axis=0, keepdims=True)
    row = lax.broadcasted_iota(jnp.int32, (SUB, sector), 0)
    turned_ref[0, terms * sector :] = jnp.where(row == 0, corr, jnp.where(row == 1, norm, 0.0))


def arrive_kernel(terms, came_ref, turned_hbm, parts_hbm, moved_ref, sums_ref, marks, turned_ref, lefts_ref, weights_ref, sems):
    count, height, sector = came_ref.shape
    get_marks = pltpu.make_async_copy(came_ref.at[:, pl.ds(sector, height - sector)], marks, sems.at[0])
    get_lefts = pltpu.make_async_copy(parts_hbm.at[pl.ds(0, lefts_ref.shape[0])], lefts_ref, sems.at[1])
    quarter = count // math.gcd(count, 4)
    spans = [pl.ds(first, quarter) for first in range(0, count, quarter)]
    get_turned = [
        pltpu.make_async_copy(turned_hbm.at[span], turned_ref.at[span], sems.at[2 + k]) for k, span in enumerate(spans)
    ]
    for copy in (get_marks, get_lefts, *get_turned):
        copy.start()

    def split(i, carry):
        weights_ref[i] = doubled(came_ref[i, :sector])
        return carry

    lax.fori_loop(0, count, split, 0, unroll=4)
    get_marks.wait()
    get_lefts.wait()

    def block(i, total):
        stack = [lefts_ref[marks[i, 0, g].astype(jnp.int32)] for g in range(terms)]
        moved = product(jnp.concatenate(stack, axis=0), weights_ref[i])
        for g in range(terms):
            part = slice(g * sector, (g + 1) * sector)
            one = moved[part] * marks[i, 0, terms + g]
            moved_ref[i, part] = halves(one)
            total += jnp.sum((one * turned_ref[i, part]).reshape(-1, SUB, sector), axis=0)
        return total

    total = jnp.zeros((SUB, sector), F32)
    for k, copy in enumerate(get_turned):
        copy.wait()
        total = lax.fori_loop(k * quarter, (k + 1) * quarter, block, total, unroll=4)
    corr = jnp.sum(total, axis=0, keepdims=True)
    row = lax.broadcasted_iota(jnp.int32, total.shape, 0)
    mine = turned_ref[0, terms * sector :] + jnp.where(row == 0, corr, 0.0)
    folded = mine + pltpu.roll(mine, sector // 2, 1)
    lane = lax.broadcasted_iota(jnp.int32, (1, sector), 1)
    shared = jnp.where(lane < sector // 2, folded[0:1], folded[1:2])
    for i in range(sums_ref.shape[0]):
        sums_ref[i] = shared


def remote_kernel(rindex_ref, out_index_ref, moved_ref, turned_hbm, parts_hbm, hpsi_rows, hpsi_hbm, acc, near_ref, rights_ref, sems):
    slots, terms, peers = rindex_ref.shape
    senders, height, _ = moved_ref.shape
    sector = height // terms
    rights = rights_ref.shape[0]
    get_rights = pltpu.make_async_copy(parts_hbm.at[pl.ds(parts_hbm.shape[0] - rights, rights)], rights_ref, sems.at[0])
    get_rights.start()
    slabs = []
    for k in range(acc.shape[0] // height):
        near = turned_hbm.at[senders + k, pl.ds(0, height)]
        slabs.append(pltpu.make_async_copy(near, near_ref.at[pl.ds(k * height, height)], sems.at[1 + k]))
        slabs[k].start()
    acc[...] = jnp.zeros_like(acc)
    get_rights.wait()

    def right_step(i, carry):
        slot, peer = i % slots, member(i // slots, peers)
        for g in range(terms):
            right = rights_ref[rindex_ref[slot, g, peer]]
            spot = pl.multiple_of(out_index_ref[slot, g, peer] * sector, sector)
            acc[pl.ds(spot, sector)] += product(moved_ref[i, g * sector : (g + 1) * sector], twice(right))
        return carry

    lax.fori_loop(0, senders, right_step, 0, unroll=4)
    for copy in slabs:
        copy.wait()
    for b in range(acc.shape[0] // sector):
        start = (b // SUB) * (SUB * sector) + b % SUB
        part = slice(b * sector, (b + 1) * sector)
        hpsi_rows[pl.ds(start, sector, stride=SUB), :] = acc[part] + near_ref[part]
    put = pltpu.make_async_copy(hpsi_rows, hpsi_hbm, sems.at[0])
    put.start()
    put.wait()


def residual_kernel(sums_ref, hpsi_rows, psi_rows, out_ref):
    total = jnp.sum(sums_ref[...], axis=0)
    lane = lax.broadcasted_iota(jnp.int32, total.shape, 1)
    first = lane < total.shape[1] // 2
    corr = jnp.sum(jnp.where(first, total, 0.0), axis=1, keepdims=True)
    norm = jnp.sum(jnp.where(first, 0.0, total), axis=1, keepdims=True)
    theta = corr / (norm + 1e-06)
    out_ref[...] = hpsi_rows[...] - theta * psi_rows[...]


def shards(
    psi,
    left_env,
    right_env,
    send_block,
    send_left,
    send_live,
    recv_right,
    recv_out,
    loc_block,
    loc_left,
    loc_right,
):
    peers = lax.axis_size("renv")
    owned = psi.shape[0]
    sector = math.isqrt(psi.shape[1])
    slots = send_block.shape[1]
    terms = send_left.shape[2]
    count = peers * slots
    lefts = left_env.shape[0]
    rights = right_env.shape[0]
    height = sector + SUB
    psi_rows = as_rows(psi, sector)
    left_rows = as_rows(left_env, sector)
    right_rows = as_rows(right_env, sector)
    by_slot = [index.transpose(1, 2, 0) for index in (send_left, send_live, recv_right, recv_out)]
    blocks = jax.ShapeDtypeStruct((count, height, sector), F32)
    rows = jax.ShapeDtypeStruct((owned * sector, sector), F32)

    sent = pl.pallas_call(
        gather_kernel,
        out_shape=blocks,
        in_specs=[SMEM] * 3 + [VMEM],
        out_specs=HBM,
        scratch_shapes=[pltpu.VMEM(blocks.shape, F32), pltpu.SemaphoreType.DMA((count,))],
        compiler_params=roomy(56),
        name="gather_blocks",
    )(send_block.reshape(-1), *by_slot[:2], psi_rows)
    came = lax.all_to_all(
        sent.reshape(peers, slots, height, sector),
        "renv",
        split_axis=0,
        concat_axis=0,
        tiled=True,
        axis_index_groups=[[member(position, peers) for position in range(peers)]],
    )
    came = came.reshape(count, height, sector)

    slabs = owned // terms
    turned, parts = pl.pallas_call(
        prepare_kernel,
        out_shape=(
            jax.ShapeDtypeStruct((count + slabs, terms * sector + SUB, sector), F32),
            jax.ShapeDtypeStruct((lefts + rights, sector, 2 * sector), BF16),
        ),
        in_specs=[HBM] + [SMEM] * 5 + [VMEM] * 3,
        out_specs=(VMEM,) * 2,
        scratch_shapes=[
            pltpu.VMEM((owned, sector, sector), F32),
            pltpu.VMEM((owned, sector, 2 * sector), BF16),
            pltpu.VMEM((rights, 2 * sector, 2 * sector), BF16),
            pltpu.VMEM((loc_block.shape[0], sector, 2 * sector), BF16),
        ],
        compiler_params=roomy(56),
        cost_estimate=LIGHT,
        name="prepare",
    )(sent, *by_slot[2:], loc_block, loc_left, loc_right, psi_rows, right_rows, left_rows)

    chunk = math.gcd(count, 16)
    moved = []
    sums = 0.0
    for first in range(0, count, chunk):
        part = slice(first, first + chunk) if count > chunk else slice(None)
        kept, share = pl.pallas_call(
            lambda *refs: arrive_kernel(terms, *refs),
            out_shape=(
                jax.ShapeDtypeStruct((chunk, terms * sector, 2 * sector), BF16),
                jax.ShapeDtypeStruct((peers, 1, sector), F32),
            ),
            in_specs=[VMEM] + [HBM] * 2,
            out_specs=(VMEM,) * 2,
            scratch_shapes=[
                pltpu.SMEM((chunk, SUB, sector), F32),
                pltpu.VMEM((chunk, terms * sector + SUB, sector), F32),
                pltpu.VMEM((lefts, sector, 2 * sector), BF16),
                pltpu.VMEM((chunk, 2 * sector, 2 * sector), BF16),
                pltpu.SemaphoreType.DMA((6,)),
            ],
            compiler_params=roomy(50),
            name="arrive",
        )(came[part], turned if count == chunk else turned[part], parts)
        moved.append(kept)
        sums = share if count == chunk else sums + share
    moved = moved[0] if len(moved) == 1 else jnp.concatenate(moved, axis=0)
    totals = lax.all_to_all(sums, "renv", split_axis=0, concat_axis=0, tiled=True)

    hpsi_rows, hpsi = pl.pallas_call(
        remote_kernel,
        out_shape=(rows, rows),
        in_specs=[SMEM] * 2 + [VMEM] + [HBM] * 2,
        out_specs=(VMEM, HBM),
        scratch_shapes=[
            pltpu.VMEM(rows.shape, F32),
            pltpu.VMEM(rows.shape, F32),
            pltpu.VMEM((rights, sector, 2 * sector), BF16),
            pltpu.SemaphoreType.DMA((1 + slabs,)),
        ],
        compiler_params=roomy(50),
        cost_estimate=pl.CostEstimate(flops=4 * 10**9, bytes_accessed=6 * MIB, transcendentals=0),
        name="remote_terms",
    )(*by_slot[2:], moved, turned, parts)

    residual_rows = pl.pallas_call(
        residual_kernel,
        out_shape=rows,
        in_specs=[VMEM] * 3,
        out_specs=VMEM,
        compiler_params=roomy(16),
        name="residual",
    )(totals, hpsi_rows, psi_rows)
    return (from_rows(hpsi, owned), from_rows(residual_rows, owned))


def solution(mesh):
    placed = (
        P(("groups", "renv"), None),
        P("groups", None),
        P(("groups", "renv"), None),
        P(("groups", "renv"), None),
        P(("groups", "renv"), None, None),
        P(("groups", "renv"), None, None),
        P(("groups", "renv"), None, None),
        P(("groups", "renv"), None, None),
        P(("groups", "renv")),
        P(("groups", "renv")),
        P(("groups", "renv")),
    )
    return jax.shard_map(
        shards,
        mesh=mesh,
        in_specs=placed,
        out_specs=(P(("groups", "renv"), None), P(("groups", "renv"), None)),
        check_vma=False,
    )
```

```python
import math

import jax
import jax.numpy as jnp
from jax import lax
from jax.experimental import pallas as pl
from jax.experimental.pallas import tpu as pltpu
from jax.sharding import PartitionSpec as P

F32 = jnp.float32
BF16 = jnp.bfloat16
SUB = 8
VMEM = pl.BlockSpec(memory_space=pltpu.VMEM)
SMEM = pl.BlockSpec(memory_space=pltpu.SMEM)
HBM = pl.BlockSpec(memory_space=pltpu.HBM)
MIB = 2**20
LIGHT = pl.CostEstimate(flops=10**6, bytes_accessed=2**16, transcendentals=0)


def as_rows(blocks, sector):
    count = blocks.shape[0]
    split = blocks.reshape(count // SUB, SUB, sector, sector)
    return split.transpose(0, 2, 1, 3).reshape(count * sector, sector)


def from_rows(rows, count):
    sector = rows.shape[1]
    split = rows.reshape(count // SUB, sector, SUB, sector)
    return split.transpose(0, 2, 1, 3).reshape(count, sector * sector)


def pick(ref, block):
    sector = ref.shape[1]
    start = (block // SUB) * (SUB * sector) + block % SUB
    return ref[pl.ds(start, sector, stride=SUB), :]


def halves(mat):
    high = mat.astype(BF16)
    low = (mat - high.astype(F32)).astype(BF16)
    return jnp.concatenate([high, low], axis=1)


def doubled(mat):
    both = halves(mat)
    return jnp.concatenate([both, both], axis=0)


def product(left, right):
    sector = right.shape[1] // 2
    wide = jnp.dot(left, right, preferred_element_type=F32)
    return wide[:, :sector] + wide[:, sector:]


def stacked(mat):
    high = mat.astype(BF16)
    low = (mat - high.astype(F32)).astype(BF16)
    rows = [jnp.concatenate([part, part], axis=1) for part in (high, low)]
    return jnp.concatenate(rows, axis=0)


def product_t(left, right):
    sector = right.shape[0] // 2
    wide = lax.dot_general(left, right, (((1,), (1,)), ((), ())), preferred_element_type=F32)
    return wide[:, :sector] + wide[:, sector:]


def twice(part):
    return jnp.concatenate([part, part], axis=0)


def roomy(mib):
    return pltpu.CompilerParams(vmem_limit_bytes=mib * MIB)


def gather_kernel(block_ref, left_ref, live_ref, psi_rows, out_hbm, stage, sems):
    slots, terms, _ = left_ref.shape
    sector = psi_rows.shape[1]
    lane = lax.broadcasted_iota(jnp.int32, (SUB, sector), 1)
    puts = []
    for i in range(stage.shape[0]):
        stage[i, :sector] = pick(psi_rows, block_ref[i])
        values = jnp.zeros(lane.shape, jnp.int32)
        for g in range(terms):
            values = jnp.where(lane == g, left_ref[i % slots, g, i // slots], values)
            values = jnp.where(lane == terms + g, live_ref[i % slots, g, i // slots], values)
        stage[i, sector:] = values.astype(F32)
        put = pltpu.make_async_copy(stage.at[i], out_hbm.at[i], sems.at[i])
        put.start()
        puts.append(put)
    for put in puts:
        put.wait()


def prepare_kernel(
    sent_hbm,
    rindex_ref,
    out_index_ref,
    block_ref,
    left_ref,
    right_ref,
    psi_rows,
    right_rows,
    left_rows,
    turned_ref,
    parts_ref,
    near_ref,
    psis_ref,
    stacks_ref,
    moved_ref,
):
    slots, terms, _ = rindex_ref.shape
    sector = psi_rows.shape[1]

    rights = right_rows.shape[0] // sector
    lefts = left_rows.shape[0] // sector

    def split_right(i, carry):
        mat = pick(right_rows, i)
        parts_ref[lefts + i] = halves(mat)
        stacks_ref[i] = stacked(mat)
        return carry

    lax.fori_loop(0, rights, split_right, 0, unroll=4)

    def split_psi(i, carry):
        psis_ref[i] = halves(pick(psi_rows, i))
        return carry

    lax.fori_loop(0, psis_ref.shape[0], split_psi, 0, unroll=4)

    def turn(i, carry):
        for g in range(terms):
            right = stacks_ref[rindex_ref[i % slots, g, i // slots]]
            psi = psis_ref[out_index_ref[i % slots, g, i // slots]]
            turned_ref[i, g * sector : (g + 1) * sector] = product_t(psi, right)
        turned_ref[i, terms * sector :] = jnp.zeros((SUB, sector), F32)
        return carry

    slabs = near_ref.shape[0] // terms
    senders = turned_ref.shape[0] - slabs
    lax.fori_loop(0, senders, turn, 0, unroll=4)

    def split_left(i, carry):
        parts_ref[i] = halves(pick(left_rows, i))
        return carry

    lax.fori_loop(0, lefts, split_left, 0, unroll=8)

    def left_step(k, carry):
        moved_ref[k] = halves(product(parts_ref[left_ref[k]], twice(psis_ref[block_ref[k]])))
        return carry

    lax.fori_loop(0, block_ref.shape[0], left_step, 0, unroll=8)
    near_ref[...] = jnp.zeros_like(near_ref)

    def right_step(k, carry):
        near_ref[block_ref[k]] += product(moved_ref[k], twice(parts_ref[lefts + right_ref[k]]))
        return carry

    lax.fori_loop(0, block_ref.shape[0], right_step, 0, unroll=8)
    corr = jnp.zeros((1, sector), F32)
    norm = jnp.zeros((1, sector), F32)
    for b in range(near_ref.shape[0]):
        mat = pick(psi_rows, b)
        turned_ref[senders + b // terms, (b % terms) * sector : (b % terms + 1) * sector] = near_ref[b]
        corr += jnp.sum(mat * near_ref[b], axis=0, keepdims=True)
        norm += jnp.sum(mat * mat, axis=0, keepdims=True)
    row = lax.broadcasted_iota(jnp.int32, (SUB, sector), 0)
    turned_ref[0, terms * sector :] = jnp.where(row == 0, corr, jnp.where(row == 1, norm, 0.0))


def arrive_kernel(terms, came_ref, turned_hbm, parts_hbm, moved_ref, sums_ref, marks, turned_ref, lefts_ref, weights_ref, sems):
    count, height, sector = came_ref.shape
    get_marks = pltpu.make_async_copy(came_ref.at[:, pl.ds(sector, height - sector)], marks, sems.at[0])
    get_lefts = pltpu.make_async_copy(parts_hbm.at[pl.ds(0, lefts_ref.shape[0])], lefts_ref, sems.at[1])
    quarter = count // math.gcd(count, 4)
    spans = [pl.ds(first, quarter) for first in range(0, count, quarter)]
    get_turned = [
        pltpu.make_async_copy(turned_hbm.at[span], turned_ref.at[span], sems.at[2 + k]) for k, span in enumerate(spans)
    ]
    for copy in (get_marks, get_lefts, *get_turned):
        copy.start()

    def split(i, carry):
        weights_ref[i] = doubled(came_ref[i, :sector])
        return carry

    lax.fori_loop(0, count, split, 0, unroll=4)
    get_marks.wait()
    get_lefts.wait()

    def block(i, total):
        stack = [lefts_ref[marks[i, 0, g].astype(jnp.int32)] for g in range(terms)]
        moved = product(jnp.concatenate(stack, axis=0), weights_ref[i])
        for g in range(terms):
            part = slice(g * sector, (g + 1) * sector)
            one = moved[part] * marks[i, 0, terms + g]
            moved_ref[i, part] = halves(one)
            total += jnp.sum((one * turned_ref[i, part]).reshape(-1, SUB, sector), axis=0)
        return total

    total = jnp.zeros((SUB, sector), F32)
    for k, copy in enumerate(get_turned):
        copy.wait()
        total = lax.fori_loop(k * quarter, (k + 1) * quarter, block, total, unroll=4)
    corr = jnp.sum(total, axis=0, keepdims=True)
    row = lax.broadcasted_iota(jnp.int32, total.shape, 0)
    mine = turned_ref[0, terms * sector :] + jnp.where(row == 0, corr, 0.0)
    folded = mine + pltpu.roll(mine, sector // 2, 1)
    lane = lax.broadcasted_iota(jnp.int32, (1, sector), 1)
    shared = jnp.where(lane < sector // 2, folded[0:1], folded[1:2])
    sums_ref[...] = shared


def remote_kernel(rindex_ref, out_index_ref, moved_ref, turned_hbm, parts_hbm, hpsi_rows, hpsi_hbm, acc, near_ref, rights_ref, sems):
    slots, terms, _ = rindex_ref.shape
    senders, height, _ = moved_ref.shape
    sector = height // terms
    rights = rights_ref.shape[0]
    get_rights = pltpu.make_async_copy(parts_hbm.at[pl.ds(parts_hbm.shape[0] - rights, rights)], rights_ref, sems.at[0])
    get_rights.start()
    slabs = []
    for k in range(acc.shape[0] // height):
        near = turned_hbm.at[senders + k, pl.ds(0, height)]
        slabs.append(pltpu.make_async_copy(near, near_ref.at[pl.ds(k * height, height)], sems.at[1 + k]))
        slabs[k].start()
    acc[...] = jnp.zeros_like(acc)
    get_rights.wait()

    def right_step(i, carry):
        for g in range(terms):
            right = rights_ref[rindex_ref[i % slots, g, i // slots]]
            spot = pl.multiple_of(out_index_ref[i % slots, g, i // slots] * sector, sector)
            acc[pl.ds(spot, sector)] += product(moved_ref[i, g * sector : (g + 1) * sector], twice(right))
        return carry

    lax.fori_loop(0, senders, right_step, 0, unroll=4)
    for copy in slabs:
        copy.wait()
    for b in range(acc.shape[0] // sector):
        start = (b // SUB) * (SUB * sector) + b % SUB
        part = slice(b * sector, (b + 1) * sector)
        hpsi_rows[pl.ds(start, sector, stride=SUB), :] = acc[part] + near_ref[part]
    put = pltpu.make_async_copy(hpsi_rows, hpsi_hbm, sems.at[0])
    put.start()
    put.wait()


def residual_kernel(sums_ref, hpsi_rows, psi_rows, out_ref):
    total = jnp.sum(sums_ref[...], axis=0)
    lane = lax.broadcasted_iota(jnp.int32, total.shape, 1)
    first = lane < total.shape[1] // 2
    corr = jnp.sum(jnp.where(first, total, 0.0), axis=1, keepdims=True)
    norm = jnp.sum(jnp.where(first, 0.0, total), axis=1, keepdims=True)
    theta = corr / (norm + 1e-06)
    out_ref[...] = hpsi_rows[...] - theta * psi_rows[...]


def shards(
    psi,
    left_env,
    right_env,
    send_block,
    send_left,
    send_live,
    recv_right,
    recv_out,
    loc_block,
    loc_left,
    loc_right,
):
    peers = lax.axis_size("renv")
    owned = psi.shape[0]
    sector = math.isqrt(psi.shape[1])
    slots = send_block.shape[1]
    terms = send_left.shape[2]
    count = peers * slots
    lefts = left_env.shape[0]
    rights = right_env.shape[0]
    height = sector + SUB
    psi_rows = as_rows(psi, sector)
    left_rows = as_rows(left_env, sector)
    right_rows = as_rows(right_env, sector)
    by_slot = [index.transpose(1, 2, 0) for index in (send_left, send_live, recv_right, recv_out)]
    blocks = jax.ShapeDtypeStruct((count, height, sector), F32)
    rows = jax.ShapeDtypeStruct((owned * sector, sector), F32)

    sent = pl.pallas_call(
        gather_kernel,
        out_shape=blocks,
        in_specs=[SMEM] * 3 + [VMEM],
        out_specs=HBM,
        scratch_shapes=[pltpu.VMEM(blocks.shape, F32), pltpu.SemaphoreType.DMA((count,))],
        compiler_params=roomy(56),
        name="gather_blocks",
    )(send_block.reshape(-1), *by_slot[:2], psi_rows)
    came = lax.all_to_all(sent.reshape(peers, slots, height, sector), "renv", split_axis=0, concat_axis=0, tiled=True)
    came = came.reshape(count, height, sector)

    slabs = owned // terms
    turned, parts = pl.pallas_call(
        prepare_kernel,
        out_shape=(
            jax.ShapeDtypeStruct((count + slabs, terms * sector + SUB, sector), F32),
            jax.ShapeDtypeStruct((lefts + rights, sector, 2 * sector), BF16),
        ),
        in_specs=[HBM] + [SMEM] * 5 + [VMEM] * 3,
        out_specs=(VMEM,) * 2,
        scratch_shapes=[
            pltpu.VMEM((owned, sector, sector), F32),
            pltpu.VMEM((owned, sector, 2 * sector), BF16),
            pltpu.VMEM((rights, 2 * sector, 2 * sector), BF16),
            pltpu.VMEM((loc_block.shape[0], sector, 2 * sector), BF16),
        ],
        compiler_params=roomy(56),
        cost_estimate=LIGHT,
        name="prepare",
    )(sent, *by_slot[2:], loc_block, loc_left, loc_right, psi_rows, right_rows, left_rows)

    chunk = math.gcd(count, 16)
    moved = []
    sums = 0.0
    for first in range(0, count, chunk):
        part = slice(first, first + chunk) if count > chunk else slice(None)
        kept, share = pl.pallas_call(
            lambda *refs: arrive_kernel(terms, *refs),
            out_shape=(
                jax.ShapeDtypeStruct((chunk, terms * sector, 2 * sector), BF16),
                jax.ShapeDtypeStruct((1, sector), F32),
            ),
            in_specs=[VMEM] + [HBM] * 2,
            out_specs=(VMEM,) * 2,
            scratch_shapes=[
                pltpu.SMEM((chunk, SUB, sector), F32),
                pltpu.VMEM((chunk, terms * sector + SUB, sector), F32),
                pltpu.VMEM((lefts, sector, 2 * sector), BF16),
                pltpu.VMEM((chunk, 2 * sector, 2 * sector), BF16),
                pltpu.SemaphoreType.DMA((6,)),
            ],
            compiler_params=roomy(50),
            name="arrive",
        )(came[part], turned if count == chunk else turned[part], parts)
        moved.append(kept)
        sums = share if count == chunk else sums + share
    moved = moved[0] if len(moved) == 1 else jnp.concatenate(moved, axis=0)
    pair = math.gcd(peers, 2)
    if pair == 2:
        sums = sums + lax.ppermute(sums, "renv", [(s, s ^ 1) for s in range(peers)])
    totals = jnp.broadcast_to(sums[None], (peers // pair, 1, sector))
    alike = [list(range(first, peers, pair)) for first in range(pair)]
    totals = lax.all_to_all(totals, "renv", split_axis=0, concat_axis=0, tiled=True, axis_index_groups=alike)

    hpsi_rows, hpsi = pl.pallas_call(
        remote_kernel,
        out_shape=(rows, rows),
        in_specs=[SMEM] * 2 + [VMEM] + [HBM] * 2,
        out_specs=(VMEM, HBM),
        scratch_shapes=[
            pltpu.VMEM(rows.shape, F32),
            pltpu.VMEM(rows.shape, F32),
            pltpu.VMEM((rights, sector, 2 * sector), BF16),
            pltpu.SemaphoreType.DMA((1 + slabs,)),
        ],
        compiler_params=roomy(50),
        cost_estimate=pl.CostEstimate(flops=4 * 10**9, bytes_accessed=6 * MIB, transcendentals=0),
        name="remote_terms",
    )(*by_slot[2:], moved, turned, parts)

    residual_rows = pl.pallas_call(
        residual_kernel,
        out_shape=rows,
        in_specs=[VMEM] * 3,
        out_specs=VMEM,
        compiler_params=roomy(16),
        name="residual",
    )(totals, hpsi_rows, psi_rows)
    return (from_rows(hpsi, owned), from_rows(residual_rows, owned))


def solution(mesh):
    placed = (
        P(("groups", "renv"), None),
        P("groups", None),
        P(("groups", "renv"), None),
        P(("groups", "renv"), None),
        P(("groups", "renv"), None, None),
        P(("groups", "renv"), None, None),
        P(("groups", "renv"), None, None),
        P(("groups", "renv"), None, None),
        P(("groups", "renv")),
        P(("groups", "renv")),
        P(("groups", "renv")),
    )
    return jax.shard_map(
        shards,
        mesh=mesh,
        in_specs=placed,
        out_specs=(P(("groups", "renv"), None), P(("groups", "renv"), None)),
        check_vma=False,
    )
```

```python
import math

import jax
import jax.numpy as jnp
from jax import lax
from jax.experimental import pallas as pl
from jax.experimental.pallas import tpu as pltpu
from jax.sharding import PartitionSpec as P

F32 = jnp.float32
BF16 = jnp.bfloat16
SUB = 8
VMEM = pl.BlockSpec(memory_space=pltpu.VMEM)
SMEM = pl.BlockSpec(memory_space=pltpu.SMEM)
HBM = pl.BlockSpec(memory_space=pltpu.HBM)
MIB = 2**20
LIGHT = pl.CostEstimate(flops=10**6, bytes_accessed=2**16, transcendentals=0)


def as_rows(blocks, sector):
    count = blocks.shape[0]
    split = blocks.reshape(count // SUB, SUB, sector, sector)
    return split.transpose(0, 2, 1, 3).reshape(count * sector, sector)


def from_rows(rows, count):
    sector = rows.shape[1]
    split = rows.reshape(count // SUB, sector, SUB, sector)
    return split.transpose(0, 2, 1, 3).reshape(count, sector * sector)


def pick(ref, block):
    sector = ref.shape[1]
    start = (block // SUB) * (SUB * sector) + block % SUB
    return ref[pl.ds(start, sector, stride=SUB), :]


def halves(mat):
    high = mat.astype(BF16)
    low = (mat - high.astype(F32)).astype(BF16)
    return jnp.concatenate([high, low], axis=1)


def doubled(mat):
    both = halves(mat)
    return jnp.concatenate([both, both], axis=0)


def product(left, right):
    sector = right.shape[1] // 2
    wide = jnp.dot(left, right, preferred_element_type=F32)
    return wide[:, :sector] + wide[:, sector:]


def stacked(mat):
    high = mat.astype(BF16)
    low = (mat - high.astype(F32)).astype(BF16)
    rows = [jnp.concatenate([part, part], axis=1) for part in (high, low)]
    return jnp.concatenate(rows, axis=0)


def product_t(left, right):
    sector = right.shape[0] // 2
    wide = lax.dot_general(left, right, (((1,), (1,)), ((), ())), preferred_element_type=F32)
    return wide[:, :sector] + wide[:, sector:]


def twice(part):
    return jnp.concatenate([part, part], axis=0)


def roomy(mib):
    return pltpu.CompilerParams(vmem_limit_bytes=mib * MIB)


def gather_kernel(block_ref, left_ref, live_ref, psi_rows, out_hbm, stage, sems):
    slots, terms, _ = left_ref.shape
    sector = psi_rows.shape[1]
    lane = lax.broadcasted_iota(jnp.int32, (SUB, sector), 1)
    puts = []
    for i in range(stage.shape[0]):
        stage[i, :sector] = pick(psi_rows, block_ref[i])
        values = jnp.zeros(lane.shape, jnp.int32)
        for g in range(terms):
            values = jnp.where(lane == g, left_ref[i % slots, g, i // slots], values)
            values = jnp.where(lane == terms + g, live_ref[i % slots, g, i // slots], values)
        stage[i, sector:] = values.astype(F32)
        put = pltpu.make_async_copy(stage.at[i], out_hbm.at[i], sems.at[i])
        put.start()
        puts.append(put)
    for put in puts:
        put.wait()


def prepare_kernel(
    sent_hbm,
    rindex_ref,
    out_index_ref,
    block_ref,
    left_ref,
    right_ref,
    psi_rows,
    right_rows,
    left_rows,
    turned_ref,
    parts_ref,
    near_ref,
    psis_ref,
    stacks_ref,
    moved_ref,
):
    slots, terms, _ = rindex_ref.shape
    sector = psi_rows.shape[1]

    rights = right_rows.shape[0] // sector
    lefts = left_rows.shape[0] // sector

    def split_right(i, carry):
        mat = pick(right_rows, i)
        parts_ref[lefts + i] = halves(mat)
        stacks_ref[i] = stacked(mat)
        return carry

    lax.fori_loop(0, rights, split_right, 0, unroll=4)

    def split_psi(i, carry):
        psis_ref[i] = halves(pick(psi_rows, i))
        return carry

    lax.fori_loop(0, psis_ref.shape[0], split_psi, 0, unroll=4)

    def turn(i, carry):
        for g in range(terms):
            right = stacks_ref[rindex_ref[i % slots, g, i // slots]]
            psi = psis_ref[out_index_ref[i % slots, g, i // slots]]
            turned_ref[i, g * sector : (g + 1) * sector] = product_t(psi, right)
        turned_ref[i, terms * sector :] = jnp.zeros((SUB, sector), F32)
        return carry

    slabs = near_ref.shape[0] // terms
    senders = turned_ref.shape[0] - slabs
    lax.fori_loop(0, senders, turn, 0, unroll=4)

    def split_left(i, carry):
        parts_ref[i] = halves(pick(left_rows, i))
        return carry

    lax.fori_loop(0, lefts, split_left, 0, unroll=8)

    def left_step(k, carry):
        moved_ref[k] = halves(product(parts_ref[left_ref[k]], twice(psis_ref[block_ref[k]])))
        return carry

    lax.fori_loop(0, block_ref.shape[0], left_step, 0, unroll=8)
    near_ref[...] = jnp.zeros_like(near_ref)

    def right_step(k, carry):
        near_ref[block_ref[k]] += product(moved_ref[k], twice(parts_ref[lefts + right_ref[k]]))
        return carry

    lax.fori_loop(0, block_ref.shape[0], right_step, 0, unroll=8)
    corr = jnp.zeros((1, sector), F32)
    norm = jnp.zeros((1, sector), F32)
    for b in range(near_ref.shape[0]):
        mat = pick(psi_rows, b)
        turned_ref[senders + b // terms, (b % terms) * sector : (b % terms + 1) * sector] = near_ref[b]
        corr += jnp.sum(mat * near_ref[b], axis=0, keepdims=True)
        norm += jnp.sum(mat * mat, axis=0, keepdims=True)
    row = lax.broadcasted_iota(jnp.int32, (SUB, sector), 0)
    turned_ref[0, terms * sector :] = jnp.where(row == 0, corr, jnp.where(row == 1, norm, 0.0))


def arrive_kernel(terms, came_ref, turned_hbm, parts_hbm, moved_ref, sums_ref, marks, turned_ref, lefts_ref, weights_ref, sems):
    count, height, sector = came_ref.shape
    get_marks = pltpu.make_async_copy(came_ref.at[:, pl.ds(sector, height - sector)], marks, sems.at[0])
    get_lefts = pltpu.make_async_copy(parts_hbm.at[pl.ds(0, lefts_ref.shape[0])], lefts_ref, sems.at[1])
    quarter = count // math.gcd(count, 4)
    spans = [pl.ds(first, quarter) for first in range(0, count, quarter)]
    get_turned = [
        pltpu.make_async_copy(turned_hbm.at[span], turned_ref.at[span], sems.at[2 + k]) for k, span in enumerate(spans)
    ]
    for copy in (get_marks, get_lefts, *get_turned):
        copy.start()

    def split(i, carry):
        weights_ref[i] = doubled(came_ref[i, :sector])
        return carry

    lax.fori_loop(0, count, split, 0, unroll=4)
    get_marks.wait()
    get_lefts.wait()

    def block(i, total):
        stack = [lefts_ref[marks[i, 0, g].astype(jnp.int32)] for g in range(terms)]
        moved = product(jnp.concatenate(stack, axis=0), weights_ref[i])
        for g in range(terms):
            part = slice(g * sector, (g + 1) * sector)
            one = moved[part] * marks[i, 0, terms + g]
            moved_ref[i, part] = halves(one)
            total += jnp.sum((one * turned_ref[i, part]).reshape(-1, SUB, sector), axis=0)
        return total

    total = jnp.zeros((SUB, sector), F32)
    for k, copy in enumerate(get_turned):
        copy.wait()
        total = lax.fori_loop(k * quarter, (k + 1) * quarter, block, total, unroll=4)
    corr = jnp.sum(total, axis=0, keepdims=True)
    row = lax.broadcasted_iota(jnp.int32, total.shape, 0)
    mine = turned_ref[0, terms * sector :] + jnp.where(row == 0, corr, 0.0)
    folded = mine + pltpu.roll(mine, sector // 2, 1)
    lane = lax.broadcasted_iota(jnp.int32, (1, sector), 1)
    shared = jnp.where(lane < sector // 2, folded[0:1], folded[1:2])
    for i in range(sums_ref.shape[0]):
        sums_ref[i] = shared


def remote_kernel(rindex_ref, out_index_ref, moved_ref, turned_hbm, parts_hbm, hpsi_rows, hpsi_hbm, acc, near_ref, rights_ref, sems):
    slots, terms, _ = rindex_ref.shape
    senders, height, _ = moved_ref.shape
    sector = height // terms
    rights = rights_ref.shape[0]
    get_rights = pltpu.make_async_copy(parts_hbm.at[pl.ds(parts_hbm.shape[0] - rights, rights)], rights_ref, sems.at[0])
    get_rights.start()
    slabs = []
    for k in range(acc.shape[0] // height):
        near = turned_hbm.at[senders + k, pl.ds(0, height)]
        slabs.append(pltpu.make_async_copy(near, near_ref.at[pl.ds(k * height, height)], sems.at[1 + k]))
        slabs[k].start()
    acc[...] = jnp.zeros_like(acc)
    get_rights.wait()

    def right_step(i, carry):
        for g in range(terms):
            right = rights_ref[rindex_ref[i % slots, g, i // slots]]
            spot = pl.multiple_of(out_index_ref[i % slots, g, i // slots] * sector, sector)
            acc[pl.ds(spot, sector)] += product(moved_ref[i, g * sector : (g + 1) * sector], twice(right))
        return carry

    lax.fori_loop(0, senders, right_step, 0, unroll=4)
    for copy in slabs:
        copy.wait()
    for b in range(acc.shape[0] // sector):
        start = (b // SUB) * (SUB * sector) + b % SUB
        part = slice(b * sector, (b + 1) * sector)
        hpsi_rows[pl.ds(start, sector, stride=SUB), :] = acc[part] + near_ref[part]
    put = pltpu.make_async_copy(hpsi_rows, hpsi_hbm, sems.at[0])
    put.start()
    put.wait()


def residual_kernel(sums_ref, hpsi_rows, psi_rows, out_ref):
    total = jnp.sum(sums_ref[...], axis=0)
    lane = lax.broadcasted_iota(jnp.int32, total.shape, 1)
    first = lane < total.shape[1] // 2
    corr = jnp.sum(jnp.where(first, total, 0.0), axis=1, keepdims=True)
    norm = jnp.sum(jnp.where(first, 0.0, total), axis=1, keepdims=True)
    theta = corr / (norm + 1e-06)
    out_ref[...] = hpsi_rows[...] - theta * psi_rows[...]


def shards(
    psi,
    left_env,
    right_env,
    send_block,
    send_left,
    send_live,
    recv_right,
    recv_out,
    loc_block,
    loc_left,
    loc_right,
):
    peers = lax.axis_size("renv")
    owned = psi.shape[0]
    sector = math.isqrt(psi.shape[1])
    slots = send_block.shape[1]
    terms = send_left.shape[2]
    count = peers * slots
    lefts = left_env.shape[0]
    rights = right_env.shape[0]
    height = sector + SUB
    psi_rows = as_rows(psi, sector)
    left_rows = as_rows(left_env, sector)
    right_rows = as_rows(right_env, sector)
    by_slot = [index.transpose(1, 2, 0) for index in (send_left, send_live, recv_right, recv_out)]
    blocks = jax.ShapeDtypeStruct((count, height, sector), F32)
    rows = jax.ShapeDtypeStruct((owned * sector, sector), F32)

    sent = pl.pallas_call(
        gather_kernel,
        out_shape=blocks,
        in_specs=[SMEM] * 3 + [VMEM],
        out_specs=HBM,
        scratch_shapes=[pltpu.VMEM(blocks.shape, F32), pltpu.SemaphoreType.DMA((count,))],
        compiler_params=roomy(56),
        name="gather_blocks",
    )(send_block.reshape(-1), *by_slot[:2], psi_rows)
    came = lax.all_to_all(sent.reshape(peers, slots, height, sector), "renv", split_axis=0, concat_axis=0, tiled=True)
    came = came.reshape(count, height, sector)

    slabs = owned // terms
    turned, parts = pl.pallas_call(
        prepare_kernel,
        out_shape=(
            jax.ShapeDtypeStruct((count + slabs, terms * sector + SUB, sector), F32),
            jax.ShapeDtypeStruct((lefts + rights, sector, 2 * sector), BF16),
        ),
        in_specs=[HBM] + [SMEM] * 5 + [VMEM] * 3,
        out_specs=(VMEM,) * 2,
        scratch_shapes=[
            pltpu.VMEM((owned, sector, sector), F32),
            pltpu.VMEM((owned, sector, 2 * sector), BF16),
            pltpu.VMEM((rights, 2 * sector, 2 * sector), BF16),
            pltpu.VMEM((loc_block.shape[0], sector, 2 * sector), BF16),
        ],
        compiler_params=roomy(56),
        cost_estimate=LIGHT,
        name="prepare",
    )(sent, *by_slot[2:], loc_block, loc_left, loc_right, psi_rows, right_rows, left_rows)

    chunk = math.gcd(count, 16)
    moved = []
    sums = 0.0
    for first in range(0, count, chunk):
        part = slice(first, first + chunk) if count > chunk else slice(None)
        kept, share = pl.pallas_call(
            lambda *refs: arrive_kernel(terms, *refs),
            out_shape=(
                jax.ShapeDtypeStruct((chunk, terms * sector, 2 * sector), BF16),
                jax.ShapeDtypeStruct((peers, 1, sector), F32),
            ),
            in_specs=[VMEM] + [HBM] * 2,
            out_specs=(VMEM,) * 2,
            scratch_shapes=[
                pltpu.SMEM((chunk, SUB, sector), F32),
                pltpu.VMEM((chunk, terms * sector + SUB, sector), F32),
                pltpu.VMEM((lefts, sector, 2 * sector), BF16),
                pltpu.VMEM((chunk, 2 * sector, 2 * sector), BF16),
                pltpu.SemaphoreType.DMA((6,)),
            ],
            compiler_params=roomy(50),
            name="arrive",
        )(came[part], turned if count == chunk else turned[part], parts)
        moved.append(kept)
        sums = share if count == chunk else sums + share
    moved = moved[0] if len(moved) == 1 else jnp.concatenate(moved, axis=0)
    totals = lax.all_to_all(
        sums, "renv", split_axis=0, concat_axis=0, tiled=True, axis_index_groups=[list(reversed(range(peers)))]
    )

    hpsi_rows, hpsi = pl.pallas_call(
        remote_kernel,
        out_shape=(rows, rows),
        in_specs=[SMEM] * 2 + [VMEM] + [HBM] * 2,
        out_specs=(VMEM, HBM),
        scratch_shapes=[
            pltpu.VMEM(rows.shape, F32),
            pltpu.VMEM(rows.shape, F32),
            pltpu.VMEM((rights, sector, 2 * sector), BF16),
            pltpu.SemaphoreType.DMA((1 + slabs,)),
        ],
        compiler_params=roomy(50),
        cost_estimate=pl.CostEstimate(flops=4 * 10**9, bytes_accessed=6 * MIB, transcendentals=0),
        name="remote_terms",
    )(*by_slot[2:], moved, turned, parts)

    residual_rows = pl.pallas_call(
        residual_kernel,
        out_shape=rows,
        in_specs=[VMEM] * 3,
        out_specs=VMEM,
        compiler_params=roomy(16),
        name="residual",
    )(totals, hpsi_rows, psi_rows)
    return (from_rows(hpsi, owned), from_rows(residual_rows, owned))


def solution(mesh):
    placed = (
        P(("groups", "renv"), None),
        P("groups", None),
        P(("groups", "renv"), None),
        P(("groups", "renv"), None),
        P(("groups", "renv"), None, None),
        P(("groups", "renv"), None, None),
        P(("groups", "renv"), None, None),
        P(("groups", "renv"), None, None),
        P(("groups", "renv")),
        P(("groups", "renv")),
        P(("groups", "renv")),
    )
    return jax.shard_map(
        shards,
        mesh=mesh,
        in_specs=placed,
        out_specs=(P(("groups", "renv"), None), P(("groups", "renv"), None)),
        check_vma=False,
    )
```

```python
import math

import jax
import jax.numpy as jnp
from jax import lax
from jax.experimental import pallas as pl
from jax.experimental.pallas import tpu as pltpu
from jax.sharding import PartitionSpec as P

F32 = jnp.float32
BF16 = jnp.bfloat16
SUB = 8
VMEM = pl.BlockSpec(memory_space=pltpu.VMEM)
SMEM = pl.BlockSpec(memory_space=pltpu.SMEM)
HBM = pl.BlockSpec(memory_space=pltpu.HBM)
MIB = 2**20
LIGHT = pl.CostEstimate(flops=10**6, bytes_accessed=2**16, transcendentals=0)


def as_rows(blocks, sector):
    count = blocks.shape[0]
    split = blocks.reshape(count // SUB, SUB, sector, sector)
    return split.transpose(0, 2, 1, 3).reshape(count * sector, sector)


def from_rows(rows, count):
    sector = rows.shape[1]
    split = rows.reshape(count // SUB, sector, SUB, sector)
    return split.transpose(0, 2, 1, 3).reshape(count, sector * sector)


def pick(ref, block):
    sector = ref.shape[1]
    start = (block // SUB) * (SUB * sector) + block % SUB
    return ref[pl.ds(start, sector, stride=SUB), :]


def halves(mat):
    high = mat.astype(BF16)
    low = (mat - high.astype(F32)).astype(BF16)
    return jnp.concatenate([high, low], axis=1)


def doubled(mat):
    both = halves(mat)
    return jnp.concatenate([both, both], axis=0)


def product(left, right):
    sector = right.shape[1] // 2
    wide = jnp.dot(left, right, preferred_element_type=F32)
    return wide[:, :sector] + wide[:, sector:]


def stacked(mat):
    high = mat.astype(BF16)
    low = (mat - high.astype(F32)).astype(BF16)
    rows = [jnp.concatenate([part, part], axis=1) for part in (high, low)]
    return jnp.concatenate(rows, axis=0)


def product_t(left, right):
    sector = right.shape[0] // 2
    wide = lax.dot_general(left, right, (((1,), (1,)), ((), ())), preferred_element_type=F32)
    return wide[:, :sector] + wide[:, sector:]


def twice(part):
    return jnp.concatenate([part, part], axis=0)


def roomy(mib):
    return pltpu.CompilerParams(vmem_limit_bytes=mib * MIB)


def gather_kernel(block_ref, left_ref, live_ref, psi_rows, out_hbm, stage, sems):
    slots, terms, _ = left_ref.shape
    sector = psi_rows.shape[1]
    lane = lax.broadcasted_iota(jnp.int32, (SUB, sector), 1)
    puts = []
    for i in range(stage.shape[0]):
        stage[i, :sector] = pick(psi_rows, block_ref[i])
        values = jnp.zeros(lane.shape, jnp.int32)
        for g in range(terms):
            values = jnp.where(lane == g, left_ref[i % slots, g, i // slots], values)
            values = jnp.where(lane == terms + g, live_ref[i % slots, g, i // slots], values)
        stage[i, sector:] = values.astype(F32)
        put = pltpu.make_async_copy(stage.at[i], out_hbm.at[i], sems.at[i])
        put.start()
        puts.append(put)
    for put in puts:
        put.wait()


def prepare_kernel(
    sent_hbm,
    rindex_ref,
    out_index_ref,
    block_ref,
    left_ref,
    right_ref,
    psi_rows,
    right_rows,
    left_rows,
    turned_ref,
    parts_ref,
    near_ref,
    psis_ref,
    stacks_ref,
    moved_ref,
):
    slots, terms, _ = rindex_ref.shape
    sector = psi_rows.shape[1]

    rights = right_rows.shape[0] // sector
    lefts = left_rows.shape[0] // sector

    def split_right(i, carry):
        mat = pick(right_rows, i)
        parts_ref[lefts + i] = halves(mat)
        stacks_ref[i] = stacked(mat)
        return carry

    lax.fori_loop(0, rights, split_right, 0, unroll=4)

    def split_psi(i, carry):
        psis_ref[i] = halves(pick(psi_rows, i))
        return carry

    lax.fori_loop(0, psis_ref.shape[0], split_psi, 0, unroll=4)

    def turn(i, carry):
        for g in range(terms):
            right = stacks_ref[rindex_ref[i % slots, g, i // slots]]
            psi = psis_ref[out_index_ref[i % slots, g, i // slots]]
            turned_ref[i, g * sector : (g + 1) * sector] = product_t(psi, right)
        turned_ref[i, terms * sector :] = jnp.zeros((SUB, sector), F32)
        return carry

    slabs = near_ref.shape[0] // terms
    senders = turned_ref.shape[0] - slabs
    lax.fori_loop(0, senders, turn, 0, unroll=4)

    def split_left(i, carry):
        parts_ref[i] = halves(pick(left_rows, i))
        return carry

    lax.fori_loop(0, lefts, split_left, 0, unroll=8)

    def left_step(k, carry):
        moved_ref[k] = halves(product(parts_ref[left_ref[k]], twice(psis_ref[block_ref[k]])))
        return carry

    lax.fori_loop(0, block_ref.shape[0], left_step, 0, unroll=8)
    near_ref[...] = jnp.zeros_like(near_ref)

    def right_step(k, carry):
        near_ref[block_ref[k]] += product(moved_ref[k], twice(parts_ref[lefts + right_ref[k]]))
        return carry

    lax.fori_loop(0, block_ref.shape[0], right_step, 0, unroll=8)
    corr = jnp.zeros((1, sector), F32)
    norm = jnp.zeros((1, sector), F32)
    for b in range(near_ref.shape[0]):
        mat = pick(psi_rows, b)
        turned_ref[senders + b // terms, (b % terms) * sector : (b % terms + 1) * sector] = near_ref[b]
        corr += jnp.sum(mat * near_ref[b], axis=0, keepdims=True)
        norm += jnp.sum(mat * mat, axis=0, keepdims=True)
    row = lax.broadcasted_iota(jnp.int32, (SUB, sector), 0)
    turned_ref[0, terms * sector :] = jnp.where(row == 0, corr, jnp.where(row == 1, norm, 0.0))


def arrive_kernel(terms, came_ref, turned_hbm, parts_hbm, moved_ref, sums_ref, marks, turned_ref, lefts_ref, weights_ref, sems):
    count, height, sector = came_ref.shape
    get_marks = pltpu.make_async_copy(came_ref.at[:, pl.ds(sector, height - sector)], marks, sems.at[0])
    get_lefts = pltpu.make_async_copy(parts_hbm.at[pl.ds(0, lefts_ref.shape[0])], lefts_ref, sems.at[1])
    quarter = count // math.gcd(count, 4)
    spans = [pl.ds(first, quarter) for first in range(0, count, quarter)]
    get_turned = [
        pltpu.make_async_copy(turned_hbm.at[span], turned_ref.at[span], sems.at[2 + k]) for k, span in enumerate(spans)
    ]
    for copy in (get_marks, get_lefts, *get_turned):
        copy.start()

    def split(i, carry):
        weights_ref[i] = doubled(came_ref[i, :sector])
        return carry

    lax.fori_loop(0, count, split, 0, unroll=4)
    get_marks.wait()
    get_lefts.wait()

    def block(i, total):
        stack = [lefts_ref[marks[i, 0, g].astype(jnp.int32)] for g in range(terms)]
        moved = product(jnp.concatenate(stack, axis=0), weights_ref[i])
        for g in range(terms):
            part = slice(g * sector, (g + 1) * sector)
            one = moved[part] * marks[i, 0, terms + g]
            moved_ref[i, part] = halves(one)
            total += jnp.sum((one * turned_ref[i, part]).reshape(-1, SUB, sector), axis=0)
        return total

    total = jnp.zeros((SUB, sector), F32)
    for k, copy in enumerate(get_turned):
        copy.wait()
        total = lax.fori_loop(k * quarter, (k + 1) * quarter, block, total, unroll=4)
    corr = jnp.sum(total, axis=0, keepdims=True)
    row = lax.broadcasted_iota(jnp.int32, total.shape, 0)
    mine = turned_ref[0, terms * sector :] + jnp.where(row == 0, corr, 0.0)
    folded = mine + pltpu.roll(mine, sector // 2, 1)
    lane = lax.broadcasted_iota(jnp.int32, (1, sector), 1)
    shared = jnp.where(lane < sector // 2, folded[0:1], folded[1:2])
    for i in range(sums_ref.shape[0]):
        sums_ref[i] = shared


def remote_kernel(rindex_ref, out_index_ref, moved_ref, turned_hbm, parts_hbm, hpsi_rows, hpsi_hbm, acc, near_ref, rights_ref, sems):
    slots, terms, _ = rindex_ref.shape
    senders, height, _ = moved_ref.shape
    sector = height // terms
    rights = rights_ref.shape[0]
    get_rights = pltpu.make_async_copy(parts_hbm.at[pl.ds(parts_hbm.shape[0] - rights, rights)], rights_ref, sems.at[0])
    get_rights.start()
    slabs = []
    for k in range(acc.shape[0] // height):
        near = turned_hbm.at[senders + k, pl.ds(0, height)]
        slabs.append(pltpu.make_async_copy(near, near_ref.at[pl.ds(k * height, height)], sems.at[1 + k]))
        slabs[k].start()
    acc[...] = jnp.zeros_like(acc)
    get_rights.wait()

    def right_step(i, carry):
        for g in range(terms):
            right = rights_ref[rindex_ref[i % slots, g, i // slots]]
            spot = pl.multiple_of(out_index_ref[i % slots, g, i // slots] * sector, sector)
            acc[pl.ds(spot, sector)] += product(moved_ref[i, g * sector : (g + 1) * sector], twice(right))
        return carry

    lax.fori_loop(0, senders, right_step, 0, unroll=4)
    for copy in slabs:
        copy.wait()
    for b in range(acc.shape[0] // sector):
        start = (b // SUB) * (SUB * sector) + b % SUB
        part = slice(b * sector, (b + 1) * sector)
        hpsi_rows[pl.ds(start, sector, stride=SUB), :] = acc[part] + near_ref[part]
    put = pltpu.make_async_copy(hpsi_rows, hpsi_hbm, sems.at[0])
    put.start()
    put.wait()


def scalar_order(peers):
    quarter = peers // 4
    if peers % 4:
        return list(range(peers))
    order = list(range(peers - 1, 3 * quarter - 1, -1)) + list(range(quarter))
    return order + list(range(3 * quarter - 1, quarter - 1, -1))


def residual_kernel(sums_ref, hpsi_rows, psi_rows, out_ref):
    total = jnp.sum(sums_ref[...], axis=0)
    lane = lax.broadcasted_iota(jnp.int32, total.shape, 1)
    first = lane < total.shape[1] // 2
    corr = jnp.sum(jnp.where(first, total, 0.0), axis=1, keepdims=True)
    norm = jnp.sum(jnp.where(first, 0.0, total), axis=1, keepdims=True)
    theta = corr / (norm + 1e-06)
    out_ref[...] = hpsi_rows[...] - theta * psi_rows[...]


def shards(
    psi,
    left_env,
    right_env,
    send_block,
    send_left,
    send_live,
    recv_right,
    recv_out,
    loc_block,
    loc_left,
    loc_right,
):
    peers = lax.axis_size("renv")
    owned = psi.shape[0]
    sector = math.isqrt(psi.shape[1])
    slots = send_block.shape[1]
    terms = send_left.shape[2]
    count = peers * slots
    lefts = left_env.shape[0]
    rights = right_env.shape[0]
    height = sector + SUB
    psi_rows = as_rows(psi, sector)
    left_rows = as_rows(left_env, sector)
    right_rows = as_rows(right_env, sector)
    by_slot = [index.transpose(1, 2, 0) for index in (send_left, send_live, recv_right, recv_out)]
    blocks = jax.ShapeDtypeStruct((count, height, sector), F32)
    rows = jax.ShapeDtypeStruct((owned * sector, sector), F32)

    sent = pl.pallas_call(
        gather_kernel,
        out_shape=blocks,
        in_specs=[SMEM] * 3 + [VMEM],
        out_specs=HBM,
        scratch_shapes=[pltpu.VMEM(blocks.shape, F32), pltpu.SemaphoreType.DMA((count,))],
        compiler_params=roomy(56),
        name="gather_blocks",
    )(send_block.reshape(-1), *by_slot[:2], psi_rows)
    came = lax.all_to_all(sent.reshape(peers, slots, height, sector), "renv", split_axis=0, concat_axis=0, tiled=True)
    came = came.reshape(count, height, sector)

    slabs = owned // terms
    turned, parts = pl.pallas_call(
        prepare_kernel,
        out_shape=(
            jax.ShapeDtypeStruct((count + slabs, terms * sector + SUB, sector), F32),
            jax.ShapeDtypeStruct((lefts + rights, sector, 2 * sector), BF16),
        ),
        in_specs=[HBM] + [SMEM] * 5 + [VMEM] * 3,
        out_specs=(VMEM,) * 2,
        scratch_shapes=[
            pltpu.VMEM((owned, sector, sector), F32),
            pltpu.VMEM((owned, sector, 2 * sector), BF16),
            pltpu.VMEM((rights, 2 * sector, 2 * sector), BF16),
            pltpu.VMEM((loc_block.shape[0], sector, 2 * sector), BF16),
        ],
        compiler_params=roomy(56),
        cost_estimate=LIGHT,
        name="prepare",
    )(sent, *by_slot[2:], loc_block, loc_left, loc_right, psi_rows, right_rows, left_rows)

    chunk = math.gcd(count, 16)
    moved = []
    sums = 0.0
    for first in range(0, count, chunk):
        part = slice(first, first + chunk) if count > chunk else slice(None)
        kept, share = pl.pallas_call(
            lambda *refs: arrive_kernel(terms, *refs),
            out_shape=(
                jax.ShapeDtypeStruct((chunk, terms * sector, 2 * sector), BF16),
                jax.ShapeDtypeStruct((peers, 1, sector), F32),
            ),
            in_specs=[VMEM] + [HBM] * 2,
            out_specs=(VMEM,) * 2,
            scratch_shapes=[
                pltpu.SMEM((chunk, SUB, sector), F32),
                pltpu.VMEM((chunk, terms * sector + SUB, sector), F32),
                pltpu.VMEM((lefts, sector, 2 * sector), BF16),
                pltpu.VMEM((chunk, 2 * sector, 2 * sector), BF16),
                pltpu.SemaphoreType.DMA((6,)),
            ],
            compiler_params=roomy(50),
            name="arrive",
        )(came[part], turned if count == chunk else turned[part], parts)
        moved.append(kept)
        sums = share if count == chunk else sums + share
    moved = moved[0] if len(moved) == 1 else jnp.concatenate(moved, axis=0)
    totals = lax.all_to_all(
        sums, "renv", split_axis=0, concat_axis=0, tiled=True, axis_index_groups=[scalar_order(peers)]
    )

    hpsi_rows, hpsi = pl.pallas_call(
        remote_kernel,
        out_shape=(rows, rows),
        in_specs=[SMEM] * 2 + [VMEM] + [HBM] * 2,
        out_specs=(VMEM, HBM),
        scratch_shapes=[
            pltpu.VMEM(rows.shape, F32),
            pltpu.VMEM(rows.shape, F32),
            pltpu.VMEM((rights, sector, 2 * sector), BF16),
            pltpu.SemaphoreType.DMA((1 + slabs,)),
        ],
        compiler_params=roomy(50),
        cost_estimate=pl.CostEstimate(flops=4 * 10**9, bytes_accessed=6 * MIB, transcendentals=0),
        name="remote_terms",
    )(*by_slot[2:], moved, turned, parts)

    residual_rows = pl.pallas_call(
        residual_kernel,
        out_shape=rows,
        in_specs=[VMEM] * 3,
        out_specs=VMEM,
        compiler_params=roomy(16),
        name="residual",
    )(totals, hpsi_rows, psi_rows)
    return (from_rows(hpsi, owned), from_rows(residual_rows, owned))


def solution(mesh):
    placed = (
        P(("groups", "renv"), None),
        P("groups", None),
        P(("groups", "renv"), None),
        P(("groups", "renv"), None),
        P(("groups", "renv"), None, None),
        P(("groups", "renv"), None, None),
        P(("groups", "renv"), None, None),
        P(("groups", "renv"), None, None),
        P(("groups", "renv")),
        P(("groups", "renv")),
        P(("groups", "renv")),
    )
    return jax.shard_map(
        shards,
        mesh=mesh,
        in_specs=placed,
        out_specs=(P(("groups", "renv"), None), P(("groups", "renv"), None)),
        check_vma=False,
    )
```

```python
import math

import jax
import jax.numpy as jnp
from jax import lax
from jax.experimental import pallas as pl
from jax.experimental.pallas import tpu as pltpu
from jax.sharding import PartitionSpec as P

F32 = jnp.float32
BF16 = jnp.bfloat16
SUB = 8
VMEM = pl.BlockSpec(memory_space=pltpu.VMEM)
SMEM = pl.BlockSpec(memory_space=pltpu.SMEM)
HBM = pl.BlockSpec(memory_space=pltpu.HBM)
MIB = 2**20
LIGHT = pl.CostEstimate(flops=10**6, bytes_accessed=2**16, transcendentals=0)


def as_rows(blocks, sector):
    count = blocks.shape[0]
    split = blocks.reshape(count // SUB, SUB, sector, sector)
    return split.transpose(0, 2, 1, 3).reshape(count * sector, sector)


def from_rows(rows, count):
    sector = rows.shape[1]
    split = rows.reshape(count // SUB, sector, SUB, sector)
    return split.transpose(0, 2, 1, 3).reshape(count, sector * sector)


def pick(ref, block):
    sector = ref.shape[1]
    start = (block // SUB) * (SUB * sector) + block % SUB
    return ref[pl.ds(start, sector, stride=SUB), :]


def halves(mat):
    high = mat.astype(BF16)
    low = (mat - high.astype(F32)).astype(BF16)
    return jnp.concatenate([high, low], axis=1)


def doubled(mat):
    both = halves(mat)
    return jnp.concatenate([both, both], axis=0)


def product(left, right):
    sector = right.shape[1] // 2
    wide = jnp.dot(left, right, preferred_element_type=F32)
    return wide[:, :sector] + wide[:, sector:]


def stacked(mat):
    high = mat.astype(BF16)
    low = (mat - high.astype(F32)).astype(BF16)
    rows = [jnp.concatenate([part, part], axis=1) for part in (high, low)]
    return jnp.concatenate(rows, axis=0)


def product_t(left, right):
    sector = right.shape[0] // 2
    wide = lax.dot_general(left, right, (((1,), (1,)), ((), ())), preferred_element_type=F32)
    return wide[:, :sector] + wide[:, sector:]


def twice(part):
    return jnp.concatenate([part, part], axis=0)


def roomy(mib):
    return pltpu.CompilerParams(vmem_limit_bytes=mib * MIB)


def member(position, peers):
    if peers % 2:
        return position
    middle = peers // 2 + 1
    return position + middle * (1 * (position == 0) - 1 * (position == middle))


def gather_kernel(block_ref, left_ref, live_ref, psi_rows, out_hbm, stage, sems):
    slots, terms, peers = left_ref.shape
    sector = psi_rows.shape[1]
    lane = lax.broadcasted_iota(jnp.int32, (SUB, sector), 1)
    puts = []
    for i in range(stage.shape[0]):
        slot, peer = i % slots, member(i // slots, peers)
        stage[i, :sector] = pick(psi_rows, block_ref[peer * slots + slot])
        values = jnp.zeros(lane.shape, jnp.int32)
        for g in range(terms):
            values = jnp.where(lane == g, left_ref[slot, g, peer], values)
            values = jnp.where(lane == terms + g, live_ref[slot, g, peer], values)
        stage[i, sector:] = values.astype(F32)
        put = pltpu.make_async_copy(stage.at[i], out_hbm.at[i], sems.at[i])
        put.start()
        puts.append(put)
    for put in puts:
        put.wait()


def prepare_kernel(
    sent_hbm,
    rindex_ref,
    out_index_ref,
    block_ref,
    left_ref,
    right_ref,
    psi_rows,
    right_rows,
    left_rows,
    turned_ref,
    parts_ref,
    near_ref,
    psis_ref,
    stacks_ref,
    moved_ref,
):
    slots, terms, peers = rindex_ref.shape
    sector = psi_rows.shape[1]

    rights = right_rows.shape[0] // sector
    lefts = left_rows.shape[0] // sector

    def split_right(i, carry):
        mat = pick(right_rows, i)
        parts_ref[lefts + i] = halves(mat)
        stacks_ref[i] = stacked(mat)
        return carry

    lax.fori_loop(0, rights, split_right, 0, unroll=4)

    def split_psi(i, carry):
        psis_ref[i] = halves(pick(psi_rows, i))
        return carry

    lax.fori_loop(0, psis_ref.shape[0], split_psi, 0, unroll=4)

    def turn(i, carry):
        slot, peer = i % slots, member(i // slots, peers)
        for g in range(terms):
            right = stacks_ref[rindex_ref[slot, g, peer]]
            psi = psis_ref[out_index_ref[slot, g, peer]]
            turned_ref[i, g * sector : (g + 1) * sector] = product_t(psi, right)
        turned_ref[i, terms * sector :] = jnp.zeros((SUB, sector), F32)
        return carry

    slabs = near_ref.shape[0] // terms
    senders = turned_ref.shape[0] - slabs
    lax.fori_loop(0, senders, turn, 0, unroll=4)

    def split_left(i, carry):
        parts_ref[i] = halves(pick(left_rows, i))
        return carry

    lax.fori_loop(0, lefts, split_left, 0, unroll=8)

    def left_step(k, carry):
        moved_ref[k] = halves(product(parts_ref[left_ref[k]], twice(psis_ref[block_ref[k]])))
        return carry

    lax.fori_loop(0, block_ref.shape[0], left_step, 0, unroll=8)
    near_ref[...] = jnp.zeros_like(near_ref)

    def right_step(k, carry):
        near_ref[block_ref[k]] += product(moved_ref[k], twice(parts_ref[lefts + right_ref[k]]))
        return carry

    lax.fori_loop(0, block_ref.shape[0], right_step, 0, unroll=8)
    corr = jnp.zeros((1, sector), F32)
    norm = jnp.zeros((1, sector), F32)
    for b in range(near_ref.shape[0]):
        mat = pick(psi_rows, b)
        turned_ref[senders + b // terms, (b % terms) * sector : (b % terms + 1) * sector] = near_ref[b]
        corr += jnp.sum(mat * near_ref[b], axis=0, keepdims=True)
        norm += jnp.sum(mat * mat, axis=0, keepdims=True)
    row = lax.broadcasted_iota(jnp.int32, (SUB, sector), 0)
    turned_ref[0, terms * sector :] = jnp.where(row == 0, corr, jnp.where(row == 1, norm, 0.0))


def arrive_kernel(terms, came_ref, turned_hbm, parts_hbm, moved_ref, sums_ref, marks, turned_ref, lefts_ref, weights_ref, sems):
    count, height, sector = came_ref.shape
    get_marks = pltpu.make_async_copy(came_ref.at[:, pl.ds(sector, height - sector)], marks, sems.at[0])
    get_lefts = pltpu.make_async_copy(parts_hbm.at[pl.ds(0, lefts_ref.shape[0])], lefts_ref, sems.at[1])
    quarter = count // math.gcd(count, 4)
    spans = [pl.ds(first, quarter) for first in range(0, count, quarter)]
    get_turned = [
        pltpu.make_async_copy(turned_hbm.at[span], turned_ref.at[span], sems.at[2 + k]) for k, span in enumerate(spans)
    ]
    for copy in (get_marks, get_lefts, *get_turned):
        copy.start()

    def split(i, carry):
        weights_ref[i] = doubled(came_ref[i, :sector])
        return carry

    lax.fori_loop(0, count, split, 0, unroll=4)
    get_marks.wait()
    get_lefts.wait()

    def block(i, total):
        stack = [lefts_ref[marks[i, 0, g].astype(jnp.int32)] for g in range(terms)]
        moved = product(jnp.concatenate(stack, axis=0), weights_ref[i])
        for g in range(terms):
            part = slice(g * sector, (g + 1) * sector)
            one = moved[part] * marks[i, 0, terms + g]
            moved_ref[i, part] = halves(one)
            total += jnp.sum((one * turned_ref[i, part]).reshape(-1, SUB, sector), axis=0)
        return total

    total = jnp.zeros((SUB, sector), F32)
    for k, copy in enumerate(get_turned):
        copy.wait()
        total = lax.fori_loop(k * quarter, (k + 1) * quarter, block, total, unroll=4)
    corr = jnp.sum(total, axis=0, keepdims=True)
    row = lax.broadcasted_iota(jnp.int32, total.shape, 0)
    mine = turned_ref[0, terms * sector :] + jnp.where(row == 0, corr, 0.0)
    folded = mine + pltpu.roll(mine, sector // 2, 1)
    lane = lax.broadcasted_iota(jnp.int32, (1, sector), 1)
    shared = jnp.where(lane < sector // 2, folded[0:1], folded[1:2])
    for i in range(sums_ref.shape[0]):
        sums_ref[i] = shared


def remote_kernel(rindex_ref, out_index_ref, moved_ref, turned_hbm, parts_hbm, hpsi_rows, hpsi_hbm, acc, near_ref, rights_ref, sems):
    slots, terms, peers = rindex_ref.shape
    senders, height, _ = moved_ref.shape
    sector = height // terms
    rights = rights_ref.shape[0]
    get_rights = pltpu.make_async_copy(parts_hbm.at[pl.ds(parts_hbm.shape[0] - rights, rights)], rights_ref, sems.at[0])
    get_rights.start()
    slabs = []
    for k in range(acc.shape[0] // height):
        near = turned_hbm.at[senders + k, pl.ds(0, height)]
        slabs.append(pltpu.make_async_copy(near, near_ref.at[pl.ds(k * height, height)], sems.at[1 + k]))
        slabs[k].start()
    acc[...] = jnp.zeros_like(acc)
    get_rights.wait()

    def right_step(i, carry):
        slot, peer = i % slots, member(i // slots, peers)
        for g in range(terms):
            right = rights_ref[rindex_ref[slot, g, peer]]
            spot = pl.multiple_of(out_index_ref[slot, g, peer] * sector, sector)
            acc[pl.ds(spot, sector)] += product(moved_ref[i, g * sector : (g + 1) * sector], twice(right))
        return carry

    lax.fori_loop(0, senders, right_step, 0, unroll=4)
    for copy in slabs:
        copy.wait()
    for b in range(acc.shape[0] // sector):
        start = (b // SUB) * (SUB * sector) + b % SUB
        part = slice(b * sector, (b + 1) * sector)
        hpsi_rows[pl.ds(start, sector, stride=SUB), :] = acc[part] + near_ref[part]
    put = pltpu.make_async_copy(hpsi_rows, hpsi_hbm, sems.at[0])
    put.start()
    put.wait()


def residual_kernel(sums_ref, hpsi_rows, psi_rows, out_ref):
    total = jnp.sum(sums_ref[...], axis=0)
    lane = lax.broadcasted_iota(jnp.int32, total.shape, 1)
    first = lane < total.shape[1] // 2
    corr = jnp.sum(jnp.where(first, total, 0.0), axis=1, keepdims=True)
    norm = jnp.sum(jnp.where(first, 0.0, total), axis=1, keepdims=True)
    theta = corr / (norm + 1e-06)
    out_ref[...] = hpsi_rows[...] - theta * psi_rows[...]


def shards(
    psi,
    left_env,
    right_env,
    send_block,
    send_left,
    send_live,
    recv_right,
    recv_out,
    loc_block,
    loc_left,
    loc_right,
):
    peers = lax.axis_size("renv")
    owned = psi.shape[0]
    sector = math.isqrt(psi.shape[1])
    slots = send_block.shape[1]
    terms = send_left.shape[2]
    count = peers * slots
    lefts = left_env.shape[0]
    rights = right_env.shape[0]
    height = sector + SUB
    psi_rows = as_rows(psi, sector)
    left_rows = as_rows(left_env, sector)
    right_rows = as_rows(right_env, sector)
    by_slot = [index.transpose(1, 2, 0) for index in (send_left, send_live, recv_right, recv_out)]
    blocks = jax.ShapeDtypeStruct((count, height, sector), F32)
    rows = jax.ShapeDtypeStruct((owned * sector, sector), F32)

    sent = pl.pallas_call(
        gather_kernel,
        out_shape=blocks,
        in_specs=[SMEM] * 3 + [VMEM],
        out_specs=HBM,
        scratch_shapes=[pltpu.VMEM(blocks.shape, F32), pltpu.SemaphoreType.DMA((count,))],
        compiler_params=roomy(56),
        name="gather_blocks",
    )(send_block.reshape(-1), *by_slot[:2], psi_rows)
    came = lax.all_to_all(
        sent.reshape(peers, slots, height, sector),
        "renv",
        split_axis=0,
        concat_axis=0,
        tiled=True,
        axis_index_groups=[[member(position, peers) for position in range(peers)]],
    )
    came = came.reshape(count, height, sector)

    slabs = owned // terms
    turned, parts = pl.pallas_call(
        prepare_kernel,
        out_shape=(
            jax.ShapeDtypeStruct((count + slabs, terms * sector + SUB, sector), F32),
            jax.ShapeDtypeStruct((lefts + rights, sector, 2 * sector), BF16),
        ),
        in_specs=[HBM] + [SMEM] * 5 + [VMEM] * 3,
        out_specs=(VMEM,) * 2,
        scratch_shapes=[
            pltpu.VMEM((owned, sector, sector), F32),
            pltpu.VMEM((owned, sector, 2 * sector), BF16),
            pltpu.VMEM((rights, 2 * sector, 2 * sector), BF16),
            pltpu.VMEM((loc_block.shape[0], sector, 2 * sector), BF16),
        ],
        compiler_params=roomy(56),
        cost_estimate=LIGHT,
        name="prepare",
    )(sent, *by_slot[2:], loc_block, loc_left, loc_right, psi_rows, right_rows, left_rows)

    chunk = math.gcd(count, 16)
    moved = []
    sums = 0.0
    for first in range(0, count, chunk):
        part = slice(first, first + chunk) if count > chunk else slice(None)
        kept, share = pl.pallas_call(
            lambda *refs: arrive_kernel(terms, *refs),
            out_shape=(
                jax.ShapeDtypeStruct((chunk, terms * sector, 2 * sector), BF16),
                jax.ShapeDtypeStruct((peers, 1, sector), F32),
            ),
            in_specs=[VMEM] + [HBM] * 2,
            out_specs=(VMEM,) * 2,
            scratch_shapes=[
                pltpu.SMEM((chunk, SUB, sector), F32),
                pltpu.VMEM((chunk, terms * sector + SUB, sector), F32),
                pltpu.VMEM((lefts, sector, 2 * sector), BF16),
                pltpu.VMEM((chunk, 2 * sector, 2 * sector), BF16),
                pltpu.SemaphoreType.DMA((6,)),
            ],
            compiler_params=roomy(50),
            name="arrive",
        )(came[part], turned if count == chunk else turned[part], parts)
        moved.append(kept)
        sums = share if count == chunk else sums + share
    moved = moved[0] if len(moved) == 1 else jnp.concatenate(moved, axis=0)
    order = [member(position, peers) for position in range(peers)]
    totals = lax.all_to_all(sums, "renv", split_axis=0, concat_axis=0, tiled=True, axis_index_groups=[order])

    hpsi_rows, hpsi = pl.pallas_call(
        remote_kernel,
        out_shape=(rows, rows),
        in_specs=[SMEM] * 2 + [VMEM] + [HBM] * 2,
        out_specs=(VMEM, HBM),
        scratch_shapes=[
            pltpu.VMEM(rows.shape, F32),
            pltpu.VMEM(rows.shape, F32),
            pltpu.VMEM((rights, sector, 2 * sector), BF16),
            pltpu.SemaphoreType.DMA((1 + slabs,)),
        ],
        compiler_params=roomy(50),
        cost_estimate=pl.CostEstimate(flops=4 * 10**9, bytes_accessed=6 * MIB, transcendentals=0),
        name="remote_terms",
    )(*by_slot[2:], moved, turned, parts)

    residual_rows = pl.pallas_call(
        residual_kernel,
        out_shape=rows,
        in_specs=[VMEM] * 3,
        out_specs=VMEM,
        compiler_params=roomy(16),
        name="residual",
    )(totals, hpsi_rows, psi_rows)
    return (from_rows(hpsi, owned), from_rows(residual_rows, owned))


def solution(mesh):
    placed = (
        P(("groups", "renv"), None),
        P("groups", None),
        P(("groups", "renv"), None),
        P(("groups", "renv"), None),
        P(("groups", "renv"), None, None),
        P(("groups", "renv"), None, None),
        P(("groups", "renv"), None, None),
        P(("groups", "renv"), None, None),
        P(("groups", "renv")),
        P(("groups", "renv")),
        P(("groups", "renv")),
    )
    return jax.shard_map(
        shards,
        mesh=mesh,
        in_specs=placed,
        out_specs=(P(("groups", "renv"), None), P(("groups", "renv"), None)),
        check_vma=False,
    )
```

```python
import math

import jax
import jax.numpy as jnp
from jax import lax
from jax.experimental import pallas as pl
from jax.experimental.pallas import tpu as pltpu
from jax.sharding import PartitionSpec as P

F32 = jnp.float32
BF16 = jnp.bfloat16
SUB = 8
VMEM = pl.BlockSpec(memory_space=pltpu.VMEM)
SMEM = pl.BlockSpec(memory_space=pltpu.SMEM)
HBM = pl.BlockSpec(memory_space=pltpu.HBM)
MIB = 2**20
LIGHT = pl.CostEstimate(flops=10**6, bytes_accessed=2**16, transcendentals=0)


def as_rows(blocks, sector):
    count = blocks.shape[0]
    split = blocks.reshape(count // SUB, SUB, sector, sector)
    return split.transpose(0, 2, 1, 3).reshape(count * sector, sector)


def from_rows(rows, count):
    sector = rows.shape[1]
    split = rows.reshape(count // SUB, sector, SUB, sector)
    return split.transpose(0, 2, 1, 3).reshape(count, sector * sector)


def pick(ref, block):
    sector = ref.shape[1]
    start = (block // SUB) * (SUB * sector) + block % SUB
    return ref[pl.ds(start, sector, stride=SUB), :]


def halves(mat):
    high = mat.astype(BF16)
    low = (mat - high.astype(F32)).astype(BF16)
    return jnp.concatenate([high, low], axis=1)


def doubled(mat):
    both = halves(mat)
    return jnp.concatenate([both, both], axis=0)


def product(left, right):
    sector = right.shape[1] // 2
    wide = jnp.dot(left, right, preferred_element_type=F32)
    return wide[:, :sector] + wide[:, sector:]


def stacked(mat):
    high = mat.astype(BF16)
    low = (mat - high.astype(F32)).astype(BF16)
    rows = [jnp.concatenate([part, part], axis=1) for part in (high, low)]
    return jnp.concatenate(rows, axis=0)


def product_t(left, right):
    sector = right.shape[0] // 2
    wide = lax.dot_general(left, right, (((1,), (1,)), ((), ())), preferred_element_type=F32)
    return wide[:, :sector] + wide[:, sector:]


def twice(part):
    return jnp.concatenate([part, part], axis=0)


def roomy(mib):
    return pltpu.CompilerParams(vmem_limit_bytes=mib * MIB)


def member(position, peers):
    if peers % 2:
        return position
    middle = peers // 2 + 1
    return position + middle * (position == 0) - 1 * (position > 0) + 1 * (position > middle)


def gather_kernel(block_ref, left_ref, live_ref, psi_rows, out_hbm, stage, sems):
    slots, terms, peers = left_ref.shape
    sector = psi_rows.shape[1]
    lane = lax.broadcasted_iota(jnp.int32, (SUB, sector), 1)
    puts = []
    for i in range(stage.shape[0]):
        slot, peer = i % slots, member(i // slots, peers)
        stage[i, :sector] = pick(psi_rows, block_ref[peer * slots + slot])
        values = jnp.zeros(lane.shape, jnp.int32)
        for g in range(terms):
            values = jnp.where(lane == g, left_ref[slot, g, peer], values)
            values = jnp.where(lane == terms + g, live_ref[slot, g, peer], values)
        stage[i, sector:] = values.astype(F32)
        put = pltpu.make_async_copy(stage.at[i], out_hbm.at[i], sems.at[i])
        put.start()
        puts.append(put)
    for put in puts:
        put.wait()


def prepare_kernel(
    sent_hbm,
    rindex_ref,
    out_index_ref,
    block_ref,
    left_ref,
    right_ref,
    psi_rows,
    right_rows,
    left_rows,
    turned_ref,
    parts_ref,
    near_ref,
    psis_ref,
    stacks_ref,
    moved_ref,
):
    slots, terms, peers = rindex_ref.shape
    sector = psi_rows.shape[1]

    rights = right_rows.shape[0] // sector
    lefts = left_rows.shape[0] // sector

    def split_right(i, carry):
        mat = pick(right_rows, i)
        parts_ref[lefts + i] = halves(mat)
        stacks_ref[i] = stacked(mat)
        return carry

    lax.fori_loop(0, rights, split_right, 0, unroll=4)

    def split_psi(i, carry):
        psis_ref[i] = halves(pick(psi_rows, i))
        return carry

    lax.fori_loop(0, psis_ref.shape[0], split_psi, 0, unroll=4)

    def turn(i, carry):
        slot, peer = i % slots, member(i // slots, peers)
        for g in range(terms):
            right = stacks_ref[rindex_ref[slot, g, peer]]
            psi = psis_ref[out_index_ref[slot, g, peer]]
            turned_ref[i, g * sector : (g + 1) * sector] = product_t(psi, right)
        turned_ref[i, terms * sector :] = jnp.zeros((SUB, sector), F32)
        return carry

    slabs = near_ref.shape[0] // terms
    senders = turned_ref.shape[0] - slabs
    lax.fori_loop(0, senders, turn, 0, unroll=4)

    def split_left(i, carry):
        parts_ref[i] = halves(pick(left_rows, i))
        return carry

    lax.fori_loop(0, lefts, split_left, 0, unroll=8)

    def left_step(k, carry):
        moved_ref[k] = halves(product(parts_ref[left_ref[k]], twice(psis_ref[block_ref[k]])))
        return carry

    lax.fori_loop(0, block_ref.shape[0], left_step, 0, unroll=8)
    near_ref[...] = jnp.zeros_like(near_ref)

    def right_step(k, carry):
        near_ref[block_ref[k]] += product(moved_ref[k], twice(parts_ref[lefts + right_ref[k]]))
        return carry

    lax.fori_loop(0, block_ref.shape[0], right_step, 0, unroll=8)
    corr = jnp.zeros((1, sector), F32)
    norm = jnp.zeros((1, sector), F32)
    for b in range(near_ref.shape[0]):
        mat = pick(psi_rows, b)
        turned_ref[senders + b // terms, (b % terms) * sector : (b % terms + 1) * sector] = near_ref[b]
        corr += jnp.sum(mat * near_ref[b], axis=0, keepdims=True)
        norm += jnp.sum(mat * mat, axis=0, keepdims=True)
    row = lax.broadcasted_iota(jnp.int32, (SUB, sector), 0)
    turned_ref[0, terms * sector :] = jnp.where(row == 0, corr, jnp.where(row == 1, norm, 0.0))


def arrive_kernel(terms, came_ref, turned_hbm, parts_hbm, moved_ref, sums_ref, marks, turned_ref, lefts_ref, weights_ref, sems):
    count, height, sector = came_ref.shape
    get_marks = pltpu.make_async_copy(came_ref.at[:, pl.ds(sector, height - sector)], marks, sems.at[0])
    get_lefts = pltpu.make_async_copy(parts_hbm.at[pl.ds(0, lefts_ref.shape[0])], lefts_ref, sems.at[1])
    quarter = count // math.gcd(count, 4)
    spans = [pl.ds(first, quarter) for first in range(0, count, quarter)]
    get_turned = [
        pltpu.make_async_copy(turned_hbm.at[span], turned_ref.at[span], sems.at[2 + k]) for k, span in enumerate(spans)
    ]
    for copy in (get_marks, get_lefts, *get_turned):
        copy.start()

    def split(i, carry):
        weights_ref[i] = doubled(came_ref[i, :sector])
        return carry

    lax.fori_loop(0, count, split, 0, unroll=4)
    get_marks.wait()
    get_lefts.wait()

    def block(i, total):
        stack = [lefts_ref[marks[i, 0, g].astype(jnp.int32)] for g in range(terms)]
        moved = product(jnp.concatenate(stack, axis=0), weights_ref[i])
        for g in range(terms):
            part = slice(g * sector, (g + 1) * sector)
            one = moved[part] * marks[i, 0, terms + g]
            moved_ref[i, part] = halves(one)
            total += jnp.sum((one * turned_ref[i, part]).reshape(-1, SUB, sector), axis=0)
        return total

    total = jnp.zeros((SUB, sector), F32)
    for k, copy in enumerate(get_turned):
        copy.wait()
        total = lax.fori_loop(k * quarter, (k + 1) * quarter, block, total, unroll=4)
    corr = jnp.sum(total, axis=0, keepdims=True)
    row = lax.broadcasted_iota(jnp.int32, total.shape, 0)
    mine = turned_ref[0, terms * sector :] + jnp.where(row == 0, corr, 0.0)
    folded = mine + pltpu.roll(mine, sector // 2, 1)
    lane = lax.broadcasted_iota(jnp.int32, (1, sector), 1)
    shared = jnp.where(lane < sector // 2, folded[0:1], folded[1:2])
    for i in range(sums_ref.shape[0]):
        sums_ref[i] = shared


def remote_kernel(rindex_ref, out_index_ref, moved_ref, turned_hbm, parts_hbm, hpsi_rows, hpsi_hbm, acc, near_ref, rights_ref, sems):
    slots, terms, peers = rindex_ref.shape
    senders, height, _ = moved_ref.shape
    sector = height // terms
    rights = rights_ref.shape[0]
    get_rights = pltpu.make_async_copy(parts_hbm.at[pl.ds(parts_hbm.shape[0] - rights, rights)], rights_ref, sems.at[0])
    get_rights.start()
    slabs = []
    for k in range(acc.shape[0] // height):
        near = turned_hbm.at[senders + k, pl.ds(0, height)]
        slabs.append(pltpu.make_async_copy(near, near_ref.at[pl.ds(k * height, height)], sems.at[1 + k]))
        slabs[k].start()
    acc[...] = jnp.zeros_like(acc)
    get_rights.wait()

    def right_step(i, carry):
        slot, peer = i % slots, member(i // slots, peers)
        for g in range(terms):
            right = rights_ref[rindex_ref[slot, g, peer]]
            spot = pl.multiple_of(out_index_ref[slot, g, peer] * sector, sector)
            acc[pl.ds(spot, sector)] += product(moved_ref[i, g * sector : (g + 1) * sector], twice(right))
        return carry

    lax.fori_loop(0, senders, right_step, 0, unroll=4)
    for copy in slabs:
        copy.wait()
    for b in range(acc.shape[0] // sector):
        start = (b // SUB) * (SUB * sector) + b % SUB
        part = slice(b * sector, (b + 1) * sector)
        hpsi_rows[pl.ds(start, sector, stride=SUB), :] = acc[part] + near_ref[part]
    put = pltpu.make_async_copy(hpsi_rows, hpsi_hbm, sems.at[0])
    put.start()
    put.wait()


def residual_kernel(sums_ref, hpsi_rows, psi_rows, out_ref):
    total = jnp.sum(sums_ref[...], axis=0)
    lane = lax.broadcasted_iota(jnp.int32, total.shape, 1)
    first = lane < total.shape[1] // 2
    corr = jnp.sum(jnp.where(first, total, 0.0), axis=1, keepdims=True)
    norm = jnp.sum(jnp.where(first, 0.0, total), axis=1, keepdims=True)
    theta = corr / (norm + 1e-06)
    out_ref[...] = hpsi_rows[...] - theta * psi_rows[...]


def shards(
    psi,
    left_env,
    right_env,
    send_block,
    send_left,
    send_live,
    recv_right,
    recv_out,
    loc_block,
    loc_left,
    loc_right,
):
    peers = lax.axis_size("renv")
    owned = psi.shape[0]
    sector = math.isqrt(psi.shape[1])
    slots = send_block.shape[1]
    terms = send_left.shape[2]
    count = peers * slots
    lefts = left_env.shape[0]
    rights = right_env.shape[0]
    height = sector + SUB
    psi_rows = as_rows(psi, sector)
    left_rows = as_rows(left_env, sector)
    right_rows = as_rows(right_env, sector)
    by_slot = [index.transpose(1, 2, 0) for index in (send_left, send_live, recv_right, recv_out)]
    blocks = jax.ShapeDtypeStruct((count, height, sector), F32)
    rows = jax.ShapeDtypeStruct((owned * sector, sector), F32)

    sent = pl.pallas_call(
        gather_kernel,
        out_shape=blocks,
        in_specs=[SMEM] * 3 + [VMEM],
        out_specs=HBM,
        scratch_shapes=[pltpu.VMEM(blocks.shape, F32), pltpu.SemaphoreType.DMA((count,))],
        compiler_params=roomy(56),
        name="gather_blocks",
    )(send_block.reshape(-1), *by_slot[:2], psi_rows)
    came = lax.all_to_all(
        sent.reshape(peers, slots, height, sector),
        "renv",
        split_axis=0,
        concat_axis=0,
        tiled=True,
        axis_index_groups=[[member(position, peers) for position in range(peers)]],
    )
    came = came.reshape(count, height, sector)

    slabs = owned // terms
    turned, parts = pl.pallas_call(
        prepare_kernel,
        out_shape=(
            jax.ShapeDtypeStruct((count + slabs, terms * sector + SUB, sector), F32),
            jax.ShapeDtypeStruct((lefts + rights, sector, 2 * sector), BF16),
        ),
        in_specs=[HBM] + [SMEM] * 5 + [VMEM] * 3,
        out_specs=(VMEM,) * 2,
        scratch_shapes=[
            pltpu.VMEM((owned, sector, sector), F32),
            pltpu.VMEM((owned, sector, 2 * sector), BF16),
            pltpu.VMEM((rights, 2 * sector, 2 * sector), BF16),
            pltpu.VMEM((loc_block.shape[0], sector, 2 * sector), BF16),
        ],
        compiler_params=roomy(56),
        cost_estimate=LIGHT,
        name="prepare",
    )(sent, *by_slot[2:], loc_block, loc_left, loc_right, psi_rows, right_rows, left_rows)

    chunk = math.gcd(count, 16)
    moved = []
    sums = 0.0
    for first in range(0, count, chunk):
        part = slice(first, first + chunk) if count > chunk else slice(None)
        kept, share = pl.pallas_call(
            lambda *refs: arrive_kernel(terms, *refs),
            out_shape=(
                jax.ShapeDtypeStruct((chunk, terms * sector, 2 * sector), BF16),
                jax.ShapeDtypeStruct((peers, 1, sector), F32),
            ),
            in_specs=[VMEM] + [HBM] * 2,
            out_specs=(VMEM,) * 2,
            scratch_shapes=[
                pltpu.SMEM((chunk, SUB, sector), F32),
                pltpu.VMEM((chunk, terms * sector + SUB, sector), F32),
                pltpu.VMEM((lefts, sector, 2 * sector), BF16),
                pltpu.VMEM((chunk, 2 * sector, 2 * sector), BF16),
                pltpu.SemaphoreType.DMA((6,)),
            ],
            compiler_params=roomy(50),
            name="arrive",
        )(came[part], turned if count == chunk else turned[part], parts)
        moved.append(kept)
        sums = share if count == chunk else sums + share
    moved = moved[0] if len(moved) == 1 else jnp.concatenate(moved, axis=0)
    order = [member(position, peers) for position in range(peers)]
    totals = lax.all_to_all(sums, "renv", split_axis=0, concat_axis=0, tiled=True, axis_index_groups=[order])

    hpsi_rows, hpsi = pl.pallas_call(
        remote_kernel,
        out_shape=(rows, rows),
        in_specs=[SMEM] * 2 + [VMEM] + [HBM] * 2,
        out_specs=(VMEM, HBM),
        scratch_shapes=[
            pltpu.VMEM(rows.shape, F32),
            pltpu.VMEM(rows.shape, F32),
            pltpu.VMEM((rights, sector, 2 * sector), BF16),
            pltpu.SemaphoreType.DMA((1 + slabs,)),
        ],
        compiler_params=roomy(50),
        cost_estimate=pl.CostEstimate(flops=4 * 10**9, bytes_accessed=6 * MIB, transcendentals=0),
        name="remote_terms",
    )(*by_slot[2:], moved, turned, parts)

    residual_rows = pl.pallas_call(
        residual_kernel,
        out_shape=rows,
        in_specs=[VMEM] * 3,
        out_specs=VMEM,
        compiler_params=roomy(16),
        name="residual",
    )(totals, hpsi_rows, psi_rows)
    return (from_rows(hpsi, owned), from_rows(residual_rows, owned))


def solution(mesh):
    placed = (
        P(("groups", "renv"), None),
        P("groups", None),
        P(("groups", "renv"), None),
        P(("groups", "renv"), None),
        P(("groups", "renv"), None, None),
        P(("groups", "renv"), None, None),
        P(("groups", "renv"), None, None),
        P(("groups", "renv"), None, None),
        P(("groups", "renv")),
        P(("groups", "renv")),
        P(("groups", "renv")),
    )
    return jax.shard_map(
        shards,
        mesh=mesh,
        in_specs=placed,
        out_specs=(P(("groups", "renv"), None), P(("groups", "renv"), None)),
        check_vma=False,
    )
```

```python
import math

import jax
import jax.numpy as jnp
from jax import lax
from jax.experimental import pallas as pl
from jax.experimental.pallas import tpu as pltpu
from jax.sharding import PartitionSpec as P

F32 = jnp.float32
BF16 = jnp.bfloat16
SUB = 8
VMEM = pl.BlockSpec(memory_space=pltpu.VMEM)
SMEM = pl.BlockSpec(memory_space=pltpu.SMEM)
HBM = pl.BlockSpec(memory_space=pltpu.HBM)
MIB = 2**20
LIGHT = pl.CostEstimate(flops=10**6, bytes_accessed=2**16, transcendentals=0)


def as_rows(blocks, sector):
    count = blocks.shape[0]
    split = blocks.reshape(count // SUB, SUB, sector, sector)
    return split.transpose(0, 2, 1, 3).reshape(count * sector, sector)


def from_rows(rows, count):
    sector = rows.shape[1]
    split = rows.reshape(count // SUB, sector, SUB, sector)
    return split.transpose(0, 2, 1, 3).reshape(count, sector * sector)


def pick(ref, block):
    sector = ref.shape[1]
    start = (block // SUB) * (SUB * sector) + block % SUB
    return ref[pl.ds(start, sector, stride=SUB), :]


def halves(mat):
    high = mat.astype(BF16)
    low = (mat - high.astype(F32)).astype(BF16)
    return jnp.concatenate([high, low], axis=1)


def doubled(mat):
    both = halves(mat)
    return jnp.concatenate([both, both], axis=0)


def product(left, right):
    sector = right.shape[1] // 2
    wide = jnp.dot(left, right, preferred_element_type=F32)
    return wide[:, :sector] + wide[:, sector:]


def stacked(mat):
    high = mat.astype(BF16)
    low = (mat - high.astype(F32)).astype(BF16)
    rows = [jnp.concatenate([part, part], axis=1) for part in (high, low)]
    return jnp.concatenate(rows, axis=0)


def product_t(left, right):
    sector = right.shape[0] // 2
    wide = lax.dot_general(left, right, (((1,), (1,)), ((), ())), preferred_element_type=F32)
    return wide[:, :sector] + wide[:, sector:]


def twice(part):
    return jnp.concatenate([part, part], axis=0)


def roomy(mib):
    return pltpu.CompilerParams(vmem_limit_bytes=mib * MIB)


def member(position, peers):
    if peers % 2:
        return position
    middle = peers // 2 + 1
    return position + middle * (position == 0) - 1 * (position > 0) + 1 * (position > middle)


def gather_kernel(block_ref, left_ref, live_ref, psi_rows, out_hbm, stage, sems):
    slots, terms, peers = left_ref.shape
    sector = psi_rows.shape[1]
    lane = lax.broadcasted_iota(jnp.int32, (SUB, sector), 1)
    puts = []
    for i in range(stage.shape[0]):
        slot, peer = i % slots, member(i // slots, peers)
        stage[i, :sector] = pick(psi_rows, block_ref[peer * slots + slot])
        values = jnp.zeros(lane.shape, jnp.int32)
        for g in range(terms):
            values = jnp.where(lane == g, left_ref[slot, g, peer], values)
            values = jnp.where(lane == terms + g, live_ref[slot, g, peer], values)
        stage[i, sector:] = values.astype(F32)
        put = pltpu.make_async_copy(stage.at[i], out_hbm.at[i], sems.at[i])
        put.start()
        puts.append(put)
    for put in puts:
        put.wait()


def prepare_kernel(
    sent_hbm,
    rindex_ref,
    out_index_ref,
    block_ref,
    left_ref,
    right_ref,
    psi_rows,
    right_rows,
    left_rows,
    turned_ref,
    parts_ref,
    near_ref,
    psis_ref,
    stacks_ref,
    moved_ref,
):
    slots, terms, peers = rindex_ref.shape
    sector = psi_rows.shape[1]

    rights = right_rows.shape[0] // sector
    lefts = left_rows.shape[0] // sector

    def split_right(i, carry):
        mat = pick(right_rows, i)
        parts_ref[lefts + i] = halves(mat)
        stacks_ref[i] = stacked(mat)
        return carry

    lax.fori_loop(0, rights, split_right, 0, unroll=4)

    def split_psi(i, carry):
        psis_ref[i] = halves(pick(psi_rows, i))
        return carry

    lax.fori_loop(0, psis_ref.shape[0], split_psi, 0, unroll=4)

    def turn(i, carry):
        slot, peer = i % slots, member(i // slots, peers)
        for g in range(terms):
            right = stacks_ref[rindex_ref[slot, g, peer]]
            psi = psis_ref[out_index_ref[slot, g, peer]]
            turned_ref[i, g * sector : (g + 1) * sector] = product_t(psi, right)
        turned_ref[i, terms * sector :] = jnp.zeros((SUB, sector), F32)
        return carry

    slabs = near_ref.shape[0] // terms
    senders = turned_ref.shape[0] - slabs
    lax.fori_loop(0, senders, turn, 0, unroll=4)

    def split_left(i, carry):
        parts_ref[i] = halves(pick(left_rows, i))
        return carry

    lax.fori_loop(0, lefts, split_left, 0, unroll=8)

    def left_step(k, carry):
        moved_ref[k] = halves(product(parts_ref[left_ref[k]], twice(psis_ref[block_ref[k]])))
        return carry

    lax.fori_loop(0, block_ref.shape[0], left_step, 0, unroll=8)
    near_ref[...] = jnp.zeros_like(near_ref)

    def right_step(k, carry):
        near_ref[block_ref[k]] += product(moved_ref[k], twice(parts_ref[lefts + right_ref[k]]))
        return carry

    lax.fori_loop(0, block_ref.shape[0], right_step, 0, unroll=8)
    corr = jnp.zeros((1, sector), F32)
    norm = jnp.zeros((1, sector), F32)
    for b in range(near_ref.shape[0]):
        mat = pick(psi_rows, b)
        turned_ref[senders + b // terms, (b % terms) * sector : (b % terms + 1) * sector] = near_ref[b]
        corr += jnp.sum(mat * near_ref[b], axis=0, keepdims=True)
        norm += jnp.sum(mat * mat, axis=0, keepdims=True)
    row = lax.broadcasted_iota(jnp.int32, (SUB, sector), 0)
    turned_ref[0, terms * sector :] = jnp.where(row == 0, corr, jnp.where(row == 1, norm, 0.0))


def arrive_kernel(terms, came_ref, turned_hbm, parts_hbm, moved_ref, sums_ref, marks, turned_ref, lefts_ref, weights_ref, sems):
    count, height, sector = came_ref.shape
    get_marks = pltpu.make_async_copy(came_ref.at[:, pl.ds(sector, height - sector)], marks, sems.at[0])
    get_lefts = pltpu.make_async_copy(parts_hbm.at[pl.ds(0, lefts_ref.shape[0])], lefts_ref, sems.at[1])
    quarter = count // math.gcd(count, 4)
    spans = [pl.ds(first, quarter) for first in range(0, count, quarter)]
    get_turned = [
        pltpu.make_async_copy(turned_hbm.at[span], turned_ref.at[span], sems.at[2 + k]) for k, span in enumerate(spans)
    ]
    for copy in (get_marks, get_lefts, *get_turned):
        copy.start()

    def split(i, carry):
        weights_ref[i] = doubled(came_ref[i, :sector])
        return carry

    lax.fori_loop(0, count, split, 0, unroll=4)
    get_marks.wait()
    get_lefts.wait()

    def block(i, total):
        stack = [lefts_ref[marks[i, 0, g].astype(jnp.int32)] for g in range(terms)]
        moved = product(jnp.concatenate(stack, axis=0), weights_ref[i])
        for g in range(terms):
            part = slice(g * sector, (g + 1) * sector)
            one = moved[part] * marks[i, 0, terms + g]
            moved_ref[i, part] = halves(one)
            total += jnp.sum((one * turned_ref[i, part]).reshape(-1, SUB, sector), axis=0)
        return total

    total = jnp.zeros((SUB, sector), F32)
    for k, copy in enumerate(get_turned):
        copy.wait()
        total = lax.fori_loop(k * quarter, (k + 1) * quarter, block, total, unroll=4)
    corr = jnp.sum(total, axis=0, keepdims=True)
    row = lax.broadcasted_iota(jnp.int32, total.shape, 0)
    mine = turned_ref[0, terms * sector :] + jnp.where(row == 0, corr, 0.0)
    folded = mine + pltpu.roll(mine, sector // 2, 1)
    lane = lax.broadcasted_iota(jnp.int32, (1, sector), 1)
    shared = jnp.where(lane < sector // 2, folded[0:1], folded[1:2])
    for i in range(sums_ref.shape[0]):
        sums_ref[i] = shared


def remote_kernel(rindex_ref, out_index_ref, moved_ref, turned_hbm, parts_hbm, hpsi_rows, acc, rights_ref, sems):
    slots, terms, peers = rindex_ref.shape
    senders, height, _ = moved_ref.shape
    sector = height // terms
    rights = rights_ref.shape[0]
    copies = [pltpu.make_async_copy(parts_hbm.at[pl.ds(parts_hbm.shape[0] - rights, rights)], rights_ref, sems.at[0])]
    for k in range(acc.shape[0] // height):
        near = turned_hbm.at[senders + k, pl.ds(0, height)]
        copies.append(pltpu.make_async_copy(near, acc.at[pl.ds(k * height, height)], sems.at[1 + k]))
    for copy in copies:
        copy.start()
    for copy in copies:
        copy.wait()

    def right_step(i, carry):
        slot, peer = i % slots, member(i // slots, peers)
        for g in range(terms):
            right = rights_ref[rindex_ref[slot, g, peer]]
            spot = pl.multiple_of(out_index_ref[slot, g, peer] * sector, sector)
            acc[pl.ds(spot, sector)] += product(moved_ref[i, g * sector : (g + 1) * sector], twice(right))
        return carry

    lax.fori_loop(0, senders, right_step, 0, unroll=8)
    for b in range(acc.shape[0] // sector):
        start = (b // SUB) * (SUB * sector) + b % SUB
        hpsi_rows[pl.ds(start, sector, stride=SUB), :] = acc[b * sector : (b + 1) * sector]


def residual_kernel(sums_ref, hpsi_rows, psi_rows, hpsi_hbm, out_hbm, out_ref, sems):
    put_hpsi = pltpu.make_async_copy(hpsi_rows, hpsi_hbm, sems.at[0])
    put_hpsi.start()
    total = jnp.sum(sums_ref[...], axis=0)
    lane = lax.broadcasted_iota(jnp.int32, total.shape, 1)
    first = lane < total.shape[1] // 2
    corr = jnp.sum(jnp.where(first, total, 0.0), axis=1, keepdims=True)
    norm = jnp.sum(jnp.where(first, 0.0, total), axis=1, keepdims=True)
    theta = corr / (norm + 1e-06)
    out_ref[...] = hpsi_rows[...] - theta * psi_rows[...]
    put_out = pltpu.make_async_copy(out_ref, out_hbm, sems.at[1])
    put_out.start()
    put_hpsi.wait()
    put_out.wait()


def shards(
    psi,
    left_env,
    right_env,
    send_block,
    send_left,
    send_live,
    recv_right,
    recv_out,
    loc_block,
    loc_left,
    loc_right,
):
    peers = lax.axis_size("renv")
    owned = psi.shape[0]
    sector = math.isqrt(psi.shape[1])
    slots = send_block.shape[1]
    terms = send_left.shape[2]
    count = peers * slots
    lefts = left_env.shape[0]
    rights = right_env.shape[0]
    height = sector + SUB
    psi_rows = as_rows(psi, sector)
    left_rows = as_rows(left_env, sector)
    right_rows = as_rows(right_env, sector)
    by_slot = [index.transpose(1, 2, 0) for index in (send_left, send_live, recv_right, recv_out)]
    blocks = jax.ShapeDtypeStruct((count, height, sector), F32)
    rows = jax.ShapeDtypeStruct((owned * sector, sector), F32)

    sent = pl.pallas_call(
        gather_kernel,
        out_shape=blocks,
        in_specs=[SMEM] * 3 + [VMEM],
        out_specs=HBM,
        scratch_shapes=[pltpu.VMEM(blocks.shape, F32), pltpu.SemaphoreType.DMA((count,))],
        compiler_params=roomy(56),
        name="gather_blocks",
    )(send_block.reshape(-1), *by_slot[:2], psi_rows)
    came = lax.all_to_all(
        sent.reshape(peers, slots, height, sector),
        "renv",
        split_axis=0,
        concat_axis=0,
        tiled=True,
        axis_index_groups=[[member(position, peers) for position in range(peers)]],
    )
    came = came.reshape(count, height, sector)

    slabs = owned // terms
    turned, parts = pl.pallas_call(
        prepare_kernel,
        out_shape=(
            jax.ShapeDtypeStruct((count + slabs, terms * sector + SUB, sector), F32),
            jax.ShapeDtypeStruct((lefts + rights, sector, 2 * sector), BF16),
        ),
        in_specs=[HBM] + [SMEM] * 5 + [VMEM] * 3,
        out_specs=(VMEM,) * 2,
        scratch_shapes=[
            pltpu.VMEM((owned, sector, sector), F32),
            pltpu.VMEM((owned, sector, 2 * sector), BF16),
            pltpu.VMEM((rights, 2 * sector, 2 * sector), BF16),
            pltpu.VMEM((loc_block.shape[0], sector, 2 * sector), BF16),
        ],
        compiler_params=roomy(56),
        cost_estimate=LIGHT,
        name="prepare",
    )(sent, *by_slot[2:], loc_block, loc_left, loc_right, psi_rows, right_rows, left_rows)

    chunk = math.gcd(count, 16)
    moved = []
    sums = 0.0
    for first in range(0, count, chunk):
        part = slice(first, first + chunk) if count > chunk else slice(None)
        kept, share = pl.pallas_call(
            lambda *refs: arrive_kernel(terms, *refs),
            out_shape=(
                jax.ShapeDtypeStruct((chunk, terms * sector, 2 * sector), BF16),
                jax.ShapeDtypeStruct((peers, 1, sector), F32),
            ),
            in_specs=[VMEM] + [HBM] * 2,
            out_specs=(VMEM,) * 2,
            scratch_shapes=[
                pltpu.SMEM((chunk, SUB, sector), F32),
                pltpu.VMEM((chunk, terms * sector + SUB, sector), F32),
                pltpu.VMEM((lefts, sector, 2 * sector), BF16),
                pltpu.VMEM((chunk, 2 * sector, 2 * sector), BF16),
                pltpu.SemaphoreType.DMA((6,)),
            ],
            compiler_params=roomy(50),
            name="arrive",
        )(came[part], turned if count == chunk else turned[part], parts)
        moved.append(kept)
        sums = share if count == chunk else sums + share
    moved = moved[0] if len(moved) == 1 else jnp.concatenate(moved, axis=0)
    order = [member(position, peers) for position in range(peers)]
    totals = lax.all_to_all(sums, "renv", split_axis=0, concat_axis=0, tiled=True, axis_index_groups=[order])

    hpsi_rows = pl.pallas_call(
        remote_kernel,
        out_shape=rows,
        in_specs=[SMEM] * 2 + [VMEM] + [HBM] * 2,
        out_specs=VMEM,
        scratch_shapes=[
            pltpu.VMEM(rows.shape, F32),
            pltpu.VMEM((rights, sector, 2 * sector), BF16),
            pltpu.SemaphoreType.DMA((1 + slabs,)),
        ],
        compiler_params=roomy(50),
        cost_estimate=pl.CostEstimate(flops=4 * 10**9, bytes_accessed=6 * MIB, transcendentals=0),
        name="remote_terms",
    )(*by_slot[2:], moved, turned, parts)

    hpsi, residual_rows = pl.pallas_call(
        residual_kernel,
        out_shape=(rows, rows),
        in_specs=[VMEM] * 3,
        out_specs=(HBM,) * 2,
        scratch_shapes=[pltpu.VMEM(rows.shape, F32), pltpu.SemaphoreType.DMA((2,))],
        compiler_params=roomy(16),
        name="residual",
    )(totals, hpsi_rows, psi_rows)
    return (from_rows(hpsi, owned), from_rows(residual_rows, owned))


def solution(mesh):
    placed = (
        P(("groups", "renv"), None),
        P("groups", None),
        P(("groups", "renv"), None),
        P(("groups", "renv"), None),
        P(("groups", "renv"), None, None),
        P(("groups", "renv"), None, None),
        P(("groups", "renv"), None, None),
        P(("groups", "renv"), None, None),
        P(("groups", "renv")),
        P(("groups", "renv")),
        P(("groups", "renv")),
    )
    return jax.shard_map(
        shards,
        mesh=mesh,
        in_specs=placed,
        out_specs=(P(("groups", "renv"), None), P(("groups", "renv"), None)),
        check_vma=False,
    )
```

```python
import math

import jax
import jax.numpy as jnp
from jax import lax
from jax.experimental import pallas as pl
from jax.experimental.pallas import tpu as pltpu
from jax.sharding import PartitionSpec as P

F32 = jnp.float32
BF16 = jnp.bfloat16
SUB = 8
VMEM = pl.BlockSpec(memory_space=pltpu.VMEM)
SMEM = pl.BlockSpec(memory_space=pltpu.SMEM)
HBM = pl.BlockSpec(memory_space=pltpu.HBM)
MIB = 2**20
LIGHT = pl.CostEstimate(flops=10**6, bytes_accessed=2**16, transcendentals=0)


def as_rows(blocks, sector):
    count = blocks.shape[0]
    split = blocks.reshape(count // SUB, SUB, sector, sector)
    return split.transpose(0, 2, 1, 3).reshape(count * sector, sector)


def from_rows(rows, count):
    sector = rows.shape[1]
    split = rows.reshape(count // SUB, sector, SUB, sector)
    return split.transpose(0, 2, 1, 3).reshape(count, sector * sector)


def pick(ref, block):
    sector = ref.shape[1]
    start = (block // SUB) * (SUB * sector) + block % SUB
    return ref[pl.ds(start, sector, stride=SUB), :]


def halves(mat):
    high = mat.astype(BF16)
    low = (mat - high.astype(F32)).astype(BF16)
    return jnp.concatenate([high, low], axis=1)


def doubled(mat):
    both = halves(mat)
    return jnp.concatenate([both, both], axis=0)


def product(left, right):
    sector = right.shape[1] // 2
    wide = jnp.dot(left, right, preferred_element_type=F32)
    return wide[:, :sector] + wide[:, sector:]


def stacked(mat):
    high = mat.astype(BF16)
    low = (mat - high.astype(F32)).astype(BF16)
    rows = [jnp.concatenate([part, part], axis=1) for part in (high, low)]
    return jnp.concatenate(rows, axis=0)


def product_t(left, right):
    sector = right.shape[0] // 2
    wide = lax.dot_general(left, right, (((1,), (1,)), ((), ())), preferred_element_type=F32)
    return wide[:, :sector] + wide[:, sector:]


def twice(part):
    return jnp.concatenate([part, part], axis=0)


def roomy(mib):
    return pltpu.CompilerParams(vmem_limit_bytes=mib * MIB)


def member(position, peers):
    if peers % 2:
        return position
    middle = peers // 2 + 1
    return position + middle * (position == 0) - 1 * (position > 0) + 1 * (position > middle)


def gather_kernel(block_ref, left_ref, live_ref, psi_rows, out_hbm, stage, sems):
    slots, terms, peers = left_ref.shape
    sector = psi_rows.shape[1]
    lane = lax.broadcasted_iota(jnp.int32, (SUB, sector), 1)
    puts = []
    for i in range(stage.shape[0]):
        slot, peer = i % slots, member(i // slots, peers)
        stage[i, :sector] = pick(psi_rows, block_ref[peer * slots + slot])
        values = jnp.zeros(lane.shape, jnp.int32)
        for g in range(terms):
            values = jnp.where(lane == g, left_ref[slot, g, peer], values)
            values = jnp.where(lane == terms + g, live_ref[slot, g, peer], values)
        stage[i, sector:] = values.astype(F32)
        put = pltpu.make_async_copy(stage.at[i], out_hbm.at[i], sems.at[i])
        put.start()
        puts.append(put)
    for put in puts:
        put.wait()


def prepare_kernel(
    sent_hbm,
    rindex_ref,
    out_index_ref,
    block_ref,
    left_ref,
    right_ref,
    psi_rows,
    right_rows,
    left_rows,
    turned_ref,
    parts_ref,
    near_ref,
    psis_ref,
    stacks_ref,
    moved_ref,
):
    slots, terms, peers = rindex_ref.shape
    sector = psi_rows.shape[1]

    rights = right_rows.shape[0] // sector
    lefts = left_rows.shape[0] // sector

    def split_right(i, carry):
        mat = pick(right_rows, i)
        parts_ref[lefts + i] = halves(mat)
        stacks_ref[i] = stacked(mat)
        return carry

    lax.fori_loop(0, rights, split_right, 0, unroll=4)

    def split_psi(i, carry):
        psis_ref[i] = halves(pick(psi_rows, i))
        return carry

    lax.fori_loop(0, psis_ref.shape[0], split_psi, 0, unroll=4)

    def turn(i, carry):
        slot, peer = i % slots, member(i // slots, peers)
        for g in range(terms):
            right = stacks_ref[rindex_ref[slot, g, peer]]
            psi = psis_ref[out_index_ref[slot, g, peer]]
            turned_ref[i, g * sector : (g + 1) * sector] = product_t(psi, right)
        turned_ref[i, terms * sector :] = jnp.zeros((SUB, sector), F32)
        return carry

    slabs = near_ref.shape[0] // terms
    senders = turned_ref.shape[0] - slabs
    lax.fori_loop(0, senders, turn, 0, unroll=4)

    def split_left(i, carry):
        parts_ref[i] = halves(pick(left_rows, i))
        return carry

    lax.fori_loop(0, lefts, split_left, 0, unroll=8)

    def left_step(k, carry):
        moved_ref[k] = halves(product(parts_ref[left_ref[k]], twice(psis_ref[block_ref[k]])))
        return carry

    lax.fori_loop(0, block_ref.shape[0], left_step, 0, unroll=8)
    near_ref[...] = jnp.zeros_like(near_ref)

    def right_step(k, carry):
        near_ref[block_ref[k]] += product(moved_ref[k], twice(parts_ref[lefts + right_ref[k]]))
        return carry

    lax.fori_loop(0, block_ref.shape[0], right_step, 0, unroll=8)
    corr = jnp.zeros((1, sector), F32)
    norm = jnp.zeros((1, sector), F32)
    for b in range(near_ref.shape[0]):
        mat = pick(psi_rows, b)
        turned_ref[senders + b // terms, (b % terms) * sector : (b % terms + 1) * sector] = near_ref[b]
        corr += jnp.sum(mat * near_ref[b], axis=0, keepdims=True)
        norm += jnp.sum(mat * mat, axis=0, keepdims=True)
    row = lax.broadcasted_iota(jnp.int32, (SUB, sector), 0)
    turned_ref[0, terms * sector :] = jnp.where(row == 0, corr, jnp.where(row == 1, norm, 0.0))


def arrive_kernel(terms, came_ref, turned_hbm, parts_hbm, moved_ref, sums_ref, marks, turned_ref, lefts_ref, weights_ref, sems):
    count, height, sector = came_ref.shape
    get_marks = pltpu.make_async_copy(came_ref.at[:, pl.ds(sector, height - sector)], marks, sems.at[0])
    get_lefts = pltpu.make_async_copy(parts_hbm.at[pl.ds(0, lefts_ref.shape[0])], lefts_ref, sems.at[1])
    quarter = count // math.gcd(count, 4)
    spans = [pl.ds(first, quarter) for first in range(0, count, quarter)]
    get_turned = [
        pltpu.make_async_copy(turned_hbm.at[span], turned_ref.at[span], sems.at[2 + k]) for k, span in enumerate(spans)
    ]
    for copy in (get_marks, get_lefts, *get_turned):
        copy.start()

    def split(i, carry):
        weights_ref[i] = doubled(came_ref[i, :sector])
        return carry

    lax.fori_loop(0, count, split, 0, unroll=4)
    get_marks.wait()
    get_lefts.wait()

    def block(i, total):
        stack = [lefts_ref[marks[i, 0, g].astype(jnp.int32)] for g in range(terms)]
        moved = product(jnp.concatenate(stack, axis=0), weights_ref[i])
        for g in range(terms):
            part = slice(g * sector, (g + 1) * sector)
            one = moved[part] * marks[i, 0, terms + g]
            moved_ref[i, part] = halves(one)
            total += jnp.sum((one * turned_ref[i, part]).reshape(-1, SUB, sector), axis=0)
        return total

    total = jnp.zeros((SUB, sector), F32)
    for k, copy in enumerate(get_turned):
        copy.wait()
        total = lax.fori_loop(k * quarter, (k + 1) * quarter, block, total, unroll=4)
    corr = jnp.sum(total, axis=0, keepdims=True)
    row = lax.broadcasted_iota(jnp.int32, total.shape, 0)
    mine = turned_ref[0, terms * sector :] + jnp.where(row == 0, corr, 0.0)
    folded = mine + pltpu.roll(mine, sector // 2, 1)
    lane = lax.broadcasted_iota(jnp.int32, (1, sector), 1)
    shared = jnp.where(lane < sector // 2, folded[0:1], folded[1:2])
    for i in range(sums_ref.shape[0]):
        sums_ref[i] = shared


def remote_kernel(rindex_ref, out_index_ref, moved_ref, turned_hbm, parts_hbm, hpsi_rows, acc, rights_ref, sems):
    slots, terms, peers = rindex_ref.shape
    senders, height, _ = moved_ref.shape
    sector = height // terms
    rights = rights_ref.shape[0]
    copies = [pltpu.make_async_copy(parts_hbm.at[pl.ds(parts_hbm.shape[0] - rights, rights)], rights_ref, sems.at[0])]
    for k in range(acc.shape[0] // height):
        near = turned_hbm.at[senders + k, pl.ds(0, height)]
        copies.append(pltpu.make_async_copy(near, acc.at[pl.ds(k * height, height)], sems.at[1 + k]))
    for copy in copies:
        copy.start()
    for copy in copies:
        copy.wait()

    def right_step(i, carry):
        slot, peer = i % slots, member(i // slots, peers)
        for g in range(terms):
            right = rights_ref[rindex_ref[slot, g, peer]]
            spot = pl.multiple_of(out_index_ref[slot, g, peer] * sector, sector)
            acc[pl.ds(spot, sector)] += product(moved_ref[i, g * sector : (g + 1) * sector], twice(right))
        return carry

    lax.fori_loop(0, senders, right_step, 0, unroll=8)
    for b in range(acc.shape[0] // sector):
        start = (b // SUB) * (SUB * sector) + b % SUB
        hpsi_rows[pl.ds(start, sector, stride=SUB), :] = acc[b * sector : (b + 1) * sector]


def residual_kernel(sums_ref, hpsi_rows, psi_rows, hpsi_hbm, out_hbm, out_ref, sems):
    put_hpsi = pltpu.make_async_copy(hpsi_rows, hpsi_hbm, sems.at[0])
    put_hpsi.start()
    total = jnp.sum(sums_ref[...], axis=0)
    lane = lax.broadcasted_iota(jnp.int32, total.shape, 1)
    first = lane < total.shape[1] // 2
    corr = jnp.sum(jnp.where(first, total, 0.0), axis=1, keepdims=True)
    norm = jnp.sum(jnp.where(first, 0.0, total), axis=1, keepdims=True)
    theta = corr / (norm + 1e-06)
    out_ref[...] = hpsi_rows[...] - theta * psi_rows[...]
    put_out = pltpu.make_async_copy(out_ref, out_hbm, sems.at[1])
    put_out.start()
    put_hpsi.wait()
    put_out.wait()


def shards(
    psi,
    left_env,
    right_env,
    send_block,
    send_left,
    send_live,
    recv_right,
    recv_out,
    loc_block,
    loc_left,
    loc_right,
):
    peers = lax.axis_size("renv")
    owned = psi.shape[0]
    sector = math.isqrt(psi.shape[1])
    slots = send_block.shape[1]
    terms = send_left.shape[2]
    count = peers * slots
    lefts = left_env.shape[0]
    rights = right_env.shape[0]
    height = sector + SUB
    psi_rows = as_rows(psi, sector)
    left_rows = as_rows(left_env, sector)
    right_rows = as_rows(right_env, sector)
    by_slot = [index.transpose(1, 2, 0) for index in (send_left, send_live, recv_right, recv_out)]
    blocks = jax.ShapeDtypeStruct((count, height, sector), F32)
    rows = jax.ShapeDtypeStruct((owned * sector, sector), F32)

    sent = pl.pallas_call(
        gather_kernel,
        out_shape=blocks,
        in_specs=[SMEM] * 3 + [VMEM],
        out_specs=HBM,
        scratch_shapes=[pltpu.VMEM(blocks.shape, F32), pltpu.SemaphoreType.DMA((count,))],
        compiler_params=roomy(56),
        name="gather_blocks",
    )(send_block.reshape(-1), *by_slot[:2], psi_rows)
    came = lax.all_to_all(
        sent.reshape(peers, slots, height, sector),
        "renv",
        split_axis=0,
        concat_axis=0,
        tiled=True,
        axis_index_groups=[[member(position, peers) for position in range(peers)]],
    )
    came = came.reshape(count, height, sector)

    slabs = owned // terms
    turned, parts = pl.pallas_call(
        prepare_kernel,
        out_shape=(
            jax.ShapeDtypeStruct((count + slabs, terms * sector + SUB, sector), F32),
            jax.ShapeDtypeStruct((lefts + rights, sector, 2 * sector), BF16),
        ),
        in_specs=[HBM] + [SMEM] * 5 + [VMEM] * 3,
        out_specs=(VMEM,) * 2,
        scratch_shapes=[
            pltpu.VMEM((owned, sector, sector), F32),
            pltpu.VMEM((owned, sector, 2 * sector), BF16),
            pltpu.VMEM((rights, 2 * sector, 2 * sector), BF16),
            pltpu.VMEM((loc_block.shape[0], sector, 2 * sector), BF16),
        ],
        compiler_params=roomy(56),
        cost_estimate=LIGHT,
        name="prepare",
    )(sent, *by_slot[2:], loc_block, loc_left, loc_right, psi_rows, right_rows, left_rows)

    chunk = math.gcd(count, 16)
    moved = []
    sums = 0.0
    for first in range(0, count, chunk):
        part = slice(first, first + chunk) if count > chunk else slice(None)
        kept, share = pl.pallas_call(
            lambda *refs: arrive_kernel(terms, *refs),
            out_shape=(
                jax.ShapeDtypeStruct((chunk, terms * sector, 2 * sector), BF16),
                jax.ShapeDtypeStruct((peers, 1, sector), F32),
            ),
            in_specs=[VMEM] + [HBM] * 2,
            out_specs=(VMEM,) * 2,
            scratch_shapes=[
                pltpu.SMEM((chunk, SUB, sector), F32),
                pltpu.VMEM((chunk, terms * sector + SUB, sector), F32),
                pltpu.VMEM((lefts, sector, 2 * sector), BF16),
                pltpu.VMEM((chunk, 2 * sector, 2 * sector), BF16),
                pltpu.SemaphoreType.DMA((6,)),
            ],
            compiler_params=roomy(50),
            name="arrive",
        )(came[part], turned if count == chunk else turned[part], parts)
        moved.append(kept)
        sums = share if count == chunk else sums + share
    moved = moved[0] if len(moved) == 1 else jnp.concatenate(moved, axis=0)
    order = [member(position, peers) for position in range(peers)]
    order = order[:1] + order[:0:-1]
    totals = lax.all_to_all(sums, "renv", split_axis=0, concat_axis=0, tiled=True, axis_index_groups=[order])

    hpsi_rows = pl.pallas_call(
        remote_kernel,
        out_shape=rows,
        in_specs=[SMEM] * 2 + [VMEM] + [HBM] * 2,
        out_specs=VMEM,
        scratch_shapes=[
            pltpu.VMEM(rows.shape, F32),
            pltpu.VMEM((rights, sector, 2 * sector), BF16),
            pltpu.SemaphoreType.DMA((1 + slabs,)),
        ],
        compiler_params=roomy(50),
        cost_estimate=pl.CostEstimate(flops=4 * 10**9, bytes_accessed=6 * MIB, transcendentals=0),
        name="remote_terms",
    )(*by_slot[2:], moved, turned, parts)

    hpsi, residual_rows = pl.pallas_call(
        residual_kernel,
        out_shape=(rows, rows),
        in_specs=[VMEM] * 3,
        out_specs=(HBM,) * 2,
        scratch_shapes=[pltpu.VMEM(rows.shape, F32), pltpu.SemaphoreType.DMA((2,))],
        compiler_params=roomy(16),
        name="residual",
    )(totals, hpsi_rows, psi_rows)
    return (from_rows(hpsi, owned), from_rows(residual_rows, owned))


def solution(mesh):
    placed = (
        P(("groups", "renv"), None),
        P("groups", None),
        P(("groups", "renv"), None),
        P(("groups", "renv"), None),
        P(("groups", "renv"), None, None),
        P(("groups", "renv"), None, None),
        P(("groups", "renv"), None, None),
        P(("groups", "renv"), None, None),
        P(("groups", "renv")),
        P(("groups", "renv")),
        P(("groups", "renv")),
    )
    return jax.shard_map(
        shards,
        mesh=mesh,
        in_specs=placed,
        out_specs=(P(("groups", "renv"), None), P(("groups", "renv"), None)),
        check_vma=False,
    )
```

```python
import math

import jax
import jax.numpy as jnp
from jax import lax
from jax.experimental import pallas as pl
from jax.experimental.pallas import tpu as pltpu
from jax.sharding import PartitionSpec as P

F32 = jnp.float32
BF16 = jnp.bfloat16
SUB = 8
VMEM = pl.BlockSpec(memory_space=pltpu.VMEM)
SMEM = pl.BlockSpec(memory_space=pltpu.SMEM)
HBM = pl.BlockSpec(memory_space=pltpu.HBM)
MIB = 2**20
LIGHT = pl.CostEstimate(flops=10**6, bytes_accessed=2**16, transcendentals=0)


def as_rows(blocks, sector):
    count = blocks.shape[0]
    split = blocks.reshape(count // SUB, SUB, sector, sector)
    return split.transpose(0, 2, 1, 3).reshape(count * sector, sector)


def from_rows(rows, count):
    sector = rows.shape[1]
    split = rows.reshape(count // SUB, sector, SUB, sector)
    return split.transpose(0, 2, 1, 3).reshape(count, sector * sector)


def pick(ref, block):
    sector = ref.shape[1]
    start = (block // SUB) * (SUB * sector) + block % SUB
    return ref[pl.ds(start, sector, stride=SUB), :]


def halves(mat):
    high = mat.astype(BF16)
    low = (mat - high.astype(F32)).astype(BF16)
    return jnp.concatenate([high, low], axis=1)


def doubled(mat):
    both = halves(mat)
    return jnp.concatenate([both, both], axis=0)


def product(left, right):
    sector = right.shape[1] // 2
    wide = jnp.dot(left, right, preferred_element_type=F32)
    return wide[:, :sector] + wide[:, sector:]


def stacked(mat):
    high = mat.astype(BF16)
    low = (mat - high.astype(F32)).astype(BF16)
    rows = [jnp.concatenate([part, part], axis=1) for part in (high, low)]
    return jnp.concatenate(rows, axis=0)


def product_t(left, right):
    sector = right.shape[0] // 2
    wide = lax.dot_general(left, right, (((1,), (1,)), ((), ())), preferred_element_type=F32)
    return wide[:, :sector] + wide[:, sector:]


def twice(part):
    return jnp.concatenate([part, part], axis=0)


def roomy(mib):
    return pltpu.CompilerParams(vmem_limit_bytes=mib * MIB)


def member(position, peers):
    if peers % 2:
        return position
    middle = min(peers // 2 + 3, peers - 1)
    return position + middle * (position == 0) - 1 * (position > 0) + 1 * (position > middle)


def gather_kernel(block_ref, left_ref, live_ref, psi_rows, out_hbm, stage, sems):
    slots, terms, peers = left_ref.shape
    sector = psi_rows.shape[1]
    lane = lax.broadcasted_iota(jnp.int32, (SUB, sector), 1)
    puts = []
    for i in range(stage.shape[0]):
        slot, peer = i % slots, member(i // slots, peers)
        stage[i, :sector] = pick(psi_rows, block_ref[peer * slots + slot])
        values = jnp.zeros(lane.shape, jnp.int32)
        for g in range(terms):
            values = jnp.where(lane == g, left_ref[slot, g, peer], values)
            values = jnp.where(lane == terms + g, live_ref[slot, g, peer], values)
        stage[i, sector:] = values.astype(F32)
        put = pltpu.make_async_copy(stage.at[i], out_hbm.at[i], sems.at[i])
        put.start()
        puts.append(put)
    for put in puts:
        put.wait()


def prepare_kernel(
    sent_hbm,
    rindex_ref,
    out_index_ref,
    block_ref,
    left_ref,
    right_ref,
    psi_rows,
    right_rows,
    left_rows,
    turned_ref,
    parts_ref,
    near_ref,
    psis_ref,
    stacks_ref,
    moved_ref,
):
    slots, terms, peers = rindex_ref.shape
    sector = psi_rows.shape[1]

    rights = right_rows.shape[0] // sector
    lefts = left_rows.shape[0] // sector

    def split_right(i, carry):
        mat = pick(right_rows, i)
        parts_ref[lefts + i] = halves(mat)
        stacks_ref[i] = stacked(mat)
        return carry

    lax.fori_loop(0, rights, split_right, 0, unroll=4)

    def split_psi(i, carry):
        psis_ref[i] = halves(pick(psi_rows, i))
        return carry

    lax.fori_loop(0, psis_ref.shape[0], split_psi, 0, unroll=4)

    def turn(i, carry):
        slot, peer = i % slots, member(i // slots, peers)
        for g in range(terms):
            right = stacks_ref[rindex_ref[slot, g, peer]]
            psi = psis_ref[out_index_ref[slot, g, peer]]
            turned_ref[i, g * sector : (g + 1) * sector] = product_t(psi, right)
        turned_ref[i, terms * sector :] = jnp.zeros((SUB, sector), F32)
        return carry

    slabs = near_ref.shape[0] // terms
    senders = turned_ref.shape[0] - slabs
    lax.fori_loop(0, senders, turn, 0, unroll=4)

    def split_left(i, carry):
        parts_ref[i] = halves(pick(left_rows, i))
        return carry

    lax.fori_loop(0, lefts, split_left, 0, unroll=8)

    def left_step(k, carry):
        moved_ref[k] = halves(product(parts_ref[left_ref[k]], twice(psis_ref[block_ref[k]])))
        return carry

    lax.fori_loop(0, block_ref.shape[0], left_step, 0, unroll=8)
    near_ref[...] = jnp.zeros_like(near_ref)

    def right_step(k, carry):
        near_ref[block_ref[k]] += product(moved_ref[k], twice(parts_ref[lefts + right_ref[k]]))
        return carry

    lax.fori_loop(0, block_ref.shape[0], right_step, 0, unroll=8)
    corr = jnp.zeros((1, sector), F32)
    norm = jnp.zeros((1, sector), F32)
    for b in range(near_ref.shape[0]):
        mat = pick(psi_rows, b)
        turned_ref[senders + b // terms, (b % terms) * sector : (b % terms + 1) * sector] = near_ref[b]
        corr += jnp.sum(mat * near_ref[b], axis=0, keepdims=True)
        norm += jnp.sum(mat * mat, axis=0, keepdims=True)
    row = lax.broadcasted_iota(jnp.int32, (SUB, sector), 0)
    turned_ref[0, terms * sector :] = jnp.where(row == 0, corr, jnp.where(row == 1, norm, 0.0))


def arrive_kernel(terms, came_ref, turned_hbm, parts_hbm, moved_ref, sums_ref, marks, turned_ref, lefts_ref, weights_ref, sems):
    count, height, sector = came_ref.shape
    get_marks = pltpu.make_async_copy(came_ref.at[:, pl.ds(sector, height - sector)], marks, sems.at[0])
    get_lefts = pltpu.make_async_copy(parts_hbm.at[pl.ds(0, lefts_ref.shape[0])], lefts_ref, sems.at[1])
    quarter = count // math.gcd(count, 4)
    spans = [pl.ds(first, quarter) for first in range(0, count, quarter)]
    get_turned = [
        pltpu.make_async_copy(turned_hbm.at[span], turned_ref.at[span], sems.at[2 + k]) for k, span in enumerate(spans)
    ]
    for copy in (get_marks, get_lefts, *get_turned):
        copy.start()

    def split(i, carry):
        weights_ref[i] = doubled(came_ref[i, :sector])
        return carry

    lax.fori_loop(0, count, split, 0, unroll=4)
    get_marks.wait()
    get_lefts.wait()

    def block(i, total):
        stack = [lefts_ref[marks[i, 0, g].astype(jnp.int32)] for g in range(terms)]
        moved = product(jnp.concatenate(stack, axis=0), weights_ref[i])
        for g in range(terms):
            part = slice(g * sector, (g + 1) * sector)
            one = moved[part] * marks[i, 0, terms + g]
            moved_ref[i, part] = halves(one)
            total += jnp.sum((one * turned_ref[i, part]).reshape(-1, SUB, sector), axis=0)
        return total

    total = jnp.zeros((SUB, sector), F32)
    for k, copy in enumerate(get_turned):
        copy.wait()
        total = lax.fori_loop(k * quarter, (k + 1) * quarter, block, total, unroll=4)
    corr = jnp.sum(total, axis=0, keepdims=True)
    row = lax.broadcasted_iota(jnp.int32, total.shape, 0)
    mine = turned_ref[0, terms * sector :] + jnp.where(row == 0, corr, 0.0)
    folded = mine + pltpu.roll(mine, sector // 2, 1)
    lane = lax.broadcasted_iota(jnp.int32, (1, sector), 1)
    shared = jnp.where(lane < sector // 2, folded[0:1], folded[1:2])
    for i in range(sums_ref.shape[0]):
        sums_ref[i] = shared


def remote_kernel(rindex_ref, out_index_ref, moved_ref, turned_hbm, parts_hbm, hpsi_rows, acc, rights_ref, sems):
    slots, terms, peers = rindex_ref.shape
    senders, height, _ = moved_ref.shape
    sector = height // terms
    rights = rights_ref.shape[0]
    copies = [pltpu.make_async_copy(parts_hbm.at[pl.ds(parts_hbm.shape[0] - rights, rights)], rights_ref, sems.at[0])]
    for k in range(acc.shape[0] // height):
        near = turned_hbm.at[senders + k, pl.ds(0, height)]
        copies.append(pltpu.make_async_copy(near, acc.at[pl.ds(k * height, height)], sems.at[1 + k]))
    for copy in copies:
        copy.start()
    for copy in copies:
        copy.wait()

    def right_step(i, carry):
        slot, peer = i % slots, member(i // slots, peers)
        for g in range(terms):
            right = rights_ref[rindex_ref[slot, g, peer]]
            spot = pl.multiple_of(out_index_ref[slot, g, peer] * sector, sector)
            acc[pl.ds(spot, sector)] += product(moved_ref[i, g * sector : (g + 1) * sector], twice(right))
        return carry

    lax.fori_loop(0, senders, right_step, 0, unroll=8)
    for b in range(acc.shape[0] // sector):
        start = (b // SUB) * (SUB * sector) + b % SUB
        hpsi_rows[pl.ds(start, sector, stride=SUB), :] = acc[b * sector : (b + 1) * sector]


def residual_kernel(sums_ref, hpsi_rows, psi_rows, hpsi_hbm, out_hbm, out_ref, sems):
    put_hpsi = pltpu.make_async_copy(hpsi_rows, hpsi_hbm, sems.at[0])
    put_hpsi.start()
    total = jnp.sum(sums_ref[...], axis=0)
    lane = lax.broadcasted_iota(jnp.int32, total.shape, 1)
    first = lane < total.shape[1] // 2
    corr = jnp.sum(jnp.where(first, total, 0.0), axis=1, keepdims=True)
    norm = jnp.sum(jnp.where(first, 0.0, total), axis=1, keepdims=True)
    theta = corr / (norm + 1e-06)
    out_ref[...] = hpsi_rows[...] - theta * psi_rows[...]
    put_out = pltpu.make_async_copy(out_ref, out_hbm, sems.at[1])
    put_out.start()
    put_hpsi.wait()
    put_out.wait()


def shards(
    psi,
    left_env,
    right_env,
    send_block,
    send_left,
    send_live,
    recv_right,
    recv_out,
    loc_block,
    loc_left,
    loc_right,
):
    peers = lax.axis_size("renv")
    owned = psi.shape[0]
    sector = math.isqrt(psi.shape[1])
    slots = send_block.shape[1]
    terms = send_left.shape[2]
    count = peers * slots
    lefts = left_env.shape[0]
    rights = right_env.shape[0]
    height = sector + SUB
    psi_rows = as_rows(psi, sector)
    left_rows = as_rows(left_env, sector)
    right_rows = as_rows(right_env, sector)
    by_slot = [index.transpose(1, 2, 0) for index in (send_left, send_live, recv_right, recv_out)]
    blocks = jax.ShapeDtypeStruct((count, height, sector), F32)
    rows = jax.ShapeDtypeStruct((owned * sector, sector), F32)

    sent = pl.pallas_call(
        gather_kernel,
        out_shape=blocks,
        in_specs=[SMEM] * 3 + [VMEM],
        out_specs=HBM,
        scratch_shapes=[pltpu.VMEM(blocks.shape, F32), pltpu.SemaphoreType.DMA((count,))],
        compiler_params=roomy(56),
        name="gather_blocks",
    )(send_block.reshape(-1), *by_slot[:2], psi_rows)
    came = lax.all_to_all(
        sent.reshape(peers, slots, height, sector),
        "renv",
        split_axis=0,
        concat_axis=0,
        tiled=True,
        axis_index_groups=[[member(position, peers) for position in range(peers)]],
    )
    came = came.reshape(count, height, sector)

    slabs = owned // terms
    turned, parts = pl.pallas_call(
        prepare_kernel,
        out_shape=(
            jax.ShapeDtypeStruct((count + slabs, terms * sector + SUB, sector), F32),
            jax.ShapeDtypeStruct((lefts + rights, sector, 2 * sector), BF16),
        ),
        in_specs=[HBM] + [SMEM] * 5 + [VMEM] * 3,
        out_specs=(VMEM,) * 2,
        scratch_shapes=[
            pltpu.VMEM((owned, sector, sector), F32),
            pltpu.VMEM((owned, sector, 2 * sector), BF16),
            pltpu.VMEM((rights, 2 * sector, 2 * sector), BF16),
            pltpu.VMEM((loc_block.shape[0], sector, 2 * sector), BF16),
        ],
        compiler_params=roomy(56),
        cost_estimate=LIGHT,
        name="prepare",
    )(sent, *by_slot[2:], loc_block, loc_left, loc_right, psi_rows, right_rows, left_rows)

    chunk = math.gcd(count, 16)
    moved = []
    sums = 0.0
    for first in range(0, count, chunk):
        part = slice(first, first + chunk) if count > chunk else slice(None)
        kept, share = pl.pallas_call(
            lambda *refs: arrive_kernel(terms, *refs),
            out_shape=(
                jax.ShapeDtypeStruct((chunk, terms * sector, 2 * sector), BF16),
                jax.ShapeDtypeStruct((peers, 1, sector), F32),
            ),
            in_specs=[VMEM] + [HBM] * 2,
            out_specs=(VMEM,) * 2,
            scratch_shapes=[
                pltpu.SMEM((chunk, SUB, sector), F32),
                pltpu.VMEM((chunk, terms * sector + SUB, sector), F32),
                pltpu.VMEM((lefts, sector, 2 * sector), BF16),
                pltpu.VMEM((chunk, 2 * sector, 2 * sector), BF16),
                pltpu.SemaphoreType.DMA((6,)),
            ],
            compiler_params=roomy(50),
            name="arrive",
        )(came[part], turned if count == chunk else turned[part], parts)
        moved.append(kept)
        sums = share if count == chunk else sums + share
    moved = moved[0] if len(moved) == 1 else jnp.concatenate(moved, axis=0)
    order = [member(position, peers) for position in range(peers)]
    order = order[:1] + order[:0:-1]
    totals = lax.all_to_all(sums, "renv", split_axis=0, concat_axis=0, tiled=True, axis_index_groups=[order])

    hpsi_rows = pl.pallas_call(
        remote_kernel,
        out_shape=rows,
        in_specs=[SMEM] * 2 + [VMEM] + [HBM] * 2,
        out_specs=VMEM,
        scratch_shapes=[
            pltpu.VMEM(rows.shape, F32),
            pltpu.VMEM((rights, sector, 2 * sector), BF16),
            pltpu.SemaphoreType.DMA((1 + slabs,)),
        ],
        compiler_params=roomy(50),
        cost_estimate=pl.CostEstimate(flops=4 * 10**9, bytes_accessed=6 * MIB, transcendentals=0),
        name="remote_terms",
    )(*by_slot[2:], moved, turned, parts)

    hpsi, residual_rows = pl.pallas_call(
        residual_kernel,
        out_shape=(rows, rows),
        in_specs=[VMEM] * 3,
        out_specs=(HBM,) * 2,
        scratch_shapes=[pltpu.VMEM(rows.shape, F32), pltpu.SemaphoreType.DMA((2,))],
        compiler_params=roomy(16),
        name="residual",
    )(totals, hpsi_rows, psi_rows)
    return (from_rows(hpsi, owned), from_rows(residual_rows, owned))


def solution(mesh):
    placed = (
        P(("groups", "renv"), None),
        P("groups", None),
        P(("groups", "renv"), None),
        P(("groups", "renv"), None),
        P(("groups", "renv"), None, None),
        P(("groups", "renv"), None, None),
        P(("groups", "renv"), None, None),
        P(("groups", "renv"), None, None),
        P(("groups", "renv")),
        P(("groups", "renv")),
        P(("groups", "renv")),
    )
    return jax.shard_map(
        shards,
        mesh=mesh,
        in_specs=placed,
        out_specs=(P(("groups", "renv"), None), P(("groups", "renv"), None)),
        check_vma=False,
    )
```

```python
import math

import jax
import jax.numpy as jnp
from jax import lax
from jax.experimental import pallas as pl
from jax.experimental.pallas import tpu as pltpu
from jax.sharding import PartitionSpec as P

F32 = jnp.float32
BF16 = jnp.bfloat16
SUB = 8
VMEM = pl.BlockSpec(memory_space=pltpu.VMEM)
SMEM = pl.BlockSpec(memory_space=pltpu.SMEM)
HBM = pl.BlockSpec(memory_space=pltpu.HBM)
MIB = 2**20
LIGHT = pl.CostEstimate(flops=10**6, bytes_accessed=2**16, transcendentals=0)


def as_rows(blocks, sector):
    count = blocks.shape[0]
    split = blocks.reshape(count // SUB, SUB, sector, sector)
    return split.transpose(0, 2, 1, 3).reshape(count * sector, sector)


def from_rows(rows, count):
    sector = rows.shape[1]
    split = rows.reshape(count // SUB, sector, SUB, sector)
    return split.transpose(0, 2, 1, 3).reshape(count, sector * sector)


def pick(ref, block):
    sector = ref.shape[1]
    start = (block // SUB) * (SUB * sector) + block % SUB
    return ref[pl.ds(start, sector, stride=SUB), :]


def halves(mat):
    high = mat.astype(BF16)
    low = (mat - high.astype(F32)).astype(BF16)
    return jnp.concatenate([high, low], axis=1)


def doubled(mat):
    both = halves(mat)
    return jnp.concatenate([both, both], axis=0)


def product(left, right):
    sector = right.shape[1] // 2
    wide = jnp.dot(left, right, preferred_element_type=F32)
    return wide[:, :sector] + wide[:, sector:]


def stacked(mat):
    high = mat.astype(BF16)
    low = (mat - high.astype(F32)).astype(BF16)
    rows = [jnp.concatenate([part, part], axis=1) for part in (high, low)]
    return jnp.concatenate(rows, axis=0)


def product_t(left, right):
    sector = right.shape[0] // 2
    wide = lax.dot_general(left, right, (((1,), (1,)), ((), ())), preferred_element_type=F32)
    return wide[:, :sector] + wide[:, sector:]


def twice(part):
    return jnp.concatenate([part, part], axis=0)


def roomy(mib):
    return pltpu.CompilerParams(vmem_limit_bytes=mib * MIB)


def member(position, peers):
    if peers % 2:
        return position
    middle = peers // 2 + 1
    return position + middle * (position == 0) - 1 * (position > 0) + 1 * (position > middle)


def gather_kernel(block_ref, left_ref, live_ref, psi_rows, out_hbm, mats, tails, sems):
    slots, terms, peers = left_ref.shape
    owned, sector, _ = mats.shape
    count = tails.shape[0]
    for b in range(owned):
        mats[b] = pick(psi_rows, b)
    puts = []
    for i in range(count):
        slot, peer = i % slots, member(i // slots, peers)
        block = mats.at[block_ref[peer * slots + slot]]
        puts.append(pltpu.make_async_copy(block, out_hbm.at[i, pl.ds(0, sector)], sems.at[i]))
        puts[i].start()
    lane = lax.broadcasted_iota(jnp.int32, (SUB, sector), 1)
    for i in range(count):
        slot, peer = i % slots, member(i // slots, peers)
        values = jnp.zeros(lane.shape, jnp.int32)
        for g in range(terms):
            values = jnp.where(lane == g, left_ref[slot, g, peer], values)
            values = jnp.where(lane == terms + g, live_ref[slot, g, peer], values)
        tails[i] = values.astype(F32)
    puts.append(pltpu.make_async_copy(tails, out_hbm.at[:, pl.ds(sector, SUB)], sems.at[count]))
    puts[count].start()
    for put in puts:
        put.wait()


def prepare_kernel(
    sent_hbm,
    rindex_ref,
    out_index_ref,
    block_ref,
    left_ref,
    right_ref,
    psi_rows,
    right_rows,
    left_rows,
    turned_ref,
    parts_ref,
    near_ref,
    psis_ref,
    stacks_ref,
    moved_ref,
):
    slots, terms, peers = rindex_ref.shape
    sector = psi_rows.shape[1]

    rights = right_rows.shape[0] // sector
    lefts = left_rows.shape[0] // sector

    def split_right(i, carry):
        mat = pick(right_rows, i)
        parts_ref[lefts + i] = halves(mat)
        stacks_ref[i] = stacked(mat)
        return carry

    lax.fori_loop(0, rights, split_right, 0, unroll=4)

    def split_psi(i, carry):
        psis_ref[i] = halves(pick(psi_rows, i))
        return carry

    lax.fori_loop(0, psis_ref.shape[0], split_psi, 0, unroll=4)

    def turn(i, carry):
        slot, peer = i % slots, member(i // slots, peers)
        for g in range(terms):
            right = stacks_ref[rindex_ref[slot, g, peer]]
            psi = psis_ref[out_index_ref[slot, g, peer]]
            turned_ref[i, g * sector : (g + 1) * sector] = product_t(psi, right)
        turned_ref[i, terms * sector :] = jnp.zeros((SUB, sector), F32)
        return carry

    slabs = near_ref.shape[0] // terms
    senders = turned_ref.shape[0] - slabs
    lax.fori_loop(0, senders, turn, 0, unroll=4)

    def split_left(i, carry):
        parts_ref[i] = halves(pick(left_rows, i))
        return carry

    lax.fori_loop(0, lefts, split_left, 0, unroll=8)

    def left_step(k, carry):
        moved_ref[k] = halves(product(parts_ref[left_ref[k]], twice(psis_ref[block_ref[k]])))
        return carry

    lax.fori_loop(0, block_ref.shape[0], left_step, 0, unroll=8)
    near_ref[...] = jnp.zeros_like(near_ref)

    def right_step(k, carry):
        near_ref[block_ref[k]] += product(moved_ref[k], twice(parts_ref[lefts + right_ref[k]]))
        return carry

    lax.fori_loop(0, block_ref.shape[0], right_step, 0, unroll=8)
    corr = jnp.zeros((1, sector), F32)
    norm = jnp.zeros((1, sector), F32)
    for b in range(near_ref.shape[0]):
        mat = pick(psi_rows, b)
        turned_ref[senders + b // terms, (b % terms) * sector : (b % terms + 1) * sector] = near_ref[b]
        corr += jnp.sum(mat * near_ref[b], axis=0, keepdims=True)
        norm += jnp.sum(mat * mat, axis=0, keepdims=True)
    row = lax.broadcasted_iota(jnp.int32, (SUB, sector), 0)
    turned_ref[0, terms * sector :] = jnp.where(row == 0, corr, jnp.where(row == 1, norm, 0.0))


def arrive_kernel(terms, came_ref, turned_hbm, parts_hbm, moved_ref, sums_ref, marks, turned_ref, lefts_ref, weights_ref, sems):
    count, height, sector = came_ref.shape
    get_marks = pltpu.make_async_copy(came_ref.at[:, pl.ds(sector, height - sector)], marks, sems.at[0])
    get_lefts = pltpu.make_async_copy(parts_hbm.at[pl.ds(0, lefts_ref.shape[0])], lefts_ref, sems.at[1])
    quarter = count // math.gcd(count, 4)
    spans = [pl.ds(first, quarter) for first in range(0, count, quarter)]
    get_turned = [
        pltpu.make_async_copy(turned_hbm.at[span], turned_ref.at[span], sems.at[2 + k]) for k, span in enumerate(spans)
    ]
    for copy in (get_marks, get_lefts, *get_turned):
        copy.start()

    def split(i, carry):
        weights_ref[i] = doubled(came_ref[i, :sector])
        return carry

    lax.fori_loop(0, count, split, 0, unroll=4)
    get_marks.wait()
    get_lefts.wait()

    def block(i, total):
        stack = [lefts_ref[marks[i, 0, g].astype(jnp.int32)] for g in range(terms)]
        moved = product(jnp.concatenate(stack, axis=0), weights_ref[i])
        for g in range(terms):
            part = slice(g * sector, (g + 1) * sector)
            one = moved[part] * marks[i, 0, terms + g]
            moved_ref[i, part] = halves(one)
            total += jnp.sum((one * turned_ref[i, part]).reshape(-1, SUB, sector), axis=0)
        return total

    total = jnp.zeros((SUB, sector), F32)
    for k, copy in enumerate(get_turned):
        copy.wait()
        total = lax.fori_loop(k * quarter, (k + 1) * quarter, block, total, unroll=4)
    corr = jnp.sum(total, axis=0, keepdims=True)
    row = lax.broadcasted_iota(jnp.int32, total.shape, 0)
    mine = turned_ref[0, terms * sector :] + jnp.where(row == 0, corr, 0.0)
    folded = mine + pltpu.roll(mine, sector // 2, 1)
    lane = lax.broadcasted_iota(jnp.int32, (1, sector), 1)
    shared = jnp.where(lane < sector // 2, folded[0:1], folded[1:2])
    for i in range(sums_ref.shape[0]):
        sums_ref[i] = shared


def remote_kernel(rindex_ref, out_index_ref, moved_ref, turned_hbm, parts_hbm, hpsi_rows, acc, rights_ref, sems):
    slots, terms, peers = rindex_ref.shape
    senders, height, _ = moved_ref.shape
    sector = height // terms
    rights = rights_ref.shape[0]
    copies = [pltpu.make_async_copy(parts_hbm.at[pl.ds(parts_hbm.shape[0] - rights, rights)], rights_ref, sems.at[0])]
    for k in range(acc.shape[0] // height):
        near = turned_hbm.at[senders + k, pl.ds(0, height)]
        copies.append(pltpu.make_async_copy(near, acc.at[pl.ds(k * height, height)], sems.at[1 + k]))
    for copy in copies:
        copy.start()
    for copy in copies:
        copy.wait()

    def right_step(i, carry):
        slot, peer = i % slots, member(i // slots, peers)
        for g in range(terms):
            right = rights_ref[rindex_ref[slot, g, peer]]
            spot = pl.multiple_of(out_index_ref[slot, g, peer] * sector, sector)
            acc[pl.ds(spot, sector)] += product(moved_ref[i, g * sector : (g + 1) * sector], twice(right))
        return carry

    lax.fori_loop(0, senders, right_step, 0, unroll=8)
    for b in range(acc.shape[0] // sector):
        start = (b // SUB) * (SUB * sector) + b % SUB
        hpsi_rows[pl.ds(start, sector, stride=SUB), :] = acc[b * sector : (b + 1) * sector]


def residual_kernel(sums_ref, hpsi_rows, psi_rows, hpsi_hbm, out_hbm, out_ref, sems):
    put_hpsi = pltpu.make_async_copy(hpsi_rows, hpsi_hbm, sems.at[0])
    put_hpsi.start()
    total = jnp.sum(sums_ref[...], axis=0)
    lane = lax.broadcasted_iota(jnp.int32, total.shape, 1)
    first = lane < total.shape[1] // 2
    corr = jnp.sum(jnp.where(first, total, 0.0), axis=1, keepdims=True)
    norm = jnp.sum(jnp.where(first, 0.0, total), axis=1, keepdims=True)
    theta = corr / (norm + 1e-06)
    out_ref[...] = hpsi_rows[...] - theta * psi_rows[...]
    put_out = pltpu.make_async_copy(out_ref, out_hbm, sems.at[1])
    put_out.start()
    put_hpsi.wait()
    put_out.wait()


def shards(
    psi,
    left_env,
    right_env,
    send_block,
    send_left,
    send_live,
    recv_right,
    recv_out,
    loc_block,
    loc_left,
    loc_right,
):
    peers = lax.axis_size("renv")
    owned = psi.shape[0]
    sector = math.isqrt(psi.shape[1])
    slots = send_block.shape[1]
    terms = send_left.shape[2]
    count = peers * slots
    lefts = left_env.shape[0]
    rights = right_env.shape[0]
    height = sector + SUB
    psi_rows = as_rows(psi, sector)
    left_rows = as_rows(left_env, sector)
    right_rows = as_rows(right_env, sector)
    by_slot = [index.transpose(1, 2, 0) for index in (send_left, send_live, recv_right, recv_out)]
    blocks = jax.ShapeDtypeStruct((count, height, sector), F32)
    rows = jax.ShapeDtypeStruct((owned * sector, sector), F32)

    sent = pl.pallas_call(
        gather_kernel,
        out_shape=blocks,
        in_specs=[SMEM] * 3 + [VMEM],
        out_specs=HBM,
        scratch_shapes=[
            pltpu.VMEM((owned, sector, sector), F32),
            pltpu.VMEM((count, SUB, sector), F32),
            pltpu.SemaphoreType.DMA((count + 1,)),
        ],
        compiler_params=roomy(56),
        name="gather_blocks",
    )(send_block.reshape(-1), *by_slot[:2], psi_rows)
    came = lax.all_to_all(
        sent.reshape(peers, slots, height, sector),
        "renv",
        split_axis=0,
        concat_axis=0,
        tiled=True,
        axis_index_groups=[[member(position, peers) for position in range(peers)]],
    )
    came = came.reshape(count, height, sector)

    slabs = owned // terms
    turned, parts = pl.pallas_call(
        prepare_kernel,
        out_shape=(
            jax.ShapeDtypeStruct((count + slabs, terms * sector + SUB, sector), F32),
            jax.ShapeDtypeStruct((lefts + rights, sector, 2 * sector), BF16),
        ),
        in_specs=[HBM] + [SMEM] * 5 + [VMEM] * 3,
        out_specs=(VMEM,) * 2,
        scratch_shapes=[
            pltpu.VMEM((owned, sector, sector), F32),
            pltpu.VMEM((owned, sector, 2 * sector), BF16),
            pltpu.VMEM((rights, 2 * sector, 2 * sector), BF16),
            pltpu.VMEM((loc_block.shape[0], sector, 2 * sector), BF16),
        ],
        compiler_params=roomy(56),
        cost_estimate=LIGHT,
        name="prepare",
    )(sent, *by_slot[2:], loc_block, loc_left, loc_right, psi_rows, right_rows, left_rows)

    chunk = math.gcd(count, 16)
    moved = []
    sums = 0.0
    for first in range(0, count, chunk):
        part = slice(first, first + chunk) if count > chunk else slice(None)
        kept, share = pl.pallas_call(
            lambda *refs: arrive_kernel(terms, *refs),
            out_shape=(
                jax.ShapeDtypeStruct((chunk, terms * sector, 2 * sector), BF16),
                jax.ShapeDtypeStruct((peers, 1, sector), F32),
            ),
            in_specs=[VMEM] + [HBM] * 2,
            out_specs=(VMEM,) * 2,
            scratch_shapes=[
                pltpu.SMEM((chunk, SUB, sector), F32),
                pltpu.VMEM((chunk, terms * sector + SUB, sector), F32),
                pltpu.VMEM((lefts, sector, 2 * sector), BF16),
                pltpu.VMEM((chunk, 2 * sector, 2 * sector), BF16),
                pltpu.SemaphoreType.DMA((6,)),
            ],
            compiler_params=roomy(50),
            name="arrive",
        )(came[part], turned if count == chunk else turned[part], parts)
        moved.append(kept)
        sums = share if count == chunk else sums + share
    moved = moved[0] if len(moved) == 1 else jnp.concatenate(moved, axis=0)
    order = [member(position, peers) for position in range(peers)]
    order = order[:1] + order[:0:-1]
    totals = lax.all_to_all(sums, "renv", split_axis=0, concat_axis=0, tiled=True, axis_index_groups=[order])

    hpsi_rows = pl.pallas_call(
        remote_kernel,
        out_shape=rows,
        in_specs=[SMEM] * 2 + [VMEM] + [HBM] * 2,
        out_specs=VMEM,
        scratch_shapes=[
            pltpu.VMEM(rows.shape, F32),
            pltpu.VMEM((rights, sector, 2 * sector), BF16),
            pltpu.SemaphoreType.DMA((1 + slabs,)),
        ],
        compiler_params=roomy(50),
        cost_estimate=pl.CostEstimate(flops=4 * 10**9, bytes_accessed=6 * MIB, transcendentals=0),
        name="remote_terms",
    )(*by_slot[2:], moved, turned, parts)

    hpsi, residual_rows = pl.pallas_call(
        residual_kernel,
        out_shape=(rows, rows),
        in_specs=[VMEM] * 3,
        out_specs=(HBM,) * 2,
        scratch_shapes=[pltpu.VMEM(rows.shape, F32), pltpu.SemaphoreType.DMA((2,))],
        compiler_params=roomy(16),
        name="residual",
    )(totals, hpsi_rows, psi_rows)
    return (from_rows(hpsi, owned), from_rows(residual_rows, owned))


def solution(mesh):
    placed = (
        P(("groups", "renv"), None),
        P("groups", None),
        P(("groups", "renv"), None),
        P(("groups", "renv"), None),
        P(("groups", "renv"), None, None),
        P(("groups", "renv"), None, None),
        P(("groups", "renv"), None, None),
        P(("groups", "renv"), None, None),
        P(("groups", "renv")),
        P(("groups", "renv")),
        P(("groups", "renv")),
    )
    return jax.shard_map(
        shards,
        mesh=mesh,
        in_specs=placed,
        out_specs=(P(("groups", "renv"), None), P(("groups", "renv"), None)),
        check_vma=False,
    )
```
